32 devices in a mesh: gx: 4 (over y, core), gy: 2 (over x), gz: 4 (over z).
Axes of the slice: x: 2, y: 2, z: 4, core: 2. Of those that a mesh axis runs over, the one named last changes fastest.
Arguments:
- rhs: float32 [16, 8, 128, 512], P('gx', 'gy', 'gz'), may hold values from -6 to 6
- coef: float32 [16, 8, 128], P('gx', 'gy', 'gz'), may hold values from 1 to 4
- mass: float32 [512, 512], replicated, as said below
- smoother: float32 [512, 512], replicated, as said below
- lift: float32 [384, 512], replicated, may hold values from -0.15 to 0.15
- restrict: float32 [512, 8], replicated, may hold values from -0.25 to 0.25
- coarse_block_matrix: float32 [8, 8], replicated
- element_cluster_index: int32 [16, 8, 128], P('gx', 'gy', 'gz'), may hold values from 0 to 63
Outputs:
- corrected: float32 [16, 8, 128, 512], P('gx', 'gy', 'gz')
The draws below stay inside these ranges and needn't reach their ends.
Inputs may be any that keep to these rules, and one draw needn't show every extreme that they name: `element_cluster_index`: index of an agglomerate within the element's own device block. `mass`: identity plus independent entries of deviation 0.15 / sqrt(512). `smoother`: identity minus the off-diagonal part of mass.
All inputs are finite; a program needn't handle non-finite values.
Results may differ from the reference program's by a relative error of at most 0.00005.
Values sent between devices are 32-bit elements; how exact they have to be, the bound alone decides.
No kernel may reach another device: no remote copies, remote signals or barrier semaphores. Data moves between devices by JAX's collectives and lax.ppermute only.
A program may use at most 64 MiB of HBM per device.

```python
import math
import jax
import jax.numpy as jnp
from jax import lax

EDGE = 8
ELEMENT_DOFS = 512
FACE = 64
COARSE = 8
EX = 4
EY = 4
EZ = 32
DEVICE_CLUSTERS = 64
ELEMENTS_X = 16
ELEMENTS_Y = 8
ELEMENTS_Z = 128
N_GX = 4
N_GY = 2
N_GZ = 4


def shared_part(key):
    noise = jax.random.normal(key, (ELEMENT_DOFS, ELEMENT_DOFS), jnp.float32)
    noise = jnp.clip(noise, -5.0, 5.0) * (0.15 / ELEMENT_DOFS ** 0.5)
    return noise * (1.0 - jnp.eye(ELEMENT_DOFS, dtype=jnp.float32))


def draw_mass(key, part):
    offdiag = shared_part(key)
    return jnp.eye(ELEMENT_DOFS, dtype=jnp.float32) + offdiag


def draw_smoother(key, part):
    offdiag = shared_part(key)
    return jnp.eye(ELEMENT_DOFS, dtype=jnp.float32) - offdiag


def draw_coarse_block_matrix(key, part):
    key = jax.random.fold_in(key, 7)
    noise = jnp.clip(jax.random.normal(key, (COARSE, COARSE), jnp.float32), -4.0, 4.0)
    return jnp.eye(COARSE, dtype=jnp.float32) + 0.1 * noise


def set_ends(array, stream_key, smallest, top_value):
    longest = array.shape.index(max(array.shape))
    spots = []
    for shift in (0, 1):
        where = [jax.random.randint(jax.random.fold_in(stream_key, axis), (), 0, length) for axis, length in enumerate(array.shape)]
        where[longest] = (where[longest] + shift) % array.shape[longest]
        spots.append(tuple(where))
    return array.at[spots[0]].set(smallest).at[spots[1]].set(top_value)


def block_levels(own_key, shape, shards, smallest, largest):
    def one(position, shards_of):
        heights = jax.random.uniform(jax.random.fold_in(jax.random.fold_in(own_key, 6), position), (shards_of,), jnp.float32, smallest / len(shards), largest / len(shards))
        return jnp.repeat(jnp.exp(heights), shape[position] // shards_of).reshape((-1,) + (1,) * (len(shape) - position - 1))

    factor_of = one(*shards[0])
    for cut in shards[1:]:
        factor_of = factor_of * one(*cut)
    return factor_of


def centred(rng, dims, spread, most, cuts=(), kind=jnp.bfloat16):
    gain = block_levels(rng, dims, cuts, -0.22, 0.18) if cuts else 1.0
    array = jax.random.normal(rng, dims, jnp.float32) * spread * gain
    return jnp.minimum(jnp.maximum(array, -most), most).astype(kind)


def setup_inputs(seed: int = 0) -> dict:
    arg_keys = jax.random.split(jax.random.key(seed), 9)
    return {
        "rhs": centred(arg_keys[0], (ELEMENTS_X, ELEMENTS_Y, ELEMENTS_Z, ELEMENT_DOFS), 1.0, 6.0, ((0, 4), (1, 2), (2, 4)), jnp.float32),
        "coef": jnp.clip(jnp.exp(math.log(4.0) - 1.3862944 * jax.random.uniform(arg_keys[1], (ELEMENTS_X, ELEMENTS_Y, ELEMENTS_Z), jnp.float32) ** block_levels(arg_keys[1], (ELEMENTS_X, ELEMENTS_Y, ELEMENTS_Z), ((0, 4), (1, 2), (2, 4)), -0.2, 0.2)), 1.0, 4.0),
        "mass": draw_mass(jax.random.fold_in(arg_keys[8], 71), 0),
        "smoother": draw_smoother(jax.random.fold_in(arg_keys[8], 71), 0),
        "lift": centred(arg_keys[4], (6 * FACE, ELEMENT_DOFS), 0.025, 0.15, (), jnp.float32),
        "restrict": centred(arg_keys[5], (ELEMENT_DOFS, COARSE), ELEMENT_DOFS ** -0.5, 0.25, (), jnp.float32),
        "coarse_block_matrix": draw_coarse_block_matrix(jax.random.fold_in(arg_keys[8], 71), 0),
        "element_cluster_index": set_ends(jax.random.randint(arg_keys[7], (ELEMENTS_X, ELEMENTS_Y, ELEMENTS_Z), 0, DEVICE_CLUSTERS), jax.random.fold_in(arg_keys[7], 1), 0, DEVICE_CLUSTERS - 1).astype(jnp.int32),
    }


def face_traces(field):
    cube = field.reshape(field.shape[:-1] + (EDGE, EDGE, EDGE))
    lead = field.shape[:-1]
    last = EDGE - 1
    parts = [cube[..., 0, :, :], cube[..., last, :, :], cube[..., :, 0, :], cube[..., :, last, :], cube[..., :, :, 0], cube[..., :, :, last]]
    return jnp.concatenate([p.reshape(lead + (FACE,)) for p in parts], -1)


def neighbour_faces(padded):
    width = FACE
    return jnp.concatenate([
        padded[:-2, 1:-1, 1:-1, width:2 * width], padded[2:, 1:-1, 1:-1, 0:width],
        padded[1:-1, :-2, 1:-1, 3 * width:4 * width], padded[1:-1, 2:, 1:-1, 2 * width:3 * width],
        padded[1:-1, 1:-1, :-2, 5 * width:6 * width], padded[1:-1, 1:-1, 2:, 4 * width:5 * width]], -1)


def reference(rhs, coef, mass, smoother, lift, restrict, coarse_block_matrix, element_cluster_index):
    high = lax.Precision.HIGHEST

    def mult(a, b):
        return jnp.matmul(a, b, precision=high)

    def operate(field):
        padded = jnp.pad(face_traces(field), ((1, 1), (1, 1), (1, 1), (0, 0)))
        return coef[..., None] * mult(field, mass) - mult(neighbour_faces(padded), lift)

    first = mult(rhs, smoother) / coef[..., None]
    second = first + mult(rhs - operate(first), smoother) / coef[..., None]
    resid = rhs - operate(second)
    small = mult(resid, restrict)
    gxn, gyn, gzn = N_GX, N_GY, N_GZ
    blocks = small.reshape(gxn, EX, gyn, EY, gzn, EZ, COARSE).transpose(2, 4, 0, 1, 3, 5, 6)
    blocks = blocks.reshape(gyn, gzn, gxn, EX * EY * EZ, COARSE)
    labels = element_cluster_index.reshape(gxn, EX, gyn, EY, gzn, EZ).transpose(2, 4, 0, 1, 3, 5)
    labels = labels.reshape(gyn, gzn, gxn, EX * EY * EZ)
    onehot = (labels[..., None] == jnp.arange(DEVICE_CLUSTERS, dtype=jnp.int32)).astype(jnp.float32)
    coarse_rhs = jnp.einsum('yzgea,yzgek->yzkga', onehot, blocks, precision=high).reshape(gyn, gzn, COARSE, gxn * DEVICE_CLUSTERS)
    weight_factor = (1.0 + jnp.sum(onehot, 3)).reshape(gyn, gzn, 1, gxn * DEVICE_CLUSTERS)
    zone = coarse_rhs / weight_factor
    zpad = jnp.pad(zone, ((1, 1), (1, 1), (0, 0), (0, 0)))
    nearby = zpad[:-2, 1:-1] + zpad[2:, 1:-1] + zpad[1:-1, :-2] + zpad[1:-1, 2:]
    line_sum = jnp.sum(zone.reshape(gyn, gzn, COARSE, gxn, DEVICE_CLUSTERS), 3, keepdims=True)
    line_sum = jnp.broadcast_to(line_sum, (gyn, gzn, COARSE, gxn, DEVICE_CLUSTERS)).reshape(zone.shape)
    applied = weight_factor * jnp.einsum('kl,yzla->yzka', coarse_block_matrix, zone, precision=high) - nearby - line_sum
    ztwo = zone + (coarse_rhs - applied) / weight_factor
    ztwo = ztwo.reshape(gyn, gzn, COARSE, gxn, DEVICE_CLUSTERS)
    picked = jnp.einsum('yzgea,yzkga->yzgek', onehot, ztwo, precision=high)
    corr = mult(picked, restrict.T)
    corr = corr.reshape(gyn, gzn, gxn, EX, EY, EZ, ELEMENT_DOFS).transpose(2, 3, 0, 4, 1, 5, 6)
    return second + corr.reshape(second.shape)
```

```python
import functools

import jax
import jax.numpy as jnp
from jax import lax
from jax.experimental import pallas as pl
from jax.experimental.pallas import tpu as pltpu
from jax.sharding import PartitionSpec as P

EDGE = 8
DOFS = 512
FACE = 64
COARSE = 8
CLUSTERS = 64
LANES = 128
META = 8

F32 = jnp.float32
BF16 = jnp.bfloat16
NT = (((1,), (1,)), ((), ()))
TN = (((0,), (0,)), ((), ()))


def selection():
    column = lane((1, 4 * FACE))
    face, a, b = column // FACE, column % FACE // EDGE, column % EDGE
    node = jnp.where(face < 2, a * 64 + face * 56 + b, a * 64 + b * 8 + (face - 2) * 7)
    at = lax.broadcasted_iota(jnp.int32, (DOFS, 4 * FACE), 0)
    return jnp.where(at == node, 1.0, 0.0).astype(BF16)


def halves(x):
    high = x.astype(BF16)
    return high, (x - high.astype(F32)).astype(BF16)


def dot(a, b, dims=(((1,), (0,)), ((), ()))):
    return lax.dot_general(a, b, dims, preferred_element_type=F32)


def dot3(a, b, dims=(((1,), (0,)), ((), ()))):
    return dot(a[0], b[0], dims) + (dot(a[0], b[1], dims) + dot(a[1], b[0], dims))


def dot3_few(a, b):
    n = a[0].shape[0]
    both = dot(jnp.concatenate(a, 0), b[0], NT)
    return both[:n] + (both[n:] + dot(a[0], b[1], NT))


def lane(shape):
    return lax.broadcasted_iota(jnp.int32, shape, len(shape) - 1)


def swap(x):
    return pltpu.roll(x, FACE, 1)


def pack0(t):
    n = t.shape[0] // 2
    return jnp.where(lane((n, LANES)) < FACE, t[:n], swap(t[n:]))


def pack7(t):
    n = t.shape[0] // 2
    return jnp.where(lane((n, LANES)) < FACE, swap(t[:n]), t[n:])


def unpack0(p):
    return jnp.concatenate([p, swap(p)], 0)


def unpack7(p):
    return jnp.concatenate([swap(p), p], 0)


def cell_rows(ref):
    ex, ey, ez = ref.shape
    rows = []
    for x in range(ex):
        rows.append(jnp.concatenate([ref[x, y : y + 1, :] for y in range(ey)], 1))
    return jnp.concatenate(rows, 0).astype(F32)


def reciprocal(rows):
    n = rows.shape[0]
    columns = (1.0 / jnp.concatenate([rows, jnp.ones((LANES - n, LANES), F32)], 0)).T
    return jnp.concatenate([jnp.broadcast_to(columns[:, x : x + 1], (LANES, LANES)) for x in range(n)], 0)


def as_row(rows):
    return jnp.concatenate([rows[x : x + 1] for x in range(rows.shape[0])], 1)


def onehot_rows(row):
    n = row.shape[1]
    at = lax.broadcasted_iota(jnp.int32, (CLUSTERS, n), 0).astype(F32)
    return jnp.where(at == row, 1.0, 0.0).astype(BF16)


def position(sizes):
    return lax.axis_index("gx"), lax.axis_index("gy"), lax.axis_index("gz")


def near_identity(s_ref, part):
    n = part.stop - part.start
    row = lax.broadcasted_iota(jnp.int32, (n, DOFS), 0) + part.start
    return halves(jnp.where(row == lane((n, DOFS)), 1.0, 0.0) - s_ref[part])


def start_all(pairs, sems, second=()):
    copies = [pltpu.make_async_copy(src, dst, sems.at[i]) for i, (src, dst) in enumerate(pairs)]
    for i, copy in enumerate(copies):
        copy.start(priority=1 if i in second else 0)
    return copies


def fetch(names, sems, rhs=None, s=None, m=None, l=None, rt=None, c=None):
    pairs = {"rhs": [rhs], "s": [s], "rt": [rt], "c": [c], "m": [], "l": []}
    for i in range(DOFS // LANES if m else 0):
        block = slice(i * LANES, (i + 1) * LANES)
        pairs["m"].append((m[0].at[block, block], m[1].at[i]))
    for f in range(6 if l else 0):
        g = f ^ 1
        pairs["l"].append((l[0].at[f * FACE : (f + 1) * FACE], l[1].at[g * FACE : (g + 1) * FACE]))
    counts = [len(pairs[name]) for name in names]
    first = [sum(counts[:i]) for i in range(len(names))]
    second = first[names.index("rhs")] if "rhs" in names else -1
    copies = start_all([pair for name in names for pair in pairs[name]], sems, [second])

    def wait(name):
        i = names.index(name)
        for copy in copies[first[i] : first[i] + counts[i]]:
            copy.wait()

    return wait


def diagonal_rows(d_ref):
    here = lax.broadcasted_iota(jnp.int32, (LANES, LANES), 0) == lane((LANES, LANES))
    return jnp.concatenate(
        [jnp.sum(jnp.where(here, d_ref[i], 0.0), 0, keepdims=True) for i in range(d_ref.shape[0])], 0
    )


def traces(u, split, pick, scale):
    lower = lane((u.shape[0], LANES)) < FACE
    picked = dot(split[0], pick) + dot(split[1], pick)
    x_pair = jnp.where(lower, u[:, :LANES], u[:, DOFS - LANES :]) * scale
    return x_pair, picked[:, :LANES] * scale, picked[:, LANES:] * scale


def smooth_kernel(sizes, rhs_hbm, s_hbm, coef_hbm, lab_hbm, rt_hbm, c_hbm,
                  uh_ref, ul_ref, th_ref, nh_ref, tr_ref, meta_ref, xy_ref, zu_ref, zd_ref, rt_ref, c_ref, rn_ref,
                  rhs_ref, s_ref, coef_ref, lab_ref, sems, late_sems):
    ngx, ngy, ngz = sizes
    gx, gy, gz = position(sizes)
    half = DOFS // 2
    blocks = [slice(0, half), slice(half, DOFS)]
    small = start_all([(coef_hbm, coef_ref), (lab_hbm, lab_ref)], sems)
    wait = fetch(
        ("rt", "c", "s"), late_sems, s=(s_hbm, s_ref), rt=(rt_hbm, rt_ref), c=(c_hbm, c_ref)
    )
    copies = [
        pltpu.make_async_copy(rhs_hbm.at[rows], rhs_ref.at[rows], sems.at[2 + i]) for i, rows in enumerate(blocks)
    ]
    for copy in copies:
        copy.start()
    ex, ey, ez = lab_ref.shape
    plane = ey * ez
    pick = selection()
    small[0].wait()
    small[1].wait()
    lab = cell_rows(lab_ref)
    counts = dot(jnp.ones((8, DOFS), BF16), onehot_rows(as_row(lab)), NT)
    weights = jnp.concatenate([1.0 + counts[0:1], jnp.ones((1, FACE), F32)], 1)
    meta = jnp.concatenate([lab, weights, jnp.zeros((META - 5, LANES), F32)], 0)
    meta_ref[:META] = meta
    meta_ref[META : META + ex] = cell_rows(coef_ref)
    rc = reciprocal(meta_ref[META : META + ex])

    wait("rt")
    wait("c")
    wait("s")
    near = near_identity(s_ref, slice(0, DOFS))
    nh_ref[...] = near[0]
    rn_ref[...] = dot3_few(halves(rt_ref[...]), near)
    pairs = []
    for rows, copy in zip(blocks, copies):
        copy.wait()
        rhs = rhs_ref[rows]
        t = dot3(halves(rhs), near)
        th_ref[rows] = t.astype(BF16)
        u = rhs - t
        split = halves(u)
        uh_ref[rows], ul_ref[rows] = split
        pairs.append(traces(u, split, pick, rc[rows]))
        for i, pair in enumerate(pairs[-1]):
            tr_ref[rows, i * LANES : (i + 1) * LANES] = pair
    x_pair, y_pair, z_pair = [jnp.concatenate([block[i] for block in pairs], 0) for i in range(3)]

    def y_rows(y):
        return jnp.concatenate(
            [y_pair[x * plane + y * ez : x * plane + (y + 1) * ez] for x in range(ex)], 0
        )

    def z_rows(z):
        return jnp.concatenate([z_pair[i * ez + z : i * ez + z + 1] for i in range(ex * ey)], 0)

    def send(ref, slot, payload):
        n = payload.shape[0]
        ref[slot, :n] = payload
        ref[slot, n:] = meta

    here = gx * ngy + gy
    send(xy_ref, jnp.where(gx < ngx - 1, here + ngy, here), pack7(x_pair[(ex - 1) * plane :]))
    send(xy_ref, jnp.where(gx > 0, here - ngy, here), pack0(x_pair[:plane]))
    send(xy_ref, jnp.where(gy < ngy - 1, here + 1, here), pack7(y_rows(ey - 1)))
    send(xy_ref, jnp.where(gy > 0, here - 1, here), pack0(y_rows(0)))
    zu_ref[...] = jnp.concatenate([pack7(z_rows(ez - 1)), meta], 0)
    zd_ref[...] = jnp.concatenate([pack0(z_rows(0)), meta], 0)


def receive(sizes, dims, xy_ref, zu_ref, zd_ref):
    ngx, ngy, ngz = sizes
    gx, gy, gz = position(sizes)

    def one(got, there):
        n = got.shape[0] - META
        payload = jnp.where(there, got[:n], 0.0)
        labels = jnp.where(there, got[n : n + dims[0]], -1.0)
        weights = jnp.where(there, got[n + dims[0] : n + dims[0] + 1], 1.0)
        return payload, labels, weights

    return [
        one(xy_ref[jnp.minimum(gx + 1, ngx - 1) * ngy + gy], gx < ngx - 1),
        one(xy_ref[jnp.maximum(gx - 1, 0) * ngy + gy], gx > 0),
        one(xy_ref[gx * ngy + jnp.minimum(gy + 1, ngy - 1)], gy < ngy - 1),
        one(xy_ref[gx * ngy + jnp.maximum(gy - 1, 0)], gy > 0),
        one(zd_ref[...], gz < ngz - 1),
        one(zu_ref[...], gz > 0),
    ]


def faces(f_ref, dims, tr_ref, around):
    ex, ey, ez = dims
    lower = lane((ez, LANES)) < FACE
    inner = lax.broadcasted_iota(jnp.int32, (ez, LANES), 0)
    none = jnp.zeros((ez, LANES), F32)
    outer = None
    if around is not None:
        outer = [(unpack0 if i % 2 == 0 else unpack7)(a[0]) for i, a in enumerate(around)]

    def local(i, pair):
        if tr_ref is None:
            return none
        return tr_ref[i * ez : (i + 1) * ez, pair]

    def remote(side, strip):
        return none if outer is None else outer[side][strip]

    for x in range(ex):
        for y in range(ey):
            i = x * ey + y
            rows = slice(i * ez, (i + 1) * ez)
            pair = slice(0, LANES)
            strip = slice(y * ez, (y + 1) * ez)
            above = local(i + ey, pair) if x < ex - 1 else remote(0, strip)
            below = local(i - ey, pair) if x > 0 else remote(1, strip)
            f_ref[rows, pair] = jnp.where(lower, above, below)
            pair = slice(LANES, 2 * LANES)
            strip = slice(x * ez, (x + 1) * ez)
            above = local(i + 1, pair) if y < ey - 1 else remote(2, strip)
            below = local(i - 1, pair) if y > 0 else remote(3, strip)
            f_ref[rows, pair] = jnp.where(lower, above, below)
            pair = slice(2 * LANES, 3 * LANES)
            above = below = none
            if tr_ref is not None:
                column = tr_ref[rows, pair]
                above = jnp.where(inner == ez - 1, 0.0, pltpu.roll(column, ez - 1, 0))
                below = jnp.where(inner == 0, 0.0, pltpu.roll(column, 1, 0))
            if outer is not None:
                above = jnp.where(inner == ez - 1, outer[4][i : i + 1], above)
                below = jnp.where(inner == 0, outer[5][i : i + 1], below)
            f_ref[rows, pair] = jnp.where(lower, above, below)


def prepare_kernel(dims, l_hbm, m_hbm, uh_ref, ul_ref, th_ref, nh_ref, tr_ref, rt_ref, rn_ref,
                   p_ref, own_ref, qh_ref, ql_ref, d_out_ref, l_ref, d_ref, f_ref, sems):
    wait = fetch(("l", "m"), sems, l=(l_hbm, l_ref), m=(m_hbm, d_ref))
    faces(f_ref, dims, tr_ref, None)
    inside = halves(f_ref[...])
    near = nh_ref[...]
    pick = selection()
    wait("l")
    wait("m")
    diagonal = diagonal_rows(d_ref)
    d_out_ref[...] = diagonal
    d = as_row(diagonal)
    lift = halves(l_ref[...])
    lrt = dot3_few(halves(rt_ref[...]), lift)
    zeros = jnp.zeros((COARSE, DOFS - FACE), F32)
    x0 = jnp.concatenate([lrt[:, :FACE], zeros], 1)
    x7 = jnp.concatenate([zeros, lrt[:, FACE:LANES]], 1)
    yz = lrt[:, LANES:]
    group = lane((COARSE, 4 * FACE)) // FACE
    spread = jnp.concatenate([jnp.where(group == f, yz, 0.0) for f in range(4)], 0)
    both = dot(jnp.concatenate(halves(spread), 0), pick, NT)
    yz = both[: 4 * COARSE] + both[4 * COARSE :]
    mrt = rt_ref[...] * d + rn_ref[...]
    q = jnp.concatenate([x0, x7, yz, mrt, jnp.zeros_like(mrt)], 0)
    rows = q.shape[0]
    both = dot(jnp.concatenate(halves(q), 0), near, NT)
    swept = q - (both[:rows] + both[rows:])
    split = halves(swept)
    of_t = dot(split[0], near, NT)
    of_f = halves(dot3_few(split, lift))
    qh_ref[...], ql_ref[...] = of_f
    of_u = halves(jnp.concatenate([q + swept * (1.0 - d), rt_ref[...]], 0))
    of_t = jnp.concatenate([of_t, rt_ref[...]], 0).astype(BF16)
    both = dot3_few(of_u, (uh_ref[...], ul_ref[...])) + dot(of_t, th_ref[...], NT)
    p_ref[...] = both[:rows] + dot3_few(of_f, inside)
    own_ref[...] = both[rows:]


def relax_kernel(sizes, dims, p_ref, own_ref, qh_ref, ql_ref, c_ref, meta_ref, xy_ref, zd_ref, zu_ref,
                 slots_ref, f_ref, bins_ref):
    ngx, ngy, ngz = sizes
    gx, gy, gz = position(sizes)
    ex, ey, ez = dims
    plane = ey * ez
    around = receive(sizes, dims, xy_ref, zu_ref, zd_ref)
    x_up, x_down, y_up, y_down, z_up, z_down = around
    q = qh_ref[...], ql_ref[...]
    rows = q[0].shape[0]
    keep = lane((rows, LANES)) < FACE

    def through(side, payload):
        pair = slice(side // 2 * LANES, (side // 2 + 1) * LANES)
        mine = keep if side % 2 == 0 else ~keep
        few = [jnp.where(mine, a[:, pair].astype(F32), 0.0).astype(BF16) for a in q]
        return dot3_few(few, halves(payload))

    added = []
    x_above, x_below = through(0, unpack0(x_up[0])), through(1, unpack7(x_down[0]))
    y_above, y_below = through(2, unpack0(y_up[0])), through(3, unpack7(y_down[0]))
    z_above, z_below = unpack0(z_up[0]), unpack7(z_down[0])
    inner = lax.broadcasted_iota(jnp.int32, (ez, LANES), 0)
    for i in range(ex * ey):
        f_ref[i * ez : (i + 1) * ez] = jnp.where(
            lane((ez, LANES)) < FACE,
            jnp.where(inner == ez - 1, z_above[i : i + 1], 0.0),
            jnp.where(inner == 0, z_below[i : i + 1], 0.0),
        )
    z_both = dot3_few([a[:, 2 * LANES :] for a in q], halves(f_ref[...]))
    at = lane((rows, LANES))
    for x in range(ex):
        tile = z_both[:, x * LANES : (x + 1) * LANES]
        up, down = (plane - ez - x * ez) % LANES, (LANES - x * ez) % LANES
        tile = tile + jnp.where(at >= plane - ez, pltpu.roll(y_above, up, 1) if up else y_above, 0.0)
        tile = tile + jnp.where(at < ez, pltpu.roll(y_below, down, 1) if down else y_below, 0.0)
        tile = tile + (x_above if x == ex - 1 else 0.0) + (x_below if x == 0 else 0.0)
        added.append(tile)
    p = p_ref[...] + jnp.concatenate(added, 1)
    own = own_ref[...]
    small = own - p[6 * COARSE : 7 * COARSE]
    p = p / as_row(meta_ref[META : META + ex])
    p_x0, p_x7, p_y0, p_y7, p_z0, p_z7 = [p[8 * f : 8 * f + 8] for f in range(6)]
    at = lane((COARSE, LANES))

    def tiles(a):
        return [a[:, x * LANES : (x + 1) * LANES] for x in range(ex)]

    none = jnp.zeros((COARSE, LANES), F32)
    total = []
    parts = [tiles(a) for a in (small, p_x0, p_x7, p_y0, p_y7, p_z0, p_z7)]
    for x in range(ex):
        s, _, _, y0, y7, z0, z7 = [a[x] for a in parts]
        s = s + (parts[1][x + 1] if x < ex - 1 else none)
        s = s + (parts[2][x - 1] if x > 0 else none)
        s = s + jnp.where(at < plane - ez, pltpu.roll(y0, LANES - ez, 1), 0.0)
        s = s + jnp.where(at >= ez, pltpu.roll(y7, ez, 1), 0.0)
        s = s + jnp.where(at % ez < ez - 1, pltpu.roll(z0, LANES - 1, 1), 0.0)
        s = s + jnp.where(at % ez > 0, pltpu.roll(z7, 1, 1), 0.0)
        total.append(s)
    total = jnp.concatenate(total, 1)

    def scatter(values, onehot):
        high, low = halves(values)
        out = dot(jnp.concatenate([high, low], 0), onehot, NT)
        return out[:COARSE] + out[COARSE:]

    def shifted(labels, shift, keep):
        return as_row(jnp.where(keep, pltpu.roll(labels, shift, 1), -1.0))

    rows = lane((ex, LANES))
    labels = meta_ref[0:ex]
    blocks = [
        (scatter(total, onehot_rows(as_row(labels))), meta_ref[ex : ex + 1]),
        (scatter(parts[2][ex - 1], onehot_rows(x_up[1][0:1])), x_up[2]),
        (scatter(parts[1][0], onehot_rows(x_down[1][ex - 1 : ex])), x_down[2]),
        (scatter(p_y7, onehot_rows(shifted(y_up[1], plane - ez, rows >= plane - ez))), y_up[2]),
        (scatter(p_y0, onehot_rows(shifted(y_down[1], ez, rows < ez))), y_down[2]),
        (scatter(p_z7, onehot_rows(shifted(z_up[1], ez - 1, rows % ez == ez - 1))), z_up[2]),
        (scatter(p_z0, onehot_rows(shifted(z_down[1], LANES - ez + 1, rows % ez == 0))), z_down[2]),
    ]
    raw = jnp.concatenate([z for z, _ in blocks], 1)
    mixed = raw + raw
    for k in range(COARSE):
        mixed = mixed - c_ref[:, k : k + 1] * raw[k : k + 1]

    def packed(block):
        rows = COARSE // 2
        return jnp.concatenate([block[:rows], block[rows:]], 1)

    b0, xu, xd, yu, yd, zu, zd = [packed(z / w[:, :FACE]) for z, w in blocks]
    a0, axu, axd, ayu, ayd, azu, azd = [
        packed(mixed[:, i * FACE : (i + 1) * FACE]) for i in range(len(blocks))
    ]

    count = slots_ref.shape[0]
    bins_ref[...] = jnp.zeros_like(bins_ref)

    def put(dx, dy, dz, share):
        there = (dy >= 0) & (dy < ngy) & (dz >= 0) & (dz < ngz)
        bins_ref[jnp.where(there, (dx * ngy + dy) * ngz + dz, count)] = share

    line = b0 + xu + xd
    sides = yu + yd + zu + zd
    for dx in range(ngx):
        same = (gx == dx).astype(F32)
        up = (gx + 1 == dx).astype(F32)
        down = (gx - 1 == dx).astype(F32)
        column = same * b0 + up * xu + down * xd
        put(dx, gy, gz, line + same * (sides + a0) + up * axu + down * axd)
        put(dx, gy + 1, gz, yu + column + same * ayu)
        put(dx, gy - 1, gz, yd + column + same * ayd)
        put(dx, gy, gz + 1, zu + column + same * azu)
        put(dx, gy, gz - 1, zd + column + same * azd)
    put(gx, gy + 2, gz, yu)
    put(gx, gy - 2, gz, yd)
    put(gx, gy, gz + 2, zu)
    put(gx, gy, gz - 2, zd)
    put(gx, gy + 1, gz + 1, yu + zu)
    put(gx, gy + 1, gz - 1, yu + zd)
    put(gx, gy - 1, gz + 1, yd + zu)
    put(gx, gy - 1, gz - 1, yd + zd)
    slots_ref[...] = bins_ref[:count]


def second_kernel(sizes, dims, rhs_hbm, s_hbm, l_hbm, uh_ref, ul_ref, tr_ref, d_ref, meta_ref, rt_ref, xy_ref, zd_ref, zu_ref,
                  second_ref, rs_ref, oh_ref, rhs_ref, s_ref, l_ref, f_ref, sems):
    wait = fetch(("l", "s", "rhs"), sems, rhs=(rhs_hbm, rhs_ref), s=(s_hbm, s_ref), l=(l_hbm, l_ref))
    ex = dims[0]
    faces(f_ref, dims, tr_ref, receive(sizes, dims, xy_ref, zu_ref, zd_ref))
    onehot = onehot_rows(as_row(meta_ref[:ex]))
    oh_ref[...] = jnp.concatenate([onehot, onehot], 0).astype(F32).T.astype(BF16)
    rt = halves(rt_ref[...])
    rs_ref[...] = jnp.concatenate([rt[0], rt[0], rt[1], jnp.zeros_like(rt[0])], 0)
    wait("l")
    r1 = dot3(halves(f_ref[...]), halves(l_ref[...]))
    wait("s")
    near = near_identity(s_ref, slice(0, DOFS))
    wait("rhs")
    u = uh_ref[...].astype(F32) + ul_ref[...].astype(F32)
    d = as_row(d_ref[...])
    r1 = r1 + dot3(halves(rhs_ref[...] - u), near) + u * (1.0 - d)
    v = u + (r1 - dot3(halves(r1), near))
    rc = reciprocal(meta_ref[META : META + ex])
    second_ref[...] = v * jnp.concatenate([rc] * (DOFS // LANES), 1)


def correct_kernel(second_ref, slots_ref, meta_ref, oh_ref, rs_ref, out_hbm, out_ref, sems):
    total = jnp.sum(slots_ref[...], 0)
    ztwo = jnp.concatenate([total[:, :FACE], total[:, FACE:]], 0) / meta_ref[4:5, :FACE]
    high, low = halves(ztwo)
    stacked = jnp.concatenate([high, low, high, jnp.zeros_like(high)], 0)
    prolonged = dot(stacked, rs_ref[...], TN)
    prolonged = jnp.concatenate(halves(prolonged), 0)
    chunk = DOFS // sems.shape[0]
    copies = []
    for i in range(sems.shape[0]):
        rows = slice(i * chunk, (i + 1) * chunk)
        out_ref[rows] = second_ref[rows] + dot(oh_ref[rows], prolonged)
        copy = pltpu.make_async_copy(out_ref.at[rows], out_hbm.at[rows], sems.at[i])
        copy.start()
        copies.append(copy)
    for copy in copies:
        copy.wait()


def shards(sizes, rhs, coef, mass, smoother, lift, restrict, coarse_block_matrix, element_cluster_index):
    ngx, ngy, ngz = sizes
    dims = coef.shape
    ex, ey, ez = dims
    flat = rhs.reshape(ex * ey * ez, DOFS)
    face = ey * ez * FACE // LANES
    tip = ex * ey * FACE // LANES
    params = pltpu.CompilerParams(vmem_limit_bytes=40 * 1024 * 1024)
    shape = jax.ShapeDtypeStruct
    hbm = pl.BlockSpec(memory_space=pltpu.HBM)
    vmem = pl.BlockSpec(memory_space=pltpu.VMEM)
    cost = pl.CostEstimate(flops=2 * 10**9, bytes_accessed=4 * 2**20, transcendentals=0)
    def far(*arrays):
        return [pltpu.with_memory_space_constraint(a, pltpu.HBM) for a in arrays]

    full = shape((DOFS, DOFS), F32)
    split = shape((DOFS, DOFS), BF16)
    count = ngx * ngy * ngz
    wide = shape((8 * COARSE, 3 * LANES), BF16)
    few = shape((COARSE, DOFS), F32)
    uh, ul, th, nh, tr, meta, xy, zu, zd, rt, c, rn = pl.pallas_call(
        functools.partial(smooth_kernel, sizes),
        out_shape=(
            split,
            split,
            split,
            split,
            shape((DOFS, 3 * LANES), F32),
            shape((2 * META, LANES), F32),
            shape((ngx * ngy, face + META, LANES), F32),
            shape((tip + META, LANES), F32),
            shape((tip + META, LANES), F32),
            few,
            shape((COARSE, COARSE), F32),
            few,
        ),
        in_specs=[hbm] * 6,
        scratch_shapes=[
            pltpu.VMEM((DOFS, DOFS), F32),
            pltpu.VMEM((DOFS, DOFS), F32),
            pltpu.VMEM(dims, F32),
            pltpu.VMEM(dims, jnp.int32),
            pltpu.SemaphoreType.DMA((4,)),
            pltpu.SemaphoreType.DMA((3,)),
        ],
        compiler_params=params,
        cost_estimate=cost,
        name="smooth",
    )(*far(flat, smoother, coef, element_cluster_index, restrict.T, coarse_block_matrix))
    zd = lax.ppermute(zd, "gz", [(i + 1, i) for i in range(ngz - 1)])
    zu = lax.ppermute(zu, "gz", [(i, i + 1) for i in range(ngz - 1)])
    xy = lax.all_to_all(xy, ("gx", "gy"), 0, 0, tiled=True)
    p, own, fh, fl, d = pl.pallas_call(
        functools.partial(prepare_kernel, dims),
        out_shape=(shape((8 * COARSE, DOFS), F32), few, wide, wide, shape((DOFS // LANES, LANES), F32)),
        in_specs=[hbm] * 2 + [vmem] * 7,
        scratch_shapes=[
            pltpu.VMEM((3 * LANES, DOFS), F32),
            pltpu.VMEM((DOFS // LANES, LANES, LANES), F32),
            pltpu.VMEM((DOFS, 3 * LANES), F32),
            pltpu.SemaphoreType.DMA((10,)),
        ],
        compiler_params=params,
        cost_estimate=cost,
        name="prepare",
    )(*far(lift, mass), uh, ul, th, nh, tr, rt, rn)
    slots = pl.pallas_call(
        functools.partial(relax_kernel, sizes, dims),
        out_shape=shape((count, COARSE // 2, LANES), F32),
        scratch_shapes=[
            pltpu.VMEM((DOFS, LANES), F32),
            pltpu.VMEM((count + 1, COARSE // 2, LANES), F32),
        ],
        compiler_params=params,
        cost_estimate=cost,
        name="relax",
    )(p, own, fh, fl, c, meta, xy, zd, zu)
    slots = lax.all_to_all(slots, ("gx", "gy", "gz"), 0, 0, tiled=True)
    second, rs, oh = pl.pallas_call(
        functools.partial(second_kernel, sizes, dims),
        out_shape=(
            full,
            shape((4 * COARSE, DOFS), BF16),
            shape((DOFS, LANES), BF16),
        ),
        in_specs=[hbm] * 3 + [vmem] * 9,
        scratch_shapes=[
            pltpu.VMEM((DOFS, DOFS), F32),
            pltpu.VMEM((DOFS, DOFS), F32),
            pltpu.VMEM((3 * LANES, DOFS), F32),
            pltpu.VMEM((DOFS, 3 * LANES), F32),
            pltpu.SemaphoreType.DMA((8,)),
        ],
        compiler_params=params,
        cost_estimate=cost,
        name="second",
    )(*far(flat, smoother, lift), uh, ul, tr, d, meta, rt, xy, zd, zu)
    out = pl.pallas_call(
        correct_kernel,
        out_shape=shape((DOFS, DOFS), F32),
        out_specs=hbm,
        scratch_shapes=[pltpu.VMEM((DOFS, DOFS), F32), pltpu.SemaphoreType.DMA((4,))],
        compiler_params=params,
        name="correct",
    )(second, slots, meta, oh, rs)
    return out.reshape(rhs.shape)


def solution(mesh):
    sizes = (mesh.shape["gx"], mesh.shape["gy"], mesh.shape["gz"])
    cells = P("gx", "gy", "gz")
    return jax.shard_map(
        functools.partial(shards, sizes),
        mesh=mesh,
        in_specs=(P("gx", "gy", "gz", None), cells, P(), P(), P(), P(), P(), cells),
        out_specs=P("gx", "gy", "gz", None),
        check_vma=False,
    )
```

```python
import functools

import jax
import jax.numpy as jnp
from jax import lax
from jax.experimental import pallas as pl
from jax.experimental.pallas import tpu as pltpu
from jax.sharding import PartitionSpec as P

EDGE = 8
DOFS = 512
FACE = 64
COARSE = 8
CLUSTERS = 64
LANES = 128
META = 8

F32 = jnp.float32
BF16 = jnp.bfloat16
NT = (((1,), (1,)), ((), ()))
TN = (((0,), (0,)), ((), ()))


def selection():
    column = lane((1, 4 * FACE))
    face, a, b = column // FACE, column % FACE // EDGE, column % EDGE
    node = jnp.where(face < 2, a * 64 + face * 56 + b, a * 64 + b * 8 + (face - 2) * 7)
    at = lax.broadcasted_iota(jnp.int32, (DOFS, 4 * FACE), 0)
    return jnp.where(at == node, 1.0, 0.0).astype(BF16)


def halves(x):
    high = x.astype(BF16)
    return high, (x - high.astype(F32)).astype(BF16)


def dot(a, b, dims=(((1,), (0,)), ((), ()))):
    return lax.dot_general(a, b, dims, preferred_element_type=F32)


def dot3(a, b, dims=(((1,), (0,)), ((), ()))):
    return dot(a[0], b[0], dims) + (dot(a[0], b[1], dims) + dot(a[1], b[0], dims))


def dot3_few(a, b):
    n = a[0].shape[0]
    both = dot(jnp.concatenate(a, 0), b[0], NT)
    return both[:n] + (both[n:] + dot(a[0], b[1], NT))


def lane(shape):
    return lax.broadcasted_iota(jnp.int32, shape, len(shape) - 1)


def swap(x):
    return pltpu.roll(x, FACE, 1)


def pack0(t):
    n = t.shape[0] // 2
    return jnp.where(lane((n, LANES)) < FACE, t[:n], swap(t[n:]))


def pack7(t):
    n = t.shape[0] // 2
    return jnp.where(lane((n, LANES)) < FACE, swap(t[:n]), t[n:])


def unpack0(p):
    return jnp.concatenate([p, swap(p)], 0)


def unpack7(p):
    return jnp.concatenate([swap(p), p], 0)


def cell_rows(ref):
    ex, ey, ez = ref.shape
    rows = []
    for x in range(ex):
        rows.append(jnp.concatenate([ref[x, y : y + 1, :] for y in range(ey)], 1))
    return jnp.concatenate(rows, 0).astype(F32)


def face_order(lift):
    return jnp.concatenate([lift[(f ^ 1) * FACE : ((f ^ 1) + 1) * FACE] for f in range(6)], 0)


def reciprocal(rows):
    n = rows.shape[0]
    columns = (1.0 / jnp.concatenate([rows, jnp.ones((LANES - n, LANES), F32)], 0)).T
    return jnp.concatenate([jnp.broadcast_to(columns[:, x : x + 1], (LANES, LANES)) for x in range(n)], 0)


def as_row(rows):
    return jnp.concatenate([rows[x : x + 1] for x in range(rows.shape[0])], 1)


def onehot_rows(row):
    n = row.shape[1]
    at = lax.broadcasted_iota(jnp.int32, (CLUSTERS, n), 0).astype(F32)
    return jnp.where(at == row, 1.0, 0.0).astype(BF16)


def position(sizes):
    return lax.axis_index("gx"), lax.axis_index("gy"), lax.axis_index("gz")


def near_identity(s_ref, part):
    n = part.stop - part.start
    row = lax.broadcasted_iota(jnp.int32, (n, DOFS), 0) + part.start
    return halves(jnp.where(row == lane((n, DOFS)), 1.0, 0.0) - s_ref[part])


def start_all(pairs, sems, second=()):
    copies = [pltpu.make_async_copy(src, dst, sems.at[i]) for i, (src, dst) in enumerate(pairs)]
    for i, copy in enumerate(copies):
        copy.start(priority=1 if i in second else 0)
    return copies


def fetch(names, sems, rhs=None, s=None, m=None, l=None):
    pairs = {"rhs": [rhs], "s": [s], "l": [l], "m": []}
    for i in range(DOFS // LANES if m else 0):
        block = slice(i * LANES, (i + 1) * LANES)
        pairs["m"].append((m[0].at[block, block], m[1].at[i]))
    counts = [len(pairs[name]) for name in names]
    first = [sum(counts[:i]) for i in range(len(names))]
    second = first[names.index("rhs")] if "rhs" in names else -1
    copies = start_all([pair for name in names for pair in pairs[name]], sems, [second])

    def wait(name):
        i = names.index(name)
        for copy in copies[first[i] : first[i] + counts[i]]:
            copy.wait()

    return wait


def diagonal_rows(d_ref):
    here = lax.broadcasted_iota(jnp.int32, (LANES, LANES), 0) == lane((LANES, LANES))
    return jnp.concatenate(
        [jnp.sum(jnp.where(here, d_ref[i], 0.0), 0, keepdims=True) for i in range(d_ref.shape[0])], 0
    )


def traces(u, split, pick, scale):
    lower = lane((u.shape[0], LANES)) < FACE
    picked = dot(split[0], pick) + dot(split[1], pick)
    x_pair = jnp.where(lower, u[:, :LANES], u[:, DOFS - LANES :]) * scale
    return x_pair, picked[:, :LANES] * scale, picked[:, LANES:] * scale


def smooth_kernel(sizes, rhs_hbm, s_hbm, coef_hbm, lab_hbm, rt_hbm, c_hbm,
                  uh_ref, ul_ref, th_ref, nh_ref, tr_ref, meta_ref, xy_ref, z1_ref, z2_ref, rt_ref, c_ref, rn_ref,
                  rhs_ref, s_ref, coef_ref, lab_ref, t_ref, sems):
    ngx, ngy, ngz = sizes
    gx, gy, gz = position(sizes)
    half = DOFS // 2
    blocks = [slice(0, half), slice(half, DOFS)]
    pairs = [(coef_hbm, coef_ref), (lab_hbm, lab_ref), (rt_hbm, rt_ref), (c_hbm, c_ref)]
    for part in blocks:
        quarters = [slice(part.start + i * half // 2, part.start + (i + 1) * half // 2) for i in range(2)]
        pairs += [(s_hbm.at[rows], s_ref.at[rows]) for rows in quarters]
        pairs += [(rhs_hbm.at[rows, part], rhs_ref.at[rows, part]) for rows in blocks]
    copies = start_all(pairs, sems)

    def wait(first, count):
        for copy in copies[first : first + count]:
            copy.wait()

    ex, ey, ez = lab_ref.shape
    plane = ey * ez
    pick = selection()
    wait(0, 4)
    lab = cell_rows(lab_ref)
    counts = dot(jnp.ones((8, DOFS), BF16), onehot_rows(as_row(lab)), NT)
    weights = jnp.concatenate([1.0 + counts[0:1], jnp.ones((1, FACE), F32)], 1)
    meta = jnp.concatenate([lab, weights, jnp.zeros((META - 5, LANES), F32)], 0)
    meta_ref[:META] = meta
    meta_ref[META : META + ex] = cell_rows(coef_ref)
    rc = reciprocal(meta_ref[META : META + ex])

    rt = halves(rt_ref[...])

    def near_part(part):
        near = near_identity(s_ref, part)
        nh_ref[part] = near[0]
        rn_ref[:, part] = dot3_few(rt, near)
        return near

    wait(4, 2)
    near = near_part(blocks[0])
    wait(6, 2)
    t_ref[...] = dot3(halves(rhs_ref[:, blocks[0]]), near)
    wait(8, 2)
    near = near_part(blocks[1])
    wait(10, 2)
    pairs = []
    for rows in blocks:
        t = t_ref[rows] + dot3(halves(rhs_ref[rows, blocks[1]]), near)
        th_ref[rows] = t.astype(BF16)
        u = rhs_ref[rows] - t
        split = halves(u)
        uh_ref[rows], ul_ref[rows] = split
        pairs.append(traces(u, split, pick, rc[rows]))
        for i, pair in enumerate(pairs[-1]):
            tr_ref[rows, i * LANES : (i + 1) * LANES] = pair
    x_pair, y_pair, z_pair = [jnp.concatenate([block[i] for block in pairs], 0) for i in range(3)]

    def y_rows(y):
        return jnp.concatenate(
            [y_pair[x * plane + y * ez : x * plane + (y + 1) * ez] for x in range(ex)], 0
        )

    def z_rows(z):
        return jnp.concatenate([z_pair[i * ez + z : i * ez + z + 1] for i in range(ex * ey)], 0)

    def send(ref, slot, payload):
        n = payload.shape[0]
        ref[slot, :n] = payload
        ref[slot, n:] = meta

    here = gx * ngy + gy
    send(xy_ref, jnp.where(gx < ngx - 1, here + ngy, here), pack7(x_pair[(ex - 1) * plane :]))
    send(xy_ref, jnp.where(gx > 0, here - ngy, here), pack0(x_pair[:plane]))
    send(xy_ref, jnp.where(gy < ngy - 1, here + 1, here), pack7(y_rows(ey - 1)))
    send(xy_ref, jnp.where(gy > 0, here - 1, here), pack0(y_rows(0)))
    odd = lax.rem(gz, 2) == 1
    up, down = pack7(z_rows(ez - 1)), pack0(z_rows(0))
    z1_ref[...] = jnp.concatenate([jnp.where(odd, up, down), meta], 0)
    z2_ref[...] = jnp.concatenate([jnp.where(odd, down, up), meta], 0)


def receive(sizes, dims, xy_ref, z1_ref, z2_ref):
    ngx, ngy, ngz = sizes
    gx, gy, gz = position(sizes)
    odd = lax.rem(gz, 2) == 1

    def one(got, there):
        n = got.shape[0] - META
        payload = jnp.where(there, got[:n], 0.0)
        labels = jnp.where(there, got[n : n + dims[0]], -1.0)
        weights = jnp.where(there, got[n + dims[0] : n + dims[0] + 1], 1.0)
        return payload, labels, weights

    return [
        one(xy_ref[jnp.minimum(gx + 1, ngx - 1) * ngy + gy], gx < ngx - 1),
        one(xy_ref[jnp.maximum(gx - 1, 0) * ngy + gy], gx > 0),
        one(xy_ref[gx * ngy + jnp.minimum(gy + 1, ngy - 1)], gy < ngy - 1),
        one(xy_ref[gx * ngy + jnp.maximum(gy - 1, 0)], gy > 0),
        one(jnp.where(odd, z1_ref[...], z2_ref[...]), gz < ngz - 1),
        one(jnp.where(odd, z2_ref[...], z1_ref[...]), gz > 0),
    ]


def faces(f_ref, dims, tr_ref, around):
    ex, ey, ez = dims
    lower = lane((ez, LANES)) < FACE
    inner = lax.broadcasted_iota(jnp.int32, (ez, LANES), 0)
    none = jnp.zeros((ez, LANES), F32)
    outer = None
    if around is not None:
        outer = [(unpack0 if i % 2 == 0 else unpack7)(a[0]) for i, a in enumerate(around)]

    def local(i, pair):
        if tr_ref is None:
            return none
        return tr_ref[i * ez : (i + 1) * ez, pair]

    def remote(side, strip):
        return none if outer is None else outer[side][strip]

    for x in range(ex):
        for y in range(ey):
            i = x * ey + y
            rows = slice(i * ez, (i + 1) * ez)
            pair = slice(0, LANES)
            strip = slice(y * ez, (y + 1) * ez)
            above = local(i + ey, pair) if x < ex - 1 else remote(0, strip)
            below = local(i - ey, pair) if x > 0 else remote(1, strip)
            f_ref[rows, pair] = jnp.where(lower, above, below)
            pair = slice(LANES, 2 * LANES)
            strip = slice(x * ez, (x + 1) * ez)
            above = local(i + 1, pair) if y < ey - 1 else remote(2, strip)
            below = local(i - 1, pair) if y > 0 else remote(3, strip)
            f_ref[rows, pair] = jnp.where(lower, above, below)
            pair = slice(2 * LANES, 3 * LANES)
            above = below = none
            if tr_ref is not None:
                column = tr_ref[rows, pair]
                above = jnp.where(inner == ez - 1, 0.0, pltpu.roll(column, ez - 1, 0))
                below = jnp.where(inner == 0, 0.0, pltpu.roll(column, 1, 0))
            if outer is not None:
                above = jnp.where(inner == ez - 1, outer[4][i : i + 1], above)
                below = jnp.where(inner == 0, outer[5][i : i + 1], below)
            f_ref[rows, pair] = jnp.where(lower, above, below)


def prepare_kernel(dims, l_hbm, m_hbm, uh_ref, ul_ref, th_ref, nh_ref, tr_ref, rt_ref, rn_ref,
                   p_ref, own_ref, qh_ref, ql_ref, d_out_ref, l_ref, d_ref, f_ref, sems):
    wait = fetch(("l", "m"), sems, l=(l_hbm, l_ref), m=(m_hbm, d_ref))
    faces(f_ref, dims, tr_ref, None)
    inside = halves(f_ref[...])
    near = nh_ref[...]
    pick = selection()
    wait("l")
    wait("m")
    diagonal = diagonal_rows(d_ref)
    d_out_ref[...] = diagonal
    d = as_row(diagonal)
    lift = halves(face_order(l_ref[...]))
    lrt = dot3_few(halves(rt_ref[...]), lift)
    zeros = jnp.zeros((COARSE, DOFS - FACE), F32)
    x0 = jnp.concatenate([lrt[:, :FACE], zeros], 1)
    x7 = jnp.concatenate([zeros, lrt[:, FACE:LANES]], 1)
    yz = lrt[:, LANES:]
    group = lane((COARSE, 4 * FACE)) // FACE
    spread = jnp.concatenate([jnp.where(group == f, yz, 0.0) for f in range(4)], 0)
    both = dot(jnp.concatenate(halves(spread), 0), pick, NT)
    yz = both[: 4 * COARSE] + both[4 * COARSE :]
    mrt = rt_ref[...] * d + rn_ref[...]
    q = jnp.concatenate([x0, x7, yz, mrt, jnp.zeros_like(mrt)], 0)
    rows = q.shape[0]
    both = dot(jnp.concatenate(halves(q), 0), near, NT)
    swept = q - (both[:rows] + both[rows:])
    split = halves(swept)
    of_t = dot(split[0], near, NT)
    of_f = halves(dot3_few(split, lift))
    qh_ref[...], ql_ref[...] = of_f
    of_u = halves(jnp.concatenate([q + swept * (1.0 - d), rt_ref[...] + rn_ref[...]], 0))
    by_t = dot(jnp.concatenate([of_t, rn_ref[...]], 0).astype(BF16), th_ref[...], NT)
    by_u = dot3_few(of_u, (uh_ref[...], ul_ref[...]))
    p_ref[...] = by_u[:rows] + by_t[:rows] + dot3_few(of_f, inside)
    own_ref[...] = by_u[rows:] + by_t[rows:]


def relax_kernel(sizes, dims, p_ref, own_ref, qh_ref, ql_ref, c_ref, meta_ref, xy_ref, z1_ref, z2_ref,
                 slots_ref, f_ref, bins_ref):
    ngx, ngy, ngz = sizes
    gx, gy, gz = position(sizes)
    ex, ey, ez = dims
    plane = ey * ez
    around = receive(sizes, dims, xy_ref, z1_ref, z2_ref)
    x_up, x_down, y_up, y_down, z_up, z_down = around
    q = qh_ref[...], ql_ref[...]
    rows = q[0].shape[0]
    keep = lane((rows, LANES)) < FACE

    def through(side, payload):
        pair = slice(side // 2 * LANES, (side // 2 + 1) * LANES)
        mine = keep if side % 2 == 0 else ~keep
        few = [jnp.where(mine, a[:, pair].astype(F32), 0.0).astype(BF16) for a in q]
        return dot3_few(few, halves(payload))

    added = []
    x_above, x_below = through(0, unpack0(x_up[0])), through(1, unpack7(x_down[0]))
    y_above, y_below = through(2, unpack0(y_up[0])), through(3, unpack7(y_down[0]))
    z_above, z_below = unpack0(z_up[0]), unpack7(z_down[0])
    inner = lax.broadcasted_iota(jnp.int32, (ez, LANES), 0)
    for i in range(ex * ey):
        f_ref[i * ez : (i + 1) * ez] = jnp.where(
            lane((ez, LANES)) < FACE,
            jnp.where(inner == ez - 1, z_above[i : i + 1], 0.0),
            jnp.where(inner == 0, z_below[i : i + 1], 0.0),
        )
    z_both = dot3_few([a[:, 2 * LANES :] for a in q], halves(f_ref[...]))
    at = lane((rows, LANES))
    for x in range(ex):
        tile = z_both[:, x * LANES : (x + 1) * LANES]
        up, down = (plane - ez - x * ez) % LANES, (LANES - x * ez) % LANES
        tile = tile + jnp.where(at >= plane - ez, pltpu.roll(y_above, up, 1) if up else y_above, 0.0)
        tile = tile + jnp.where(at < ez, pltpu.roll(y_below, down, 1) if down else y_below, 0.0)
        tile = tile + (x_above if x == ex - 1 else 0.0) + (x_below if x == 0 else 0.0)
        added.append(tile)
    p = p_ref[...] + jnp.concatenate(added, 1)
    own = own_ref[...]
    small = own - p[6 * COARSE : 7 * COARSE]
    p = p / as_row(meta_ref[META : META + ex])
    p_x0, p_x7, p_y0, p_y7, p_z0, p_z7 = [p[8 * f : 8 * f + 8] for f in range(6)]
    at = lane((COARSE, LANES))

    def tiles(a):
        return [a[:, x * LANES : (x + 1) * LANES] for x in range(ex)]

    none = jnp.zeros((COARSE, LANES), F32)
    total = []
    parts = [tiles(a) for a in (small, p_x0, p_x7, p_y0, p_y7, p_z0, p_z7)]
    for x in range(ex):
        s, _, _, y0, y7, z0, z7 = [a[x] for a in parts]
        s = s + (parts[1][x + 1] if x < ex - 1 else none)
        s = s + (parts[2][x - 1] if x > 0 else none)
        s = s + jnp.where(at < plane - ez, pltpu.roll(y0, LANES - ez, 1), 0.0)
        s = s + jnp.where(at >= ez, pltpu.roll(y7, ez, 1), 0.0)
        s = s + jnp.where(at % ez < ez - 1, pltpu.roll(z0, LANES - 1, 1), 0.0)
        s = s + jnp.where(at % ez > 0, pltpu.roll(z7, 1, 1), 0.0)
        total.append(s)
    total = jnp.concatenate(total, 1)

    def scatter(values, onehot):
        high, low = halves(values)
        out = dot(jnp.concatenate([high, low], 0), onehot, NT)
        return out[:COARSE] + out[COARSE:]

    def shifted(labels, shift, keep):
        return as_row(jnp.where(keep, pltpu.roll(labels, shift, 1), -1.0))

    rows = lane((ex, LANES))
    labels = meta_ref[0:ex]
    blocks = [
        (scatter(total, onehot_rows(as_row(labels))), meta_ref[ex : ex + 1]),
        (scatter(parts[2][ex - 1], onehot_rows(x_up[1][0:1])), x_up[2]),
        (scatter(parts[1][0], onehot_rows(x_down[1][ex - 1 : ex])), x_down[2]),
        (scatter(p_y7, onehot_rows(shifted(y_up[1], plane - ez, rows >= plane - ez))), y_up[2]),
        (scatter(p_y0, onehot_rows(shifted(y_down[1], ez, rows < ez))), y_down[2]),
        (scatter(p_z7, onehot_rows(shifted(z_up[1], ez - 1, rows % ez == ez - 1))), z_up[2]),
        (scatter(p_z0, onehot_rows(shifted(z_down[1], LANES - ez + 1, rows % ez == 0))), z_down[2]),
    ]
    raw = jnp.concatenate([z for z, _ in blocks], 1)
    mixed = raw + raw
    for k in range(COARSE):
        mixed = mixed - c_ref[:, k : k + 1] * raw[k : k + 1]

    def packed(block):
        rows = COARSE // 2
        return jnp.concatenate([block[:rows], block[rows:]], 1)

    b0, xu, xd, yu, yd, zu, zd = [packed(z / w[:, :FACE]) for z, w in blocks]
    a0, axu, axd, ayu, ayd, azu, azd = [
        packed(mixed[:, i * FACE : (i + 1) * FACE]) for i in range(len(blocks))
    ]

    count = slots_ref.shape[0]
    bins_ref[...] = jnp.zeros_like(bins_ref)

    def put(dx, dy, dz, share):
        there = (dy >= 0) & (dy < ngy) & (dz >= 0) & (dz < ngz)
        bins_ref[jnp.where(there, (dx * ngy + dy) * ngz + dz, count)] = share

    line = b0 + xu + xd
    sides = yu + yd + zu + zd
    for dx in range(ngx):
        same = (gx == dx).astype(F32)
        up = (gx + 1 == dx).astype(F32)
        down = (gx - 1 == dx).astype(F32)
        column = same * b0 + up * xu + down * xd
        put(dx, gy, gz, line + same * (sides + a0) + up * axu + down * axd)
        put(dx, gy + 1, gz, yu + column + same * ayu)
        put(dx, gy - 1, gz, yd + column + same * ayd)
        put(dx, gy, gz + 1, zu + column + same * azu)
        put(dx, gy, gz - 1, zd + column + same * azd)
    put(gx, gy + 2, gz, yu)
    put(gx, gy - 2, gz, yd)
    put(gx, gy, gz + 2, zu)
    put(gx, gy, gz - 2, zd)
    put(gx, gy + 1, gz + 1, yu + zu)
    put(gx, gy + 1, gz - 1, yu + zd)
    put(gx, gy - 1, gz + 1, yd + zu)
    put(gx, gy - 1, gz - 1, yd + zd)
    slots_ref[...] = bins_ref[:count]


def second_kernel(sizes, dims, rhs_hbm, s_hbm, l_hbm, uh_ref, ul_ref, tr_ref, d_ref, meta_ref, rt_ref, xy_ref, z1_ref, z2_ref,
                  second_ref, rs_ref, oh_ref, rhs_ref, s_ref, l_ref, f_ref, sems):
    wait = fetch(("l", "s", "rhs"), sems, rhs=(rhs_hbm, rhs_ref), s=(s_hbm, s_ref), l=(l_hbm, l_ref))
    ex = dims[0]
    faces(f_ref, dims, tr_ref, receive(sizes, dims, xy_ref, z1_ref, z2_ref))
    onehot = onehot_rows(as_row(meta_ref[:ex]))
    oh_ref[...] = jnp.concatenate([onehot, onehot], 0).astype(F32).T.astype(BF16)
    rt = halves(rt_ref[...])
    rs_ref[...] = jnp.concatenate([rt[0], rt[0], rt[1], jnp.zeros_like(rt[0])], 0)
    wait("l")
    r1 = dot3(halves(f_ref[...]), halves(face_order(l_ref[...])))
    wait("s")
    near = near_identity(s_ref, slice(0, DOFS))
    wait("rhs")
    u = uh_ref[...].astype(F32) + ul_ref[...].astype(F32)
    d = as_row(d_ref[...])
    r1 = r1 + dot3(halves(rhs_ref[...] - u), near) + u * (1.0 - d)
    v = u + (r1 - dot3(halves(r1), near))
    rc = reciprocal(meta_ref[META : META + ex])
    second_ref[...] = v * jnp.concatenate([rc] * (DOFS // LANES), 1)


def correct_kernel(second_ref, slots_ref, meta_ref, oh_ref, rs_ref, out_hbm, out_ref, sems):
    total = jnp.sum(slots_ref[...], 0)
    ztwo = jnp.concatenate([total[:, :FACE], total[:, FACE:]], 0) / meta_ref[4:5, :FACE]
    high, low = halves(ztwo)
    stacked = jnp.concatenate([high, low, high, jnp.zeros_like(high)], 0)
    prolonged = dot(stacked, rs_ref[...], TN)
    prolonged = jnp.concatenate(halves(prolonged), 0)
    chunk = DOFS // sems.shape[0]
    copies = []
    for i in range(sems.shape[0]):
        rows = slice(i * chunk, (i + 1) * chunk)
        out_ref[rows] = second_ref[rows] + dot(oh_ref[rows], prolonged)
        copy = pltpu.make_async_copy(out_ref.at[rows], out_hbm.at[rows], sems.at[i])
        copy.start()
        copies.append(copy)
    for copy in copies:
        copy.wait()


def shards(sizes, rhs, coef, mass, smoother, lift, restrict, coarse_block_matrix, element_cluster_index):
    ngx, ngy, ngz = sizes
    dims = coef.shape
    ex, ey, ez = dims
    flat = rhs.reshape(ex * ey * ez, DOFS)
    face = ey * ez * FACE // LANES
    tip = ex * ey * FACE // LANES
    params = pltpu.CompilerParams(vmem_limit_bytes=40 * 1024 * 1024)
    shape = jax.ShapeDtypeStruct
    hbm = pl.BlockSpec(memory_space=pltpu.HBM)
    vmem = pl.BlockSpec(memory_space=pltpu.VMEM)
    cost = pl.CostEstimate(flops=2 * 10**9, bytes_accessed=4 * 2**20, transcendentals=0)
    def far(*arrays):
        return [pltpu.with_memory_space_constraint(a, pltpu.HBM) for a in arrays]

    full = shape((DOFS, DOFS), F32)
    split = shape((DOFS, DOFS), BF16)
    count = ngx * ngy * ngz
    wide = shape((8 * COARSE, 3 * LANES), BF16)
    few = shape((COARSE, DOFS), F32)
    uh, ul, th, nh, tr, meta, xy, z1, z2, rt, c, rn = pl.pallas_call(
        functools.partial(smooth_kernel, sizes),
        out_shape=(
            split,
            split,
            split,
            split,
            shape((DOFS, 3 * LANES), F32),
            shape((2 * META, LANES), F32),
            shape((ngx * ngy, face + META, LANES), F32),
            shape((tip + META, LANES), F32),
            shape((tip + META, LANES), F32),
            few,
            shape((COARSE, COARSE), F32),
            few,
        ),
        in_specs=[hbm] * 6,
        scratch_shapes=[
            pltpu.VMEM((DOFS, DOFS), F32),
            pltpu.VMEM((DOFS, DOFS), F32),
            pltpu.VMEM(dims, F32),
            pltpu.VMEM(dims, jnp.int32),
            pltpu.VMEM((DOFS, DOFS), F32),
            pltpu.SemaphoreType.DMA((12,)),
        ],
        compiler_params=params,
        cost_estimate=cost,
        name="smooth",
    )(*far(flat, smoother, coef, element_cluster_index, restrict.T, coarse_block_matrix))
    def swaps(start):
        pairs = [(i, i + 1) for i in range(start, ngz - 1, 2)]
        return pairs + [(j, i) for i, j in pairs]

    z1 = lax.ppermute(z1, "gz", swaps(1))
    z2 = lax.ppermute(z2, "gz", swaps(0))
    xy = lax.all_to_all(xy, ("gx", "gy"), 0, 0, tiled=True)
    p, own, fh, fl, d = pl.pallas_call(
        functools.partial(prepare_kernel, dims),
        out_shape=(shape((8 * COARSE, DOFS), F32), few, wide, wide, shape((DOFS // LANES, LANES), F32)),
        in_specs=[hbm] * 2 + [vmem] * 7,
        scratch_shapes=[
            pltpu.VMEM((3 * LANES, DOFS), F32),
            pltpu.VMEM((DOFS // LANES, LANES, LANES), F32),
            pltpu.VMEM((DOFS, 3 * LANES), F32),
            pltpu.SemaphoreType.DMA((5,)),
        ],
        compiler_params=params,
        cost_estimate=cost,
        name="prepare",
    )(*far(lift, mass), uh, ul, th, nh, tr, rt, rn)
    slots = pl.pallas_call(
        functools.partial(relax_kernel, sizes, dims),
        out_shape=shape((count, COARSE // 2, LANES), F32),
        scratch_shapes=[
            pltpu.VMEM((DOFS, LANES), F32),
            pltpu.VMEM((count + 1, COARSE // 2, LANES), F32),
        ],
        compiler_params=params,
        cost_estimate=cost,
        name="relax",
    )(p, own, fh, fl, c, meta, xy, z1, z2)
    slots = lax.all_to_all(slots, ("gx", "gy", "gz"), 0, 0, tiled=True)
    second, rs, oh = pl.pallas_call(
        functools.partial(second_kernel, sizes, dims),
        out_shape=(
            full,
            shape((4 * COARSE, DOFS), BF16),
            shape((DOFS, LANES), BF16),
        ),
        in_specs=[hbm] * 3 + [vmem] * 9,
        scratch_shapes=[
            pltpu.VMEM((DOFS, DOFS), F32),
            pltpu.VMEM((DOFS, DOFS), F32),
            pltpu.VMEM((3 * LANES, DOFS), F32),
            pltpu.VMEM((DOFS, 3 * LANES), F32),
            pltpu.SemaphoreType.DMA((3,)),
        ],
        compiler_params=params,
        cost_estimate=cost,
        name="second",
    )(*far(flat, smoother, lift), uh, ul, tr, d, meta, rt, xy, z1, z2)
    out = pl.pallas_call(
        correct_kernel,
        out_shape=shape((DOFS, DOFS), F32),
        out_specs=hbm,
        scratch_shapes=[pltpu.VMEM((DOFS, DOFS), F32), pltpu.SemaphoreType.DMA((4,))],
        compiler_params=params,
        name="correct",
    )(second, slots, meta, oh, rs)
    return out.reshape(rhs.shape)


def solution(mesh):
    sizes = (mesh.shape["gx"], mesh.shape["gy"], mesh.shape["gz"])
    cells = P("gx", "gy", "gz")
    return jax.shard_map(
        functools.partial(shards, sizes),
        mesh=mesh,
        in_specs=(P("gx", "gy", "gz", None), cells, P(), P(), P(), P(), P(), cells),
        out_specs=P("gx", "gy", "gz", None),
        check_vma=False,
    )
```

```python
import functools

import jax
import jax.numpy as jnp
from jax import lax
from jax.experimental import pallas as pl
from jax.experimental.pallas import tpu as pltpu
from jax.sharding import PartitionSpec as P

EDGE = 8
DOFS = 512
FACE = 64
COARSE = 8
CLUSTERS = 64
LANES = 128
META = 8

F32 = jnp.float32
BF16 = jnp.bfloat16
NT = (((1,), (1,)), ((), ()))
TN = (((0,), (0,)), ((), ()))


def selection():
    column = lane((1, 4 * FACE))
    face, a, b = column // FACE, column % FACE // EDGE, column % EDGE
    node = jnp.where(face < 2, a * 64 + face * 56 + b, a * 64 + b * 8 + (face - 2) * 7)
    at = lax.broadcasted_iota(jnp.int32, (DOFS, 4 * FACE), 0)
    return jnp.where(at == node, 1.0, 0.0).astype(BF16)


def halves(x):
    high = x.astype(BF16)
    return high, (x - high.astype(F32)).astype(BF16)


def dot(a, b, dims=(((1,), (0,)), ((), ()))):
    return lax.dot_general(a, b, dims, preferred_element_type=F32)


def dot3(a, b):
    return dot(jnp.concatenate([a[0], a[0], a[1]], 1), jnp.concatenate([b[0], b[1], b[0]], 0))


def dot3_few(a, b):
    n = a[0].shape[0]
    both = dot(jnp.concatenate(a, 0), b[0], NT)
    return both[:n] + (both[n:] + dot(a[0], b[1], NT))


def lane(shape):
    return lax.broadcasted_iota(jnp.int32, shape, len(shape) - 1)


def swap(x):
    return pltpu.roll(x, FACE, 1)


def pack0(t):
    n = t.shape[0] // 2
    return jnp.where(lane((n, LANES)) < FACE, t[:n], swap(t[n:]))


def pack7(t):
    n = t.shape[0] // 2
    return jnp.where(lane((n, LANES)) < FACE, swap(t[:n]), t[n:])


def unpack0(p):
    return jnp.concatenate([p, swap(p)], 0)


def unpack7(p):
    return jnp.concatenate([swap(p), p], 0)


def cell_rows(ref):
    ex, ey, ez = ref.shape
    rows = []
    for x in range(ex):
        rows.append(jnp.concatenate([ref[x, y : y + 1, :] for y in range(ey)], 1))
    return jnp.concatenate(rows, 0).astype(F32)


def face_order(lift):
    return jnp.concatenate([lift[(f ^ 1) * FACE : ((f ^ 1) + 1) * FACE] for f in range(6)], 0)


def reciprocal(rows):
    n = rows.shape[0]
    columns = (1.0 / jnp.concatenate([rows, jnp.ones((LANES - n, LANES), F32)], 0)).T
    return jnp.concatenate([jnp.broadcast_to(columns[:, x : x + 1], (LANES, LANES)) for x in range(n)], 0)


def as_row(rows):
    return jnp.concatenate([rows[x : x + 1] for x in range(rows.shape[0])], 1)


def onehot_rows(row):
    n = row.shape[1]
    at = lax.broadcasted_iota(jnp.int32, (CLUSTERS, n), 0).astype(F32)
    return jnp.where(at == row, 1.0, 0.0).astype(BF16)


def position(sizes):
    return lax.axis_index("gx"), lax.axis_index("gy"), lax.axis_index("gz")


def near_identity(s_ref, part):
    n = part.stop - part.start
    row = lax.broadcasted_iota(jnp.int32, (n, DOFS), 0) + part.start
    return halves(jnp.where(row == lane((n, DOFS)), 1.0, 0.0) - s_ref[part])


def start_all(pairs, sems):
    copies = [pltpu.make_async_copy(src, dst, sems.at[i]) for i, (src, dst) in enumerate(pairs)]
    for copy in copies:
        copy.start()
    return copies


def fetch(names, sems, rhs=None, s=None, m=None, l=None):
    pairs = {"rhs": [rhs], "s": [s], "l": [l], "m": []}
    for i in range(DOFS // LANES if m else 0):
        block = slice(i * LANES, (i + 1) * LANES)
        pairs["m"].append((m[0].at[block, block], m[1].at[i]))
    counts = [len(pairs[name]) for name in names]
    first = [sum(counts[:i]) for i in range(len(names))]
    copies = start_all([pair for name in names for pair in pairs[name]], sems)

    def wait(name):
        i = names.index(name)
        for copy in copies[first[i] : first[i] + counts[i]]:
            copy.wait()

    return wait


def diagonal_rows(d_ref):
    here = lax.broadcasted_iota(jnp.int32, (LANES, LANES), 0) == lane((LANES, LANES))
    return jnp.concatenate(
        [jnp.sum(jnp.where(here, d_ref[i], 0.0), 0, keepdims=True) for i in range(d_ref.shape[0])], 0
    )


def traces(u, split, pick, scale):
    lower = lane((u.shape[0], LANES)) < FACE
    picked = dot(split[0], pick) + dot(split[1], pick)
    x_pair = jnp.where(lower, u[:, :LANES], u[:, DOFS - LANES :]) * scale
    return x_pair, picked[:, :LANES] * scale, picked[:, LANES:] * scale


def smooth_kernel(sizes, rhs_hbm, s_hbm, coef_hbm, lab_hbm, rt_hbm, c_hbm,
                  uh_ref, ul_ref, th_ref, nh_ref, tr_ref, meta_ref, xy_ref, z1_ref, z2_ref, rt_ref, c_ref, rn_ref,
                  rhs_ref, s_ref, coef_ref, lab_ref, t_ref, sems):
    ngx, ngy, ngz = sizes
    gx, gy, gz = position(sizes)
    half = DOFS // 2
    blocks = [slice(0, half), slice(half, DOFS)]
    pairs = [(coef_hbm, coef_ref), (lab_hbm, lab_ref), (rt_hbm, rt_ref), (c_hbm, c_ref)]
    for part in blocks:
        quarters = [slice(part.start + i * half // 2, part.start + (i + 1) * half // 2) for i in range(2)]
        pairs += [(s_hbm.at[rows], s_ref.at[rows]) for rows in quarters]
        pairs += [(rhs_hbm.at[rows, part], rhs_ref.at[rows, part]) for rows in blocks]
    copies = start_all(pairs, sems)

    def wait(first, count):
        for copy in copies[first : first + count]:
            copy.wait()

    ex, ey, ez = lab_ref.shape
    plane = ey * ez
    pick = selection()
    wait(0, 4)
    lab = cell_rows(lab_ref)
    counts = dot(jnp.ones((8, DOFS), BF16), onehot_rows(as_row(lab)), NT)
    weights = jnp.concatenate([1.0 + counts[0:1], jnp.ones((1, FACE), F32)], 1)
    meta = jnp.concatenate([lab, weights, jnp.zeros((META - 5, LANES), F32)], 0)
    meta_ref[:META] = meta
    meta_ref[META : META + ex] = cell_rows(coef_ref)
    rc = reciprocal(meta_ref[META : META + ex])

    rt = halves(rt_ref[...])

    def near_part(part):
        near = near_identity(s_ref, part)
        nh_ref[part] = near[0]
        rn_ref[:, part] = dot3_few(rt, near)
        return near

    wait(4, 2)
    near = near_part(blocks[0])
    wait(6, 2)
    t_ref[...] = dot3(halves(rhs_ref[:, blocks[0]]), near)
    wait(8, 2)
    near = near_part(blocks[1])
    wait(10, 2)
    pairs = []
    for rows in blocks:
        t = t_ref[rows] + dot3(halves(rhs_ref[rows, blocks[1]]), near)
        th_ref[rows] = t.astype(BF16)
        u = rhs_ref[rows] - t
        split = halves(u)
        uh_ref[rows], ul_ref[rows] = split
        pairs.append(traces(u, split, pick, rc[rows]))
        for i, pair in enumerate(pairs[-1]):
            tr_ref[rows, i * LANES : (i + 1) * LANES] = pair
    x_pair, y_pair, z_pair = [jnp.concatenate([block[i] for block in pairs], 0) for i in range(3)]

    def y_rows(y):
        return jnp.concatenate(
            [y_pair[x * plane + y * ez : x * plane + (y + 1) * ez] for x in range(ex)], 0
        )

    def z_rows(z):
        return jnp.concatenate([z_pair[i * ez + z : i * ez + z + 1] for i in range(ex * ey)], 0)

    def send(ref, slot, payload):
        n = payload.shape[0]
        ref[slot, :n] = payload
        ref[slot, n:] = meta

    here = gx * ngy + gy
    send(xy_ref, jnp.where(gx < ngx - 1, here + ngy, here), pack7(x_pair[(ex - 1) * plane :]))
    send(xy_ref, jnp.where(gx > 0, here - ngy, here), pack0(x_pair[:plane]))
    send(xy_ref, jnp.where(gy < ngy - 1, here + 1, here), pack7(y_rows(ey - 1)))
    send(xy_ref, jnp.where(gy > 0, here - 1, here), pack0(y_rows(0)))
    odd = lax.rem(gz, 2) == 1
    up, down = pack7(z_rows(ez - 1)), pack0(z_rows(0))
    z1_ref[...] = jnp.concatenate([jnp.where(odd, up, down), meta], 0)
    z2_ref[...] = jnp.concatenate([jnp.where(odd, down, up), meta], 0)


def receive(sizes, dims, xy_ref, z1_ref, z2_ref):
    ngx, ngy, ngz = sizes
    gx, gy, gz = position(sizes)
    odd = lax.rem(gz, 2) == 1

    def one(got, there):
        n = got.shape[0] - META
        payload = jnp.where(there, got[:n], 0.0)
        labels = jnp.where(there, got[n : n + dims[0]], -1.0)
        weights = jnp.where(there, got[n + dims[0] : n + dims[0] + 1], 1.0)
        return payload, labels, weights

    return [
        one(xy_ref[jnp.minimum(gx + 1, ngx - 1) * ngy + gy], gx < ngx - 1),
        one(xy_ref[jnp.maximum(gx - 1, 0) * ngy + gy], gx > 0),
        one(xy_ref[gx * ngy + jnp.minimum(gy + 1, ngy - 1)], gy < ngy - 1),
        one(xy_ref[gx * ngy + jnp.maximum(gy - 1, 0)], gy > 0),
        one(jnp.where(odd, z1_ref[...], z2_ref[...]), gz < ngz - 1),
        one(jnp.where(odd, z2_ref[...], z1_ref[...]), gz > 0),
    ]


def faces(f_ref, dims, tr_ref, around):
    ex, ey, ez = dims
    lower = lane((ez, LANES)) < FACE
    inner = lax.broadcasted_iota(jnp.int32, (ez, LANES), 0)
    none = jnp.zeros((ez, LANES), F32)
    outer = None
    if around is not None:
        outer = [(unpack0 if i % 2 == 0 else unpack7)(a[0]) for i, a in enumerate(around)]

    def local(i, pair):
        if tr_ref is None:
            return none
        return tr_ref[i * ez : (i + 1) * ez, pair]

    def remote(side, strip):
        return none if outer is None else outer[side][strip]

    for x in range(ex):
        for y in range(ey):
            i = x * ey + y
            rows = slice(i * ez, (i + 1) * ez)
            pair = slice(0, LANES)
            strip = slice(y * ez, (y + 1) * ez)
            above = local(i + ey, pair) if x < ex - 1 else remote(0, strip)
            below = local(i - ey, pair) if x > 0 else remote(1, strip)
            f_ref[rows, pair] = jnp.where(lower, above, below)
            pair = slice(LANES, 2 * LANES)
            strip = slice(x * ez, (x + 1) * ez)
            above = local(i + 1, pair) if y < ey - 1 else remote(2, strip)
            below = local(i - 1, pair) if y > 0 else remote(3, strip)
            f_ref[rows, pair] = jnp.where(lower, above, below)
            pair = slice(2 * LANES, 3 * LANES)
            above = below = none
            if tr_ref is not None:
                column = tr_ref[rows, pair]
                above = jnp.where(inner == ez - 1, 0.0, pltpu.roll(column, ez - 1, 0))
                below = jnp.where(inner == 0, 0.0, pltpu.roll(column, 1, 0))
            if outer is not None:
                above = jnp.where(inner == ez - 1, outer[4][i : i + 1], above)
                below = jnp.where(inner == 0, outer[5][i : i + 1], below)
            f_ref[rows, pair] = jnp.where(lower, above, below)


def prepare_kernel(dims, l_hbm, m_hbm, uh_ref, ul_ref, th_ref, nh_ref, tr_ref, rt_ref, rn_ref,
                   p_ref, own_ref, qh_ref, ql_ref, d_out_ref, l_ref, d_ref, f_ref, sems):
    wait = fetch(("l", "m"), sems, l=(l_hbm, l_ref), m=(m_hbm, d_ref))
    faces(f_ref, dims, tr_ref, None)
    inside = halves(f_ref[...])
    near = nh_ref[...]
    pick = selection()
    wait("l")
    wait("m")
    diagonal = diagonal_rows(d_ref)
    d_out_ref[...] = diagonal
    d = as_row(diagonal)
    lift = halves(face_order(l_ref[...]))
    lrt = dot3_few(halves(rt_ref[...]), lift)
    zeros = jnp.zeros((COARSE, DOFS - FACE), F32)
    x0 = jnp.concatenate([lrt[:, :FACE], zeros], 1)
    x7 = jnp.concatenate([zeros, lrt[:, FACE:LANES]], 1)
    yz = lrt[:, LANES:]
    group = lane((COARSE, 4 * FACE)) // FACE
    spread = jnp.concatenate([jnp.where(group == f, yz, 0.0) for f in range(4)], 0)
    both = dot(jnp.concatenate(halves(spread), 0), pick, NT)
    yz = both[: 4 * COARSE] + both[4 * COARSE :]
    mrt = rt_ref[...] * d + rn_ref[...]
    q = jnp.concatenate([x0, x7, yz, mrt, jnp.zeros_like(mrt)], 0)
    rows = q.shape[0]
    both = dot(jnp.concatenate(halves(q), 0), near, NT)
    swept = q - (both[:rows] + both[rows:])
    split = halves(swept)
    of_t = dot(split[0], near, NT)
    of_f = halves(dot3_few(split, lift))
    qh_ref[...], ql_ref[...] = of_f
    of_u = halves(jnp.concatenate([q + swept * (1.0 - d), rt_ref[...] + rn_ref[...]], 0))
    by_t = dot(jnp.concatenate([of_t, rn_ref[...]], 0).astype(BF16), th_ref[...], NT)
    by_u = dot3_few(of_u, (uh_ref[...], ul_ref[...]))
    p_ref[...] = by_u[:rows] + by_t[:rows] + dot3_few(of_f, inside)
    own_ref[...] = by_u[rows:] + by_t[rows:]


def relax_kernel(sizes, dims, p_ref, own_ref, qh_ref, ql_ref, c_ref, meta_ref, xy_ref, z1_ref, z2_ref,
                 slots_ref, f_ref, bins_ref):
    ngx, ngy, ngz = sizes
    gx, gy, gz = position(sizes)
    ex, ey, ez = dims
    plane = ey * ez
    around = receive(sizes, dims, xy_ref, z1_ref, z2_ref)
    x_up, x_down, y_up, y_down, z_up, z_down = around
    q = qh_ref[...], ql_ref[...]
    rows = q[0].shape[0]
    keep = lane((rows, LANES)) < FACE

    def through(side, payload):
        pair = slice(side // 2 * LANES, (side // 2 + 1) * LANES)
        mine = keep if side % 2 == 0 else ~keep
        few = [jnp.where(mine, a[:, pair].astype(F32), 0.0).astype(BF16) for a in q]
        return dot3_few(few, halves(payload))

    added = []
    x_above, x_below = through(0, unpack0(x_up[0])), through(1, unpack7(x_down[0]))
    y_above, y_below = through(2, unpack0(y_up[0])), through(3, unpack7(y_down[0]))
    z_above, z_below = unpack0(z_up[0]), unpack7(z_down[0])
    inner = lax.broadcasted_iota(jnp.int32, (ez, LANES), 0)
    for i in range(ex * ey):
        f_ref[i * ez : (i + 1) * ez] = jnp.where(
            lane((ez, LANES)) < FACE,
            jnp.where(inner == ez - 1, z_above[i : i + 1], 0.0),
            jnp.where(inner == 0, z_below[i : i + 1], 0.0),
        )
    z_both = dot3_few([a[:, 2 * LANES :] for a in q], halves(f_ref[...]))
    at = lane((rows, LANES))
    for x in range(ex):
        tile = z_both[:, x * LANES : (x + 1) * LANES]
        up, down = (plane - ez - x * ez) % LANES, (LANES - x * ez) % LANES
        tile = tile + jnp.where(at >= plane - ez, pltpu.roll(y_above, up, 1) if up else y_above, 0.0)
        tile = tile + jnp.where(at < ez, pltpu.roll(y_below, down, 1) if down else y_below, 0.0)
        tile = tile + (x_above if x == ex - 1 else 0.0) + (x_below if x == 0 else 0.0)
        added.append(tile)
    p = p_ref[...] + jnp.concatenate(added, 1)
    own = own_ref[...]
    small = own - p[6 * COARSE : 7 * COARSE]
    p = p / as_row(meta_ref[META : META + ex])
    p_x0, p_x7, p_y0, p_y7, p_z0, p_z7 = [p[8 * f : 8 * f + 8] for f in range(6)]
    at = lane((COARSE, LANES))

    def tiles(a):
        return [a[:, x * LANES : (x + 1) * LANES] for x in range(ex)]

    none = jnp.zeros((COARSE, LANES), F32)
    total = []
    parts = [tiles(a) for a in (small, p_x0, p_x7, p_y0, p_y7, p_z0, p_z7)]
    for x in range(ex):
        s, _, _, y0, y7, z0, z7 = [a[x] for a in parts]
        s = s + (parts[1][x + 1] if x < ex - 1 else none)
        s = s + (parts[2][x - 1] if x > 0 else none)
        s = s + jnp.where(at < plane - ez, pltpu.roll(y0, LANES - ez, 1), 0.0)
        s = s + jnp.where(at >= ez, pltpu.roll(y7, ez, 1), 0.0)
        s = s + jnp.where(at % ez < ez - 1, pltpu.roll(z0, LANES - 1, 1), 0.0)
        s = s + jnp.where(at % ez > 0, pltpu.roll(z7, 1, 1), 0.0)
        total.append(s)
    total = jnp.concatenate(total, 1)

    def scatter(values, onehot):
        high, low = halves(values)
        out = dot(jnp.concatenate([high, low], 0), onehot, NT)
        return out[:COARSE] + out[COARSE:]

    def shifted(labels, shift, keep):
        return as_row(jnp.where(keep, pltpu.roll(labels, shift, 1), -1.0))

    rows = lane((ex, LANES))
    labels = meta_ref[0:ex]
    blocks = [
        (scatter(total, onehot_rows(as_row(labels))), meta_ref[ex : ex + 1]),
        (scatter(parts[2][ex - 1], onehot_rows(x_up[1][0:1])), x_up[2]),
        (scatter(parts[1][0], onehot_rows(x_down[1][ex - 1 : ex])), x_down[2]),
        (scatter(p_y7, onehot_rows(shifted(y_up[1], plane - ez, rows >= plane - ez))), y_up[2]),
        (scatter(p_y0, onehot_rows(shifted(y_down[1], ez, rows < ez))), y_down[2]),
        (scatter(p_z7, onehot_rows(shifted(z_up[1], ez - 1, rows % ez == ez - 1))), z_up[2]),
        (scatter(p_z0, onehot_rows(shifted(z_down[1], LANES - ez + 1, rows % ez == 0))), z_down[2]),
    ]
    raw = jnp.concatenate([z for z, _ in blocks], 1)
    mixed = raw + raw
    for k in range(COARSE):
        mixed = mixed - c_ref[:, k : k + 1] * raw[k : k + 1]

    def packed(block):
        rows = COARSE // 2
        return jnp.concatenate([block[:rows], block[rows:]], 1)

    b0, xu, xd, yu, yd, zu, zd = [packed(z / w[:, :FACE]) for z, w in blocks]
    a0, axu, axd, ayu, ayd, azu, azd = [
        packed(mixed[:, i * FACE : (i + 1) * FACE]) for i in range(len(blocks))
    ]

    count = slots_ref.shape[0]
    bins_ref[...] = jnp.zeros_like(bins_ref)

    def put(dx, dy, dz, share):
        there = (dy >= 0) & (dy < ngy) & (dz >= 0) & (dz < ngz)
        bins_ref[jnp.where(there, (dx * ngy + dy) * ngz + dz, count)] = share

    line = b0 + xu + xd
    sides = yu + yd + zu + zd
    for dx in range(ngx):
        same = (gx == dx).astype(F32)
        up = (gx + 1 == dx).astype(F32)
        down = (gx - 1 == dx).astype(F32)
        column = same * b0 + up * xu + down * xd
        put(dx, gy, gz, line + same * (sides + a0) + up * axu + down * axd)
        put(dx, gy + 1, gz, yu + column + same * ayu)
        put(dx, gy - 1, gz, yd + column + same * ayd)
        put(dx, gy, gz + 1, zu + column + same * azu)
        put(dx, gy, gz - 1, zd + column + same * azd)
    put(gx, gy + 2, gz, yu)
    put(gx, gy - 2, gz, yd)
    put(gx, gy, gz + 2, zu)
    put(gx, gy, gz - 2, zd)
    put(gx, gy + 1, gz + 1, yu + zu)
    put(gx, gy + 1, gz - 1, yu + zd)
    put(gx, gy - 1, gz + 1, yd + zu)
    put(gx, gy - 1, gz - 1, yd + zd)
    slots_ref[...] = bins_ref[:count]


def second_kernel(sizes, dims, rhs_hbm, s_hbm, l_hbm, uh_ref, ul_ref, tr_ref, d_ref, meta_ref, rt_ref, xy_ref, z1_ref, z2_ref,
                  second_ref, rs_ref, oh_ref, rhs_ref, s_ref, l_ref, f_ref, sems):
    wait = fetch(("l", "s", "rhs"), sems, rhs=(rhs_hbm, rhs_ref), s=(s_hbm, s_ref), l=(l_hbm, l_ref))
    ex = dims[0]
    faces(f_ref, dims, tr_ref, receive(sizes, dims, xy_ref, z1_ref, z2_ref))
    onehot = onehot_rows(as_row(meta_ref[:ex]))
    oh_ref[...] = jnp.concatenate([onehot, onehot], 0).astype(F32).T.astype(BF16)
    rt = halves(rt_ref[...])
    rs_ref[...] = jnp.concatenate([rt[0], rt[0], rt[1], jnp.zeros_like(rt[0])], 0)
    wait("l")
    r1 = dot3(halves(f_ref[...]), halves(face_order(l_ref[...])))
    wait("s")
    near = near_identity(s_ref, slice(0, DOFS))
    wait("rhs")
    u = uh_ref[...].astype(F32) + ul_ref[...].astype(F32)
    d = as_row(d_ref[...])
    r1 = r1 + dot3(halves(rhs_ref[...] - u), near) + u * (1.0 - d)
    v = u + (r1 - dot3(halves(r1), near))
    rc = reciprocal(meta_ref[META : META + ex])
    second_ref[...] = v * jnp.concatenate([rc] * (DOFS // LANES), 1)


def correct_kernel(second_ref, slots_ref, meta_ref, oh_ref, rs_ref, out_hbm, out_ref, sems):
    total = jnp.sum(slots_ref[...], 0)
    ztwo = jnp.concatenate([total[:, :FACE], total[:, FACE:]], 0) / meta_ref[4:5, :FACE]
    high, low = halves(ztwo)
    stacked = jnp.concatenate([high, low, high, jnp.zeros_like(high)], 0)
    prolonged = dot(stacked, rs_ref[...], TN)
    prolonged = jnp.concatenate(halves(prolonged), 0)
    chunk = DOFS // sems.shape[0]
    copies = []
    for i in range(sems.shape[0]):
        rows = slice(i * chunk, (i + 1) * chunk)
        out_ref[rows] = second_ref[rows] + dot(oh_ref[rows], prolonged)
        copy = pltpu.make_async_copy(out_ref.at[rows], out_hbm.at[rows], sems.at[i])
        copy.start()
        copies.append(copy)
    for copy in copies:
        copy.wait()


def shards(sizes, rhs, coef, mass, smoother, lift, restrict, coarse_block_matrix, element_cluster_index):
    ngx, ngy, ngz = sizes
    dims = coef.shape
    ex, ey, ez = dims
    flat = rhs.reshape(ex * ey * ez, DOFS)
    face = ey * ez * FACE // LANES
    tip = ex * ey * FACE // LANES
    params = pltpu.CompilerParams(vmem_limit_bytes=40 * 1024 * 1024)
    shape = jax.ShapeDtypeStruct
    hbm = pl.BlockSpec(memory_space=pltpu.HBM)
    vmem = pl.BlockSpec(memory_space=pltpu.VMEM)
    cost = pl.CostEstimate(flops=2 * 10**9, bytes_accessed=4 * 2**20, transcendentals=0)
    def far(*arrays):
        return [pltpu.with_memory_space_constraint(a, pltpu.HBM) for a in arrays]

    full = shape((DOFS, DOFS), F32)
    split = shape((DOFS, DOFS), BF16)
    count = ngx * ngy * ngz
    wide = shape((8 * COARSE, 3 * LANES), BF16)
    few = shape((COARSE, DOFS), F32)
    uh, ul, th, nh, tr, meta, xy, z1, z2, rt, c, rn = pl.pallas_call(
        functools.partial(smooth_kernel, sizes),
        out_shape=(
            split,
            split,
            split,
            split,
            shape((DOFS, 3 * LANES), F32),
            shape((2 * META, LANES), F32),
            shape((ngx * ngy, face + META, LANES), F32),
            shape((tip + META, LANES), F32),
            shape((tip + META, LANES), F32),
            few,
            shape((COARSE, COARSE), F32),
            few,
        ),
        in_specs=[hbm] * 6,
        scratch_shapes=[
            pltpu.VMEM((DOFS, DOFS), F32),
            pltpu.VMEM((DOFS, DOFS), F32),
            pltpu.VMEM(dims, F32),
            pltpu.VMEM(dims, jnp.int32),
            pltpu.VMEM((DOFS, DOFS), F32),
            pltpu.SemaphoreType.DMA((12,)),
        ],
        compiler_params=params,
        cost_estimate=cost,
        name="smooth",
    )(*far(flat, smoother, coef, element_cluster_index, restrict.T, coarse_block_matrix))
    def swaps(start):
        pairs = [(i, i + 1) for i in range(start, ngz - 1, 2)]
        return pairs + [(j, i) for i, j in pairs]

    z1 = lax.ppermute(z1, "gz", swaps(1))
    z2 = lax.ppermute(z2, "gz", swaps(0))
    xy = lax.all_to_all(xy, ("gx", "gy"), 0, 0, tiled=True)
    p, own, fh, fl, d = pl.pallas_call(
        functools.partial(prepare_kernel, dims),
        out_shape=(shape((8 * COARSE, DOFS), F32), few, wide, wide, shape((DOFS // LANES, LANES), F32)),
        in_specs=[hbm] * 2 + [vmem] * 7,
        scratch_shapes=[
            pltpu.VMEM((3 * LANES, DOFS), F32),
            pltpu.VMEM((DOFS // LANES, LANES, LANES), F32),
            pltpu.VMEM((DOFS, 3 * LANES), F32),
            pltpu.SemaphoreType.DMA((5,)),
        ],
        compiler_params=params,
        cost_estimate=cost,
        name="prepare",
    )(*far(lift, mass), uh, ul, th, nh, tr, rt, rn)
    slots = pl.pallas_call(
        functools.partial(relax_kernel, sizes, dims),
        out_shape=shape((count, COARSE // 2, LANES), F32),
        scratch_shapes=[
            pltpu.VMEM((DOFS, LANES), F32),
            pltpu.VMEM((count + 1, COARSE // 2, LANES), F32),
        ],
        compiler_params=params,
        cost_estimate=cost,
        name="relax",
    )(p, own, fh, fl, c, meta, xy, z1, z2)
    slots = lax.all_to_all(slots, ("gx", "gy", "gz"), 0, 0, tiled=True)
    second, rs, oh = pl.pallas_call(
        functools.partial(second_kernel, sizes, dims),
        out_shape=(
            full,
            shape((4 * COARSE, DOFS), BF16),
            shape((DOFS, LANES), BF16),
        ),
        in_specs=[hbm] * 3 + [vmem] * 9,
        scratch_shapes=[
            pltpu.VMEM((DOFS, DOFS), F32),
            pltpu.VMEM((DOFS, DOFS), F32),
            pltpu.VMEM((3 * LANES, DOFS), F32),
            pltpu.VMEM((DOFS, 3 * LANES), F32),
            pltpu.SemaphoreType.DMA((3,)),
        ],
        compiler_params=params,
        cost_estimate=cost,
        name="second",
    )(*far(flat, smoother, lift), uh, ul, tr, d, meta, rt, xy, z1, z2)
    out = pl.pallas_call(
        correct_kernel,
        out_shape=shape((DOFS, DOFS), F32),
        out_specs=hbm,
        scratch_shapes=[pltpu.VMEM((DOFS, DOFS), F32), pltpu.SemaphoreType.DMA((4,))],
        compiler_params=params,
        name="correct",
    )(second, slots, meta, oh, rs)
    return out.reshape(rhs.shape)


def solution(mesh):
    sizes = (mesh.shape["gx"], mesh.shape["gy"], mesh.shape["gz"])
    cells = P("gx", "gy", "gz")
    return jax.shard_map(
        functools.partial(shards, sizes),
        mesh=mesh,
        in_specs=(P("gx", "gy", "gz", None), cells, P(), P(), P(), P(), P(), cells),
        out_specs=P("gx", "gy", "gz", None),
        check_vma=False,
    )
```

```python
import functools

import jax
import jax.numpy as jnp
from jax import lax
from jax.experimental import pallas as pl
from jax.experimental.pallas import tpu as pltpu
from jax.sharding import PartitionSpec as P

EDGE = 8
DOFS = 512
FACE = 64
COARSE = 8
CLUSTERS = 64
LANES = 128
META = 8

F32 = jnp.float32
BF16 = jnp.bfloat16
NT = (((1,), (1,)), ((), ()))
TN = (((0,), (0,)), ((), ()))


def selection():
    column = lane((1, 4 * FACE))
    face, a, b = column // FACE, column % FACE // EDGE, column % EDGE
    node = jnp.where(face < 2, a * 64 + face * 56 + b, a * 64 + b * 8 + (face - 2) * 7)
    at = lax.broadcasted_iota(jnp.int32, (DOFS, 4 * FACE), 0)
    return jnp.where(at == node, 1.0, 0.0).astype(BF16)


def halves(x):
    high = x.astype(BF16)
    return high, (x - high.astype(F32)).astype(BF16)


def dot(a, b, dims=(((1,), (0,)), ((), ()))):
    return lax.dot_general(a, b, dims, preferred_element_type=F32)


def dot3(a, b, dims=(((1,), (0,)), ((), ()))):
    return dot(a[0], b[0], dims) + (dot(a[0], b[1], dims) + dot(a[1], b[0], dims))


def dot3_few(a, b):
    n = a[0].shape[0]
    both = dot(jnp.concatenate(a, 0), b[0], NT)
    return both[:n] + (both[n:] + dot(a[0], b[1], NT))


def lane(shape):
    return lax.broadcasted_iota(jnp.int32, shape, len(shape) - 1)


def swap(x):
    return pltpu.roll(x, FACE, 1)


def pack0(t):
    n = t.shape[0] // 2
    return jnp.where(lane((n, LANES)) < FACE, t[:n], swap(t[n:]))


def pack7(t):
    n = t.shape[0] // 2
    return jnp.where(lane((n, LANES)) < FACE, swap(t[:n]), t[n:])


def unpack0(p):
    return jnp.concatenate([p, swap(p)], 0)


def unpack7(p):
    return jnp.concatenate([swap(p), p], 0)


def cell_rows(ref):
    ex, ey, ez = ref.shape
    rows = []
    for x in range(ex):
        rows.append(jnp.concatenate([ref[x, y : y + 1, :] for y in range(ey)], 1))
    return jnp.concatenate(rows, 0).astype(F32)


def face_order(lift):
    return jnp.concatenate([lift[(f ^ 1) * FACE : ((f ^ 1) + 1) * FACE] for f in range(6)], 0)


def reciprocal(rows):
    n = rows.shape[0]
    columns = (1.0 / jnp.concatenate([rows, jnp.ones((LANES - n, LANES), F32)], 0)).T
    return jnp.concatenate([jnp.broadcast_to(columns[:, x : x + 1], (LANES, LANES)) for x in range(n)], 0)


def as_row(rows):
    return jnp.concatenate([rows[x : x + 1] for x in range(rows.shape[0])], 1)


def onehot_rows(row):
    n = row.shape[1]
    at = lax.broadcasted_iota(jnp.int32, (CLUSTERS, n), 0).astype(F32)
    return jnp.where(at == row, 1.0, 0.0).astype(BF16)


def position(sizes):
    return lax.axis_index("gx"), lax.axis_index("gy"), lax.axis_index("gz")


def near_identity(s_ref, part):
    n = part.stop - part.start
    row = lax.broadcasted_iota(jnp.int32, (n, DOFS), 0) + part.start
    return halves(jnp.where(row == lane((n, DOFS)), 1.0, 0.0) - s_ref[part])


def start_all(pairs, sems):
    copies = [pltpu.make_async_copy(src, dst, sems.at[i]) for i, (src, dst) in enumerate(pairs)]
    for copy in copies:
        copy.start()
    return copies


def fetch(names, sems, rhs=None, s=None, m=None, l=None):
    pairs = {"rhs": [rhs], "s": [s], "l": [l], "m": []}
    for i in range(DOFS // LANES if m else 0):
        block = slice(i * LANES, (i + 1) * LANES)
        pairs["m"].append((m[0].at[block, block], m[1].at[i]))
    counts = [len(pairs[name]) for name in names]
    first = [sum(counts[:i]) for i in range(len(names))]
    copies = start_all([pair for name in names for pair in pairs[name]], sems)

    def wait(name):
        i = names.index(name)
        for copy in copies[first[i] : first[i] + counts[i]]:
            copy.wait()

    return wait


def diagonal_rows(d_ref):
    here = lax.broadcasted_iota(jnp.int32, (LANES, LANES), 0) == lane((LANES, LANES))
    return jnp.concatenate(
        [jnp.sum(jnp.where(here, d_ref[i], 0.0), 0, keepdims=True) for i in range(d_ref.shape[0])], 0
    )


def traces(u, split, pick, scale):
    lower = lane((u.shape[0], LANES)) < FACE
    picked = dot(split[0], pick) + dot(split[1], pick)
    x_pair = jnp.where(lower, u[:, :LANES], u[:, DOFS - LANES :]) * scale
    return x_pair, picked[:, :LANES] * scale, picked[:, LANES:] * scale


def smooth_kernel(sizes, rhs_hbm, s_hbm, coef_hbm, lab_hbm, rt_hbm, c_hbm,
                  uh_ref, ul_ref, th_ref, nh_ref, tr_ref, meta_ref, xy_hbm, z1_ref, z2_ref, rt_ref, c_ref, rn_ref,
                  rhs_ref, s_ref, coef_ref, lab_ref, t_ref, nl_ref, out_ref, sems, out_sems):
    ngx, ngy, ngz = sizes
    gx, gy, gz = position(sizes)
    half = DOFS // 2
    blocks = [slice(0, half), slice(half, DOFS)]
    pairs = [(coef_hbm, coef_ref), (lab_hbm, lab_ref), (rt_hbm, rt_ref), (c_hbm, c_ref)]
    for part in blocks:
        quarters = [slice(part.start + i * half // 2, part.start + (i + 1) * half // 2) for i in range(2)]
        pairs += [(s_hbm.at[rows], s_ref.at[rows]) for rows in quarters]
        pairs += [(rhs_hbm.at[rows, part], rhs_ref.at[rows, part]) for rows in blocks]
    copies = start_all(pairs, sems)

    def wait(first, count):
        for copy in copies[first : first + count]:
            copy.wait()

    ex, ey, ez = lab_ref.shape
    plane = ey * ez
    pick = selection()
    wait(0, 4)
    lab = cell_rows(lab_ref)
    counts = dot(jnp.ones((8, DOFS), BF16), onehot_rows(as_row(lab)), NT)
    weights = jnp.concatenate([1.0 + counts[0:1], jnp.ones((1, FACE), F32)], 1)
    meta = jnp.concatenate([lab, weights, jnp.zeros((META - 5, LANES), F32)], 0)
    meta_ref[:META] = meta
    meta_ref[META : META + ex] = cell_rows(coef_ref)
    rc = reciprocal(meta_ref[META : META + ex])

    def near_part(part):
        near = near_identity(s_ref, part)
        nh_ref[part], nl_ref[part] = near
        return near

    here = gx * ngy + gy
    outs = []

    def send(i, there, slot, packed):
        n = packed.shape[0]
        out_ref[i, :n] = packed
        out_ref[i, n:] = meta
        out = pltpu.make_async_copy(out_ref.at[i], xy_hbm.at[jnp.where(there, slot, here)], out_sems.at[i])
        pl.when(there)(out.start)
        outs.append((there, out))

    wait(4, 2)
    near = near_part(blocks[0])
    wait(6, 2)
    t_ref[...] = dot3(halves(rhs_ref[:, blocks[0]]), near)
    wait(8, 2)
    near = near_part(blocks[1])
    wait(10, 2)
    pairs = []
    for rows in blocks:
        t = t_ref[rows] + dot3(halves(rhs_ref[rows, blocks[1]]), near)
        th_ref[rows] = t.astype(BF16)
        u = rhs_ref[rows] - t
        split = halves(u)
        uh_ref[rows], ul_ref[rows] = split
        pairs.append(traces(u, split, pick, rc[rows]))
        for i, pair in enumerate(pairs[-1]):
            tr_ref[rows, i * LANES : (i + 1) * LANES] = pair
        if rows is blocks[0]:
            send(0, gx > 0, here - ngy, pack0(pairs[0][0][:plane]))
    x_pair, y_pair, z_pair = [jnp.concatenate([block[i] for block in pairs], 0) for i in range(3)]

    def y_rows(y):
        return jnp.concatenate(
            [y_pair[x * plane + y * ez : x * plane + (y + 1) * ez] for x in range(ex)], 0
        )

    def z_rows(z):
        return jnp.concatenate([z_pair[i * ez + z : i * ez + z + 1] for i in range(ex * ey)], 0)

    send(1, gx < ngx - 1, here + ngy, pack7(x_pair[(ex - 1) * plane :]))
    send(2, gy < ngy - 1, here + 1, pack7(y_rows(ey - 1)))
    send(3, gy > 0, here - 1, pack0(y_rows(0)))
    rn_ref[...] = dot3_few(halves(rt_ref[...]), (nh_ref[...], nl_ref[...]))
    odd = lax.rem(gz, 2) == 1
    up, down = pack7(z_rows(ez - 1)), pack0(z_rows(0))
    z1_ref[...] = jnp.concatenate([jnp.where(odd, up, down), meta], 0)
    z2_ref[...] = jnp.concatenate([jnp.where(odd, down, up), meta], 0)
    for there, out in outs:
        pl.when(there)(out.wait)


def receive(sizes, dims, xy_ref, z1_ref, z2_ref):
    ngx, ngy, ngz = sizes
    gx, gy, gz = position(sizes)
    odd = lax.rem(gz, 2) == 1

    def one(got, there):
        n = got.shape[0] - META
        payload = jnp.where(there, got[:n], 0.0)
        labels = jnp.where(there, got[n : n + dims[0]], -1.0)
        weights = jnp.where(there, got[n + dims[0] : n + dims[0] + 1], 1.0)
        return payload, labels, weights

    return [
        one(xy_ref[jnp.minimum(gx + 1, ngx - 1) * ngy + gy], gx < ngx - 1),
        one(xy_ref[jnp.maximum(gx - 1, 0) * ngy + gy], gx > 0),
        one(xy_ref[gx * ngy + jnp.minimum(gy + 1, ngy - 1)], gy < ngy - 1),
        one(xy_ref[gx * ngy + jnp.maximum(gy - 1, 0)], gy > 0),
        one(jnp.where(odd, z1_ref[...], z2_ref[...]), gz < ngz - 1),
        one(jnp.where(odd, z2_ref[...], z1_ref[...]), gz > 0),
    ]


def faces(f_ref, dims, tr_ref, around):
    ex, ey, ez = dims
    lower = lane((ez, LANES)) < FACE
    inner = lax.broadcasted_iota(jnp.int32, (ez, LANES), 0)
    none = jnp.zeros((ez, LANES), F32)
    outer = None
    if around is not None:
        outer = [(unpack0 if i % 2 == 0 else unpack7)(a[0]) for i, a in enumerate(around)]

    def local(i, pair):
        if tr_ref is None:
            return none
        return tr_ref[i * ez : (i + 1) * ez, pair]

    def remote(side, strip):
        return none if outer is None else outer[side][strip]

    for x in range(ex):
        for y in range(ey):
            i = x * ey + y
            rows = slice(i * ez, (i + 1) * ez)
            pair = slice(0, LANES)
            strip = slice(y * ez, (y + 1) * ez)
            above = local(i + ey, pair) if x < ex - 1 else remote(0, strip)
            below = local(i - ey, pair) if x > 0 else remote(1, strip)
            f_ref[rows, pair] = jnp.where(lower, above, below)
            pair = slice(LANES, 2 * LANES)
            strip = slice(x * ez, (x + 1) * ez)
            above = local(i + 1, pair) if y < ey - 1 else remote(2, strip)
            below = local(i - 1, pair) if y > 0 else remote(3, strip)
            f_ref[rows, pair] = jnp.where(lower, above, below)
            pair = slice(2 * LANES, 3 * LANES)
            above = below = none
            if tr_ref is not None:
                column = tr_ref[rows, pair]
                above = jnp.where(inner == ez - 1, 0.0, pltpu.roll(column, ez - 1, 0))
                below = jnp.where(inner == 0, 0.0, pltpu.roll(column, 1, 0))
            if outer is not None:
                above = jnp.where(inner == ez - 1, outer[4][i : i + 1], above)
                below = jnp.where(inner == 0, outer[5][i : i + 1], below)
            f_ref[rows, pair] = jnp.where(lower, above, below)


def prepare_kernel(dims, l_hbm, m_hbm, uh_ref, ul_ref, th_ref, nh_ref, tr_ref, rt_ref, rn_ref,
                   p_ref, own_ref, qh_ref, ql_ref, d_out_ref, l_ref, d_ref, f_ref, sems):
    wait = fetch(("l", "m"), sems, l=(l_hbm, l_ref), m=(m_hbm, d_ref))
    faces(f_ref, dims, tr_ref, None)
    inside = halves(f_ref[...])
    near = nh_ref[...]
    pick = selection()
    wait("l")
    wait("m")
    diagonal = diagonal_rows(d_ref)
    d_out_ref[...] = diagonal
    d = as_row(diagonal)
    lift = halves(face_order(l_ref[...]))
    lrt = dot3_few(halves(rt_ref[...]), lift)
    zeros = jnp.zeros((COARSE, DOFS - FACE), F32)
    x0 = jnp.concatenate([lrt[:, :FACE], zeros], 1)
    x7 = jnp.concatenate([zeros, lrt[:, FACE:LANES]], 1)
    yz = lrt[:, LANES:]
    group = lane((COARSE, 4 * FACE)) // FACE
    spread = jnp.concatenate([jnp.where(group == f, yz, 0.0) for f in range(4)], 0)
    both = dot(jnp.concatenate(halves(spread), 0), pick, NT)
    yz = both[: 4 * COARSE] + both[4 * COARSE :]
    mrt = rt_ref[...] * d + rn_ref[...]
    q = jnp.concatenate([x0, x7, yz, mrt, jnp.zeros_like(mrt)], 0)
    rows = q.shape[0]
    both = dot(jnp.concatenate(halves(q), 0), near, NT)
    swept = q - (both[:rows] + both[rows:])
    split = halves(swept)
    of_t = dot(split[0], near, NT)
    of_f = halves(dot3_few(split, lift))
    qh_ref[...], ql_ref[...] = of_f
    of_u = halves(jnp.concatenate([q + swept * (1.0 - d), rt_ref[...] + rn_ref[...]], 0))
    by_t = dot(jnp.concatenate([of_t, rn_ref[...]], 0).astype(BF16), th_ref[...], NT)
    by_u = dot3_few(of_u, (uh_ref[...], ul_ref[...]))
    p_ref[...] = by_u[:rows] + by_t[:rows] + dot3_few(of_f, inside)
    own_ref[...] = by_u[rows:] + by_t[rows:]


def relax_kernel(sizes, dims, p_ref, own_ref, qh_ref, ql_ref, c_ref, meta_ref, xy_ref, z1_ref, z2_ref,
                 slots_hbm, f_ref, bins_ref, sem):
    ngx, ngy, ngz = sizes
    gx, gy, gz = position(sizes)
    ex, ey, ez = dims
    plane = ey * ez
    around = receive(sizes, dims, xy_ref, z1_ref, z2_ref)
    x_up, x_down, y_up, y_down, z_up, z_down = around
    q = qh_ref[...], ql_ref[...]
    rows = q[0].shape[0]
    keep = lane((rows, LANES)) < FACE

    def through(side, payload):
        pair = slice(side // 2 * LANES, (side // 2 + 1) * LANES)
        mine = keep if side % 2 == 0 else ~keep
        few = [jnp.where(mine, a[:, pair].astype(F32), 0.0).astype(BF16) for a in q]
        return dot3_few(few, halves(payload))

    added = []
    x_above, x_below = through(0, unpack0(x_up[0])), through(1, unpack7(x_down[0]))
    y_above, y_below = through(2, unpack0(y_up[0])), through(3, unpack7(y_down[0]))
    z_above, z_below = unpack0(z_up[0]), unpack7(z_down[0])
    inner = lax.broadcasted_iota(jnp.int32, (ez, LANES), 0)
    for i in range(ex * ey):
        f_ref[i * ez : (i + 1) * ez] = jnp.where(
            lane((ez, LANES)) < FACE,
            jnp.where(inner == ez - 1, z_above[i : i + 1], 0.0),
            jnp.where(inner == 0, z_below[i : i + 1], 0.0),
        )
    z_both = dot3_few([a[:, 2 * LANES :] for a in q], halves(f_ref[...]))
    at = lane((rows, LANES))
    for x in range(ex):
        tile = z_both[:, x * LANES : (x + 1) * LANES]
        up, down = (plane - ez - x * ez) % LANES, (LANES - x * ez) % LANES
        tile = tile + jnp.where(at >= plane - ez, pltpu.roll(y_above, up, 1) if up else y_above, 0.0)
        tile = tile + jnp.where(at < ez, pltpu.roll(y_below, down, 1) if down else y_below, 0.0)
        tile = tile + (x_above if x == ex - 1 else 0.0) + (x_below if x == 0 else 0.0)
        added.append(tile)
    p = p_ref[...] + jnp.concatenate(added, 1)
    own = own_ref[...]
    small = own - p[6 * COARSE : 7 * COARSE]
    p = p / as_row(meta_ref[META : META + ex])
    p_x0, p_x7, p_y0, p_y7, p_z0, p_z7 = [p[8 * f : 8 * f + 8] for f in range(6)]
    at = lane((COARSE, LANES))

    def tiles(a):
        return [a[:, x * LANES : (x + 1) * LANES] for x in range(ex)]

    none = jnp.zeros((COARSE, LANES), F32)
    total = []
    parts = [tiles(a) for a in (small, p_x0, p_x7, p_y0, p_y7, p_z0, p_z7)]
    for x in range(ex):
        s, _, _, y0, y7, z0, z7 = [a[x] for a in parts]
        s = s + (parts[1][x + 1] if x < ex - 1 else none)
        s = s + (parts[2][x - 1] if x > 0 else none)
        s = s + jnp.where(at < plane - ez, pltpu.roll(y0, LANES - ez, 1), 0.0)
        s = s + jnp.where(at >= ez, pltpu.roll(y7, ez, 1), 0.0)
        s = s + jnp.where(at % ez < ez - 1, pltpu.roll(z0, LANES - 1, 1), 0.0)
        s = s + jnp.where(at % ez > 0, pltpu.roll(z7, 1, 1), 0.0)
        total.append(s)
    total = jnp.concatenate(total, 1)

    def scatter(values, onehot):
        high, low = halves(values)
        out = dot(jnp.concatenate([high, low], 0), onehot, NT)
        return out[:COARSE] + out[COARSE:]

    def shifted(labels, shift, keep):
        return as_row(jnp.where(keep, pltpu.roll(labels, shift, 1), -1.0))

    rows = lane((ex, LANES))
    labels = meta_ref[0:ex]
    blocks = [
        (scatter(total, onehot_rows(as_row(labels))), meta_ref[ex : ex + 1]),
        (scatter(parts[2][ex - 1], onehot_rows(x_up[1][0:1])), x_up[2]),
        (scatter(parts[1][0], onehot_rows(x_down[1][ex - 1 : ex])), x_down[2]),
        (scatter(p_y7, onehot_rows(shifted(y_up[1], plane - ez, rows >= plane - ez))), y_up[2]),
        (scatter(p_y0, onehot_rows(shifted(y_down[1], ez, rows < ez))), y_down[2]),
        (scatter(p_z7, onehot_rows(shifted(z_up[1], ez - 1, rows % ez == ez - 1))), z_up[2]),
        (scatter(p_z0, onehot_rows(shifted(z_down[1], LANES - ez + 1, rows % ez == 0))), z_down[2]),
    ]
    raw = jnp.concatenate([z for z, _ in blocks], 1)
    mixed = raw + raw
    for k in range(COARSE):
        mixed = mixed - c_ref[:, k : k + 1] * raw[k : k + 1]

    def packed(block):
        rows = COARSE // 2
        return jnp.concatenate([block[:rows], block[rows:]], 1)

    b0, xu, xd, yu, yd, zu, zd = [packed(z / w[:, :FACE]) for z, w in blocks]
    a0, axu, axd, ayu, ayd, azu, azd = [
        packed(mixed[:, i * FACE : (i + 1) * FACE]) for i in range(len(blocks))
    ]

    count = slots_hbm.shape[0]
    bins_ref[...] = jnp.zeros_like(bins_ref)

    def put(dx, dy, dz, share):
        there = (dy >= 0) & (dy < ngy) & (dz >= 0) & (dz < ngz)
        bins_ref[jnp.where(there, (dx * ngy + dy) * ngz + dz, count)] = share

    line = b0 + xu + xd
    sides = yu + yd + zu + zd
    for dx in range(ngx):
        same = (gx == dx).astype(F32)
        up = (gx + 1 == dx).astype(F32)
        down = (gx - 1 == dx).astype(F32)
        column = same * b0 + up * xu + down * xd
        put(dx, gy, gz, line + same * (sides + a0) + up * axu + down * axd)
        put(dx, gy + 1, gz, yu + column + same * ayu)
        put(dx, gy - 1, gz, yd + column + same * ayd)
        put(dx, gy, gz + 1, zu + column + same * azu)
        put(dx, gy, gz - 1, zd + column + same * azd)
    put(gx, gy + 2, gz, yu)
    put(gx, gy - 2, gz, yd)
    put(gx, gy, gz + 2, zu)
    put(gx, gy, gz - 2, zd)
    put(gx, gy + 1, gz + 1, yu + zu)
    put(gx, gy + 1, gz - 1, yu + zd)
    put(gx, gy - 1, gz + 1, yd + zu)
    put(gx, gy - 1, gz - 1, yd + zd)
    copy = pltpu.make_async_copy(bins_ref.at[pl.ds(0, count)], slots_hbm, sem)
    copy.start()
    copy.wait()


def second_kernel(sizes, dims, rhs_hbm, s_hbm, l_hbm, uh_ref, ul_ref, tr_ref, d_ref, meta_ref, rt_ref, xy_ref, z1_ref, z2_ref,
                  second_ref, rs_ref, oh_ref, rhs_ref, s_ref, l_ref, f_ref, sems):
    wait = fetch(("l", "s", "rhs"), sems, rhs=(rhs_hbm, rhs_ref), s=(s_hbm, s_ref), l=(l_hbm, l_ref))
    ex = dims[0]
    faces(f_ref, dims, tr_ref, receive(sizes, dims, xy_ref, z1_ref, z2_ref))
    onehot = onehot_rows(as_row(meta_ref[:ex]))
    oh_ref[...] = jnp.concatenate([onehot, onehot], 0).astype(F32).T.astype(BF16)
    rt = halves(rt_ref[...])
    rs_ref[...] = jnp.concatenate([rt[0], rt[0], rt[1], jnp.zeros_like(rt[0])], 0)
    wait("l")
    r1 = dot3(halves(f_ref[...]), halves(face_order(l_ref[...])))
    wait("s")
    near = near_identity(s_ref, slice(0, DOFS))
    wait("rhs")
    u = uh_ref[...].astype(F32) + ul_ref[...].astype(F32)
    d = as_row(d_ref[...])
    r1 = r1 + dot3(halves(rhs_ref[...] - u), near) + u * (1.0 - d)
    v = u + (r1 - dot3(halves(r1), near))
    rc = reciprocal(meta_ref[META : META + ex])
    second_ref[...] = v * jnp.concatenate([rc] * (DOFS // LANES), 1)


def correct_kernel(second_ref, slots_ref, meta_ref, oh_ref, rs_ref, out_hbm, out_ref, sems):
    total = jnp.sum(slots_ref[...], 0)
    ztwo = jnp.concatenate([total[:, :FACE], total[:, FACE:]], 0) / meta_ref[4:5, :FACE]
    high, low = halves(ztwo)
    stacked = jnp.concatenate([high, low, high, jnp.zeros_like(high)], 0)
    prolonged = dot(stacked, rs_ref[...], TN)
    prolonged = jnp.concatenate(halves(prolonged), 0)
    chunk = DOFS // sems.shape[0]
    copies = []
    for i in range(sems.shape[0]):
        rows = slice(i * chunk, (i + 1) * chunk)
        out_ref[rows] = second_ref[rows] + dot(oh_ref[rows], prolonged)
        copy = pltpu.make_async_copy(out_ref.at[rows], out_hbm.at[rows], sems.at[i])
        copy.start()
        copies.append(copy)
    for copy in copies:
        copy.wait()


def shards(sizes, rhs, coef, mass, smoother, lift, restrict, coarse_block_matrix, element_cluster_index):
    ngx, ngy, ngz = sizes
    dims = coef.shape
    ex, ey, ez = dims
    flat = rhs.reshape(ex * ey * ez, DOFS)
    face = ey * ez * FACE // LANES
    tip = ex * ey * FACE // LANES
    params = pltpu.CompilerParams(vmem_limit_bytes=40 * 1024 * 1024)
    shape = jax.ShapeDtypeStruct
    hbm = pl.BlockSpec(memory_space=pltpu.HBM)
    vmem = pl.BlockSpec(memory_space=pltpu.VMEM)
    cost = pl.CostEstimate(flops=2 * 10**9, bytes_accessed=4 * 2**20, transcendentals=0)
    def far(*arrays):
        return [pltpu.with_memory_space_constraint(a, pltpu.HBM) for a in arrays]

    full = shape((DOFS, DOFS), F32)
    split = shape((DOFS, DOFS), BF16)
    count = ngx * ngy * ngz
    wide = shape((8 * COARSE, 3 * LANES), BF16)
    few = shape((COARSE, DOFS), F32)
    uh, ul, th, nh, tr, meta, xy, z1, z2, rt, c, rn = pl.pallas_call(
        functools.partial(smooth_kernel, sizes),
        out_shape=(
            split,
            split,
            split,
            split,
            shape((DOFS, 3 * LANES), F32),
            shape((2 * META, LANES), F32),
            shape((ngx * ngy, face + META, LANES), F32),
            shape((tip + META, LANES), F32),
            shape((tip + META, LANES), F32),
            few,
            shape((COARSE, COARSE), F32),
            few,
        ),
        in_specs=[hbm] * 6,
        out_specs=[vmem] * 6 + [hbm] + [vmem] * 5,
        scratch_shapes=[
            pltpu.VMEM((DOFS, DOFS), F32),
            pltpu.VMEM((DOFS, DOFS), F32),
            pltpu.VMEM(dims, F32),
            pltpu.VMEM(dims, jnp.int32),
            pltpu.VMEM((DOFS, DOFS), F32),
            pltpu.VMEM((DOFS, DOFS), BF16),
            pltpu.VMEM((4, face + META, LANES), F32),
            pltpu.SemaphoreType.DMA((12,)),
            pltpu.SemaphoreType.DMA((4,)),
        ],
        compiler_params=params,
        cost_estimate=cost,
        name="smooth",
    )(*far(flat, smoother, coef, element_cluster_index, restrict.T, coarse_block_matrix))
    def swaps(start):
        pairs = [(i, i + 1) for i in range(start, ngz - 1, 2)]
        return pairs + [(j, i) for i, j in pairs]

    z1 = lax.ppermute(z1, "gz", swaps(1))
    z2 = lax.ppermute(z2, "gz", swaps(0))
    xy = lax.all_to_all(xy, ("gx", "gy"), 0, 0, tiled=True)
    p, own, fh, fl, d = pl.pallas_call(
        functools.partial(prepare_kernel, dims),
        out_shape=(shape((8 * COARSE, DOFS), F32), few, wide, wide, shape((DOFS // LANES, LANES), F32)),
        in_specs=[hbm] * 2 + [vmem] * 7,
        scratch_shapes=[
            pltpu.VMEM((3 * LANES, DOFS), F32),
            pltpu.VMEM((DOFS // LANES, LANES, LANES), F32),
            pltpu.VMEM((DOFS, 3 * LANES), F32),
            pltpu.SemaphoreType.DMA((5,)),
        ],
        compiler_params=params,
        cost_estimate=cost,
        name="prepare",
    )(*far(lift, mass), uh, ul, th, nh, tr, rt, rn)
    slots = pl.pallas_call(
        functools.partial(relax_kernel, sizes, dims),
        out_shape=shape((count, COARSE // 2, LANES), F32),
        out_specs=hbm,
        scratch_shapes=[
            pltpu.VMEM((DOFS, LANES), F32),
            pltpu.VMEM((count + 1, COARSE // 2, LANES), F32),
            pltpu.SemaphoreType.DMA,
        ],
        compiler_params=params,
        cost_estimate=cost,
        name="relax",
    )(p, own, fh, fl, c, meta, xy, z1, z2)
    slots = lax.all_to_all(slots, ("gx", "gy", "gz"), 0, 0, tiled=True)
    second, rs, oh = pl.pallas_call(
        functools.partial(second_kernel, sizes, dims),
        out_shape=(
            full,
            shape((4 * COARSE, DOFS), BF16),
            shape((DOFS, LANES), BF16),
        ),
        in_specs=[hbm] * 3 + [vmem] * 9,
        scratch_shapes=[
            pltpu.VMEM((DOFS, DOFS), F32),
            pltpu.VMEM((DOFS, DOFS), F32),
            pltpu.VMEM((3 * LANES, DOFS), F32),
            pltpu.VMEM((DOFS, 3 * LANES), F32),
            pltpu.SemaphoreType.DMA((3,)),
        ],
        compiler_params=params,
        cost_estimate=cost,
        name="second",
    )(*far(flat, smoother, lift), uh, ul, tr, d, meta, rt, xy, z1, z2)
    out = pl.pallas_call(
        correct_kernel,
        out_shape=shape((DOFS, DOFS), F32),
        out_specs=hbm,
        scratch_shapes=[pltpu.VMEM((DOFS, DOFS), F32), pltpu.SemaphoreType.DMA((4,))],
        compiler_params=params,
        name="correct",
    )(second, slots, meta, oh, rs)
    return out.reshape(rhs.shape)


def solution(mesh):
    sizes = (mesh.shape["gx"], mesh.shape["gy"], mesh.shape["gz"])
    cells = P("gx", "gy", "gz")
    return jax.shard_map(
        functools.partial(shards, sizes),
        mesh=mesh,
        in_specs=(P("gx", "gy", "gz", None), cells, P(), P(), P(), P(), P(), cells),
        out_specs=P("gx", "gy", "gz", None),
        check_vma=False,
    )
```

```python
import functools

import jax
import jax.numpy as jnp
from jax import lax
from jax.experimental import pallas as pl
from jax.experimental.pallas import tpu as pltpu
from jax.sharding import PartitionSpec as P

EDGE = 8
DOFS = 512
FACE = 64
COARSE = 8
CLUSTERS = 64
LANES = 128
META = 8

F32 = jnp.float32
BF16 = jnp.bfloat16
NT = (((1,), (1,)), ((), ()))
TN = (((0,), (0,)), ((), ()))


def selection():
    column = lane((1, 4 * FACE))
    face, a, b = column // FACE, column % FACE // EDGE, column % EDGE
    node = jnp.where(face < 2, a * 64 + face * 56 + b, a * 64 + b * 8 + (face - 2) * 7)
    at = lax.broadcasted_iota(jnp.int32, (DOFS, 4 * FACE), 0)
    return jnp.where(at == node, 1.0, 0.0).astype(BF16)


def halves(x):
    high = x.astype(BF16)
    return high, (x - high.astype(F32)).astype(BF16)


def dot(a, b, dims=(((1,), (0,)), ((), ()))):
    return lax.dot_general(a, b, dims, preferred_element_type=F32)


def dot3(a, b, dims=(((1,), (0,)), ((), ()))):
    return dot(a[0], b[0], dims) + (dot(a[0], b[1], dims) + dot(a[1], b[0], dims))


def dot3_few(a, b):
    n = a[0].shape[0]
    both = dot(jnp.concatenate(a, 0), b[0], NT)
    return both[:n] + (both[n:] + dot(a[0], b[1], NT))


def lane(shape):
    return lax.broadcasted_iota(jnp.int32, shape, len(shape) - 1)


def swap(x):
    return pltpu.roll(x, FACE, 1)


def pack0(t):
    n = t.shape[0] // 2
    return jnp.where(lane((n, LANES)) < FACE, t[:n], swap(t[n:]))


def pack7(t):
    n = t.shape[0] // 2
    return jnp.where(lane((n, LANES)) < FACE, swap(t[:n]), t[n:])


def unpack0(p):
    return jnp.concatenate([p, swap(p)], 0)


def unpack7(p):
    return jnp.concatenate([swap(p), p], 0)


def cell_rows(ref):
    ex, ey, ez = ref.shape
    rows = []
    for x in range(ex):
        rows.append(jnp.concatenate([ref[x, y : y + 1, :] for y in range(ey)], 1))
    return jnp.concatenate(rows, 0).astype(F32)


def face_order(lift):
    return jnp.concatenate([lift[(f ^ 1) * FACE : ((f ^ 1) + 1) * FACE] for f in range(6)], 0)


def reciprocal(rows):
    n = rows.shape[0]
    columns = (1.0 / jnp.concatenate([rows, jnp.ones((LANES - n, LANES), F32)], 0)).T
    return jnp.concatenate([jnp.broadcast_to(columns[:, x : x + 1], (LANES, LANES)) for x in range(n)], 0)


def as_row(rows):
    return jnp.concatenate([rows[x : x + 1] for x in range(rows.shape[0])], 1)


def onehot_rows(row):
    n = row.shape[1]
    at = lax.broadcasted_iota(jnp.int32, (CLUSTERS, n), 0).astype(F32)
    return jnp.where(at == row, 1.0, 0.0).astype(BF16)


def position(sizes):
    return lax.axis_index("gx"), lax.axis_index("gy"), lax.axis_index("gz")


def near_identity(s_ref, part):
    diagonal = lax.broadcasted_iota(jnp.int32, (LANES, LANES), 0) == lane((LANES, LANES))
    identity = jnp.where(diagonal, 1.0, 0.0)
    rows = []
    for start in range(part.start, part.stop, LANES):
        s = s_ref[start : start + LANES]
        tile = identity - s[:, start : start + LANES]
        pieces = [-s[:, :start], tile, -s[:, start + LANES :]]
        rows.append(jnp.concatenate([piece for piece in pieces if piece.shape[1]], 1))
    return halves(jnp.concatenate(rows, 0))


def start_all(pairs, sems):
    copies = [pltpu.make_async_copy(src, dst, sems.at[i]) for i, (src, dst) in enumerate(pairs)]
    for copy in copies:
        copy.start()
    return copies


def fetch(names, sems, rhs=None, s=None, m=None, l=None):
    pairs = {"rhs": [rhs], "s": [s], "l": [l], "m": []}
    for i in range(DOFS // LANES if m else 0):
        block = slice(i * LANES, (i + 1) * LANES)
        pairs["m"].append((m[0].at[block, block], m[1].at[i]))
    counts = [len(pairs[name]) for name in names]
    first = [sum(counts[:i]) for i in range(len(names))]
    copies = start_all([pair for name in names for pair in pairs[name]], sems)

    def wait(name):
        i = names.index(name)
        for copy in copies[first[i] : first[i] + counts[i]]:
            copy.wait()

    return wait


def diagonal_rows(d_ref):
    here = lax.broadcasted_iota(jnp.int32, (LANES, LANES), 0) == lane((LANES, LANES))
    return jnp.concatenate(
        [jnp.sum(jnp.where(here, d_ref[i], 0.0), 0, keepdims=True) for i in range(d_ref.shape[0])], 0
    )


def traces(u, split, pick, scale):
    lower = lane((u.shape[0], LANES)) < FACE
    picked = dot(split[0], pick) + dot(split[1], pick)
    x_pair = jnp.where(lower, u[:, :LANES], u[:, DOFS - LANES :]) * scale
    return x_pair, picked[:, :LANES] * scale, picked[:, LANES:] * scale


def smooth_kernel(sizes, rhs_hbm, s_hbm, coef_hbm, lab_hbm, rt_hbm, c_hbm,
                  uh_ref, ul_ref, th_ref, nh_ref, tr_ref, meta_ref, xy_hbm, z1_ref, z2_ref, rt_ref, c_ref, rn_ref,
                  rhs_ref, s_ref, coef_ref, lab_ref, t_ref, nl_ref, out_ref, sems, out_sems):
    ngx, ngy, ngz = sizes
    gx, gy, gz = position(sizes)
    half = DOFS // 2
    blocks = [slice(0, half), slice(half, DOFS)]
    pairs = [(coef_hbm, coef_ref), (lab_hbm, lab_ref), (rt_hbm, rt_ref), (c_hbm, c_ref)]
    for part in blocks:
        quarters = [slice(part.start + i * half // 2, part.start + (i + 1) * half // 2) for i in range(2)]
        pairs += [(s_hbm.at[rows], s_ref.at[rows]) for rows in quarters]
        pairs += [(rhs_hbm.at[rows, part], rhs_ref.at[rows, part]) for rows in blocks]
    copies = start_all(pairs, sems)

    def wait(first, count):
        for copy in copies[first : first + count]:
            copy.wait()

    ex, ey, ez = lab_ref.shape
    plane = ey * ez
    pick = selection()
    wait(0, 4)
    lab = cell_rows(lab_ref)
    counts = dot(jnp.ones((8, DOFS), BF16), onehot_rows(as_row(lab)), NT)
    weights = 1.0 + jnp.concatenate([counts[0:1], counts[0:1]], 1)
    meta = jnp.concatenate([lab, weights, jnp.zeros((META - 5, LANES), F32)], 0)
    meta_ref[:META] = meta
    meta_ref[META : META + ex] = cell_rows(coef_ref)
    rc = reciprocal(meta_ref[META : META + ex])

    def near_part(part):
        near = near_identity(s_ref, part)
        nh_ref[part], nl_ref[part] = near
        return near

    here = gx * ngy + gy
    outs = []

    def send(i, there, slot, packed):
        n = packed.shape[0]
        out_ref[i, :n] = packed
        out_ref[i, n:] = meta
        out = pltpu.make_async_copy(out_ref.at[i], xy_hbm.at[jnp.where(there, slot, here)], out_sems.at[i])
        pl.when(there)(out.start)
        outs.append((there, out))

    wait(4, 2)
    near = near_part(blocks[0])
    wait(6, 2)
    t_ref[...] = dot3(halves(rhs_ref[:, blocks[0]]), near)
    wait(8, 2)
    near = near_part(blocks[1])
    wait(10, 2)
    pairs = []
    for rows in blocks:
        t = t_ref[rows] + dot3(halves(rhs_ref[rows, blocks[1]]), near)
        th_ref[rows] = t.astype(BF16)
        u = rhs_ref[rows] - t
        split = halves(u)
        uh_ref[rows], ul_ref[rows] = split
        pairs.append(traces(u, split, pick, rc[rows]))
        for i, pair in enumerate(pairs[-1]):
            tr_ref[rows, i * LANES : (i + 1) * LANES] = pair
        if rows is blocks[0]:
            send(0, gx > 0, here - ngy, pack0(pairs[0][0][:plane]))
    x_pair, y_pair, z_pair = [jnp.concatenate([block[i] for block in pairs], 0) for i in range(3)]

    def y_rows(y):
        return jnp.concatenate(
            [y_pair[x * plane + y * ez : x * plane + (y + 1) * ez] for x in range(ex)], 0
        )

    def z_rows(z):
        return jnp.concatenate([z_pair[i * ez + z : i * ez + z + 1] for i in range(ex * ey)], 0)

    send(1, gx < ngx - 1, here + ngy, pack7(x_pair[(ex - 1) * plane :]))
    send(2, gy < ngy - 1, here + 1, pack7(y_rows(ey - 1)))
    send(3, gy > 0, here - 1, pack0(y_rows(0)))
    rn_ref[...] = dot3_few(halves(rt_ref[...]), (nh_ref[...], nl_ref[...]))
    odd = lax.rem(gz, 2) == 1
    up, down = pack7(z_rows(ez - 1)), pack0(z_rows(0))
    z1_ref[...] = jnp.concatenate([jnp.where(odd, up, down), meta], 0)
    z2_ref[...] = jnp.concatenate([jnp.where(odd, down, up), meta], 0)
    for there, out in outs:
        pl.when(there)(out.wait)


def receive(sizes, dims, xy_ref, z1_ref, z2_ref):
    ngx, ngy, ngz = sizes
    gx, gy, gz = position(sizes)
    odd = lax.rem(gz, 2) == 1

    def one(got, there):
        n = got.shape[0] - META
        payload = jnp.where(there, got[:n], 0.0)
        labels = jnp.where(there, got[n : n + dims[0]], -1.0)
        weights = jnp.where(there, got[n + dims[0] : n + dims[0] + 1], 1.0)
        return payload, labels, weights

    return [
        one(xy_ref[jnp.minimum(gx + 1, ngx - 1) * ngy + gy], gx < ngx - 1),
        one(xy_ref[jnp.maximum(gx - 1, 0) * ngy + gy], gx > 0),
        one(xy_ref[gx * ngy + jnp.minimum(gy + 1, ngy - 1)], gy < ngy - 1),
        one(xy_ref[gx * ngy + jnp.maximum(gy - 1, 0)], gy > 0),
        one(jnp.where(odd, z1_ref[...], z2_ref[...]), gz < ngz - 1),
        one(jnp.where(odd, z2_ref[...], z1_ref[...]), gz > 0),
    ]


def faces(f_ref, dims, tr_ref, around):
    ex, ey, ez = dims
    lower = lane((ez, LANES)) < FACE
    inner = lax.broadcasted_iota(jnp.int32, (ez, LANES), 0)
    none = jnp.zeros((ez, LANES), F32)
    outer = None
    if around is not None:
        outer = [(unpack0 if i % 2 == 0 else unpack7)(a[0]) for i, a in enumerate(around)]

    def local(i, pair):
        if tr_ref is None:
            return none
        return tr_ref[i * ez : (i + 1) * ez, pair]

    def remote(side, strip):
        return none if outer is None else outer[side][strip]

    for x in range(ex):
        for y in range(ey):
            i = x * ey + y
            rows = slice(i * ez, (i + 1) * ez)
            pair = slice(0, LANES)
            strip = slice(y * ez, (y + 1) * ez)
            above = local(i + ey, pair) if x < ex - 1 else remote(0, strip)
            below = local(i - ey, pair) if x > 0 else remote(1, strip)
            f_ref[rows, pair] = jnp.where(lower, above, below)
            pair = slice(LANES, 2 * LANES)
            strip = slice(x * ez, (x + 1) * ez)
            above = local(i + 1, pair) if y < ey - 1 else remote(2, strip)
            below = local(i - 1, pair) if y > 0 else remote(3, strip)
            f_ref[rows, pair] = jnp.where(lower, above, below)
            pair = slice(2 * LANES, 3 * LANES)
            above = below = none
            if tr_ref is not None:
                column = tr_ref[rows, pair]
                above = jnp.where(inner == ez - 1, 0.0, pltpu.roll(column, ez - 1, 0))
                below = jnp.where(inner == 0, 0.0, pltpu.roll(column, 1, 0))
            if outer is not None:
                above = jnp.where(inner == ez - 1, outer[4][i : i + 1], above)
                below = jnp.where(inner == 0, outer[5][i : i + 1], below)
            f_ref[rows, pair] = jnp.where(lower, above, below)


def prepare_kernel(dims, l_hbm, m_hbm, uh_ref, ul_ref, th_ref, nh_ref, tr_ref, rt_ref, rn_ref,
                   p_ref, own_ref, qh_ref, ql_ref, d_out_ref, l_ref, d_ref, f_ref, sems):
    wait = fetch(("l", "m"), sems, l=(l_hbm, l_ref), m=(m_hbm, d_ref))
    faces(f_ref, dims, tr_ref, None)
    inside = halves(f_ref[...])
    near = nh_ref[...]
    pick = selection()
    wait("l")
    wait("m")
    diagonal = diagonal_rows(d_ref)
    d_out_ref[...] = diagonal
    d = as_row(diagonal)
    lift = halves(face_order(l_ref[...]))
    lrt = dot3_few(halves(rt_ref[...]), lift)
    zeros = jnp.zeros((COARSE, DOFS - FACE), F32)
    x0 = jnp.concatenate([lrt[:, :FACE], zeros], 1)
    x7 = jnp.concatenate([zeros, lrt[:, FACE:LANES]], 1)
    yz = lrt[:, LANES:]
    group = lane((COARSE, 4 * FACE)) // FACE
    spread = jnp.concatenate([jnp.where(group == f, yz, 0.0) for f in range(4)], 0)
    both = dot(jnp.concatenate(halves(spread), 0), pick, NT)
    yz = both[: 4 * COARSE] + both[4 * COARSE :]
    mrt = rt_ref[...] * d + rn_ref[...]
    q = jnp.concatenate([x0, x7, yz, mrt, jnp.zeros_like(mrt)], 0)
    rows = q.shape[0]
    both = dot(jnp.concatenate(halves(q), 0), near, NT)
    swept = q - (both[:rows] + both[rows:])
    split = halves(swept)
    of_t = dot(split[0], near, NT)
    of_f = halves(dot3_few(split, lift))
    qh_ref[...], ql_ref[...] = of_f
    of_u = halves(jnp.concatenate([q + swept * (1.0 - d), rt_ref[...] + rn_ref[...]], 0))
    by_t = dot(jnp.concatenate([of_t, rn_ref[...]], 0).astype(BF16), th_ref[...], NT)
    by_u = dot3_few(of_u, (uh_ref[...], ul_ref[...]))
    p_ref[...] = by_u[:rows] + by_t[:rows] + dot3_few(of_f, inside)
    own_ref[...] = by_u[rows:] + by_t[rows:]


def relax_kernel(sizes, dims, p_ref, own_ref, qh_ref, ql_ref, c_ref, meta_ref, xy_ref, z1_ref, z2_ref,
                 slots_hbm, f_ref, bins_ref, sem):
    ngx, ngy, ngz = sizes
    gx, gy, gz = position(sizes)
    ex, ey, ez = dims
    plane = ey * ez
    around = receive(sizes, dims, xy_ref, z1_ref, z2_ref)
    x_up, x_down, y_up, y_down, z_up, z_down = around
    q = qh_ref[...], ql_ref[...]
    rows = q[0].shape[0]
    keep = lane((rows, LANES)) < FACE

    def through(side, payload):
        pair = slice(side // 2 * LANES, (side // 2 + 1) * LANES)
        mine = keep if side % 2 == 0 else ~keep
        few = [jnp.where(mine, a[:, pair].astype(F32), 0.0).astype(BF16) for a in q]
        return dot3_few(few, halves(payload))

    added = []
    x_above, x_below = through(0, unpack0(x_up[0])), through(1, unpack7(x_down[0]))
    y_above, y_below = through(2, unpack0(y_up[0])), through(3, unpack7(y_down[0]))
    z_above, z_below = unpack0(z_up[0]), unpack7(z_down[0])
    inner = lax.broadcasted_iota(jnp.int32, (ez, LANES), 0)
    for i in range(ex * ey):
        f_ref[i * ez : (i + 1) * ez] = jnp.where(
            lane((ez, LANES)) < FACE,
            jnp.where(inner == ez - 1, z_above[i : i + 1], 0.0),
            jnp.where(inner == 0, z_below[i : i + 1], 0.0),
        )
    z_both = dot3_few([a[:, 2 * LANES :] for a in q], halves(f_ref[...]))
    at = lane((rows, LANES))
    for x in range(ex):
        tile = z_both[:, x * LANES : (x + 1) * LANES]
        up, down = (plane - ez - x * ez) % LANES, (LANES - x * ez) % LANES
        tile = tile + jnp.where(at >= plane - ez, pltpu.roll(y_above, up, 1) if up else y_above, 0.0)
        tile = tile + jnp.where(at < ez, pltpu.roll(y_below, down, 1) if down else y_below, 0.0)
        tile = tile + (x_above if x == ex - 1 else 0.0) + (x_below if x == 0 else 0.0)
        added.append(tile)
    p = p_ref[...] + jnp.concatenate(added, 1)
    own = own_ref[...]
    small = own - p[6 * COARSE : 7 * COARSE]
    p = p / as_row(meta_ref[META : META + ex])
    p_x0, p_x7, p_y0, p_y7, p_z0, p_z7 = [p[8 * f : 8 * f + 8] for f in range(6)]
    at = lane((COARSE, LANES))

    def tiles(a):
        return [a[:, x * LANES : (x + 1) * LANES] for x in range(ex)]

    none = jnp.zeros((COARSE, LANES), F32)
    total = []
    parts = [tiles(a) for a in (small, p_x0, p_x7, p_y0, p_y7, p_z0, p_z7)]
    for x in range(ex):
        s, _, _, y0, y7, z0, z7 = [a[x] for a in parts]
        s = s + (parts[1][x + 1] if x < ex - 1 else none)
        s = s + (parts[2][x - 1] if x > 0 else none)
        s = s + jnp.where(at < plane - ez, pltpu.roll(y0, LANES - ez, 1), 0.0)
        s = s + jnp.where(at >= ez, pltpu.roll(y7, ez, 1), 0.0)
        s = s + jnp.where(at % ez < ez - 1, pltpu.roll(z0, LANES - 1, 1), 0.0)
        s = s + jnp.where(at % ez > 0, pltpu.roll(z7, 1, 1), 0.0)
        total.append(s)
    total = jnp.concatenate(total, 1)

    def scatter(values, onehot):
        high, low = halves(values)
        out = dot(jnp.concatenate([high, low], 0), jnp.concatenate([onehot, onehot], 0), NT)
        return out[:COARSE] + out[COARSE:]

    def shifted(labels, shift, keep):
        return as_row(jnp.where(keep, pltpu.roll(labels, shift, 1), -1.0))

    rows = lane((ex, LANES))
    labels = meta_ref[0:ex]
    blocks = [
        (scatter(total, onehot_rows(as_row(labels))), meta_ref[ex : ex + 1]),
        (scatter(parts[2][ex - 1], onehot_rows(x_up[1][0:1])), x_up[2]),
        (scatter(parts[1][0], onehot_rows(x_down[1][ex - 1 : ex])), x_down[2]),
        (scatter(p_y7, onehot_rows(shifted(y_up[1], plane - ez, rows >= plane - ez))), y_up[2]),
        (scatter(p_y0, onehot_rows(shifted(y_down[1], ez, rows < ez))), y_down[2]),
        (scatter(p_z7, onehot_rows(shifted(z_up[1], ez - 1, rows % ez == ez - 1))), z_up[2]),
        (scatter(p_z0, onehot_rows(shifted(z_down[1], LANES - ez + 1, rows % ez == 0))), z_down[2]),
    ]
    columns = [jnp.broadcast_to(c_ref[:, k : k + 1], (COARSE, LANES)) for k in range(COARSE)]

    def mixed(block):
        out = block + block
        for k in range(COARSE):
            out = out - columns[k] * block[k : k + 1]
        return out

    def packed(block):
        half = COARSE // 2
        return jnp.where(lane((half, LANES)) < FACE, block[:half], block[half:])

    b0, xu, xd, yu, yd, zu, zd = [packed(z / w) for z, w in blocks]
    a0, axu, axd, ayu, ayd, azu, azd = [packed(mixed(z)) for z, _ in blocks]

    count = slots_hbm.shape[0]
    bins_ref[...] = jnp.zeros_like(bins_ref)

    def put(dx, dy, dz, share):
        there = (dy >= 0) & (dy < ngy) & (dz >= 0) & (dz < ngz)
        bins_ref[jnp.where(there, (dx * ngy + dy) * ngz + dz, count)] = share

    line = b0 + xu + xd
    sides = yu + yd + zu + zd
    for dx in range(ngx):
        same = (gx == dx).astype(F32)
        up = (gx + 1 == dx).astype(F32)
        down = (gx - 1 == dx).astype(F32)
        column = same * b0 + up * xu + down * xd
        put(dx, gy, gz, line + same * (sides + a0) + up * axu + down * axd)
        put(dx, gy + 1, gz, yu + column + same * ayu)
        put(dx, gy - 1, gz, yd + column + same * ayd)
        put(dx, gy, gz + 1, zu + column + same * azu)
        put(dx, gy, gz - 1, zd + column + same * azd)
    put(gx, gy + 2, gz, yu)
    put(gx, gy - 2, gz, yd)
    put(gx, gy, gz + 2, zu)
    put(gx, gy, gz - 2, zd)
    put(gx, gy + 1, gz + 1, yu + zu)
    put(gx, gy + 1, gz - 1, yu + zd)
    put(gx, gy - 1, gz + 1, yd + zu)
    put(gx, gy - 1, gz - 1, yd + zd)
    copy = pltpu.make_async_copy(bins_ref.at[pl.ds(0, count)], slots_hbm, sem)
    copy.start()
    copy.wait()


def second_kernel(sizes, dims, rhs_hbm, s_hbm, l_hbm, uh_ref, ul_ref, tr_ref, d_ref, meta_ref, rt_ref, xy_ref, z1_ref, z2_ref,
                  second_ref, rs_ref, oh_ref, rhs_ref, s_ref, l_ref, f_ref, sems):
    wait = fetch(("l", "s", "rhs"), sems, rhs=(rhs_hbm, rhs_ref), s=(s_hbm, s_ref), l=(l_hbm, l_ref))
    ex = dims[0]
    faces(f_ref, dims, tr_ref, receive(sizes, dims, xy_ref, z1_ref, z2_ref))
    onehot = onehot_rows(as_row(meta_ref[:ex]))
    oh_ref[...] = jnp.concatenate([onehot, onehot], 0).astype(F32).T.astype(BF16)
    rt = halves(rt_ref[...])
    rs_ref[...] = jnp.concatenate([rt[0], rt[0], rt[1], jnp.zeros_like(rt[0])], 0)
    wait("l")
    r1 = dot3(halves(f_ref[...]), halves(face_order(l_ref[...])))
    wait("s")
    near = near_identity(s_ref, slice(0, DOFS))
    wait("rhs")
    u = uh_ref[...].astype(F32) + ul_ref[...].astype(F32)
    d = as_row(d_ref[...])
    r1 = r1 + dot3(halves(rhs_ref[...] - u), near) + u * (1.0 - d)
    v = u + (r1 - dot3(halves(r1), near))
    rc = reciprocal(meta_ref[META : META + ex])
    second_ref[...] = v * jnp.concatenate([rc] * (DOFS // LANES), 1)


def correct_kernel(second_ref, slots_ref, meta_ref, oh_ref, rs_ref, out_hbm, out_ref, sems):
    total = jnp.sum(slots_ref[...], 0)
    ztwo = jnp.concatenate([total[:, :FACE], total[:, FACE:]], 0) / meta_ref[4:5, :FACE]
    high, low = halves(ztwo)
    stacked = jnp.concatenate([high, low, high, jnp.zeros_like(high)], 0)
    prolonged = dot(stacked, rs_ref[...], TN)
    prolonged = jnp.concatenate(halves(prolonged), 0)
    chunk = DOFS // sems.shape[0]
    copies = []
    for i in range(sems.shape[0]):
        rows = slice(i * chunk, (i + 1) * chunk)
        out_ref[rows] = second_ref[rows] + dot(oh_ref[rows], prolonged)
        copy = pltpu.make_async_copy(out_ref.at[rows], out_hbm.at[rows], sems.at[i])
        copy.start()
        copies.append(copy)
    for copy in copies:
        copy.wait()


def shards(sizes, rhs, coef, mass, smoother, lift, restrict, coarse_block_matrix, element_cluster_index):
    ngx, ngy, ngz = sizes
    dims = coef.shape
    ex, ey, ez = dims
    flat = rhs.reshape(ex * ey * ez, DOFS)
    face = ey * ez * FACE // LANES
    tip = ex * ey * FACE // LANES
    params = pltpu.CompilerParams(vmem_limit_bytes=40 * 1024 * 1024)
    shape = jax.ShapeDtypeStruct
    hbm = pl.BlockSpec(memory_space=pltpu.HBM)
    vmem = pl.BlockSpec(memory_space=pltpu.VMEM)
    cost = pl.CostEstimate(flops=2 * 10**9, bytes_accessed=4 * 2**20, transcendentals=0)
    def far(*arrays):
        return [pltpu.with_memory_space_constraint(a, pltpu.HBM) for a in arrays]

    full = shape((DOFS, DOFS), F32)
    split = shape((DOFS, DOFS), BF16)
    count = ngx * ngy * ngz
    wide = shape((8 * COARSE, 3 * LANES), BF16)
    few = shape((COARSE, DOFS), F32)
    uh, ul, th, nh, tr, meta, xy, z1, z2, rt, c, rn = pl.pallas_call(
        functools.partial(smooth_kernel, sizes),
        out_shape=(
            split,
            split,
            split,
            split,
            shape((DOFS, 3 * LANES), F32),
            shape((2 * META, LANES), F32),
            shape((ngx * ngy, face + META, LANES), F32),
            shape((tip + META, LANES), F32),
            shape((tip + META, LANES), F32),
            few,
            shape((COARSE, COARSE), F32),
            few,
        ),
        in_specs=[hbm] * 6,
        out_specs=[vmem] * 6 + [hbm] + [vmem] * 5,
        scratch_shapes=[
            pltpu.VMEM((DOFS, DOFS), F32),
            pltpu.VMEM((DOFS, DOFS), F32),
            pltpu.VMEM(dims, F32),
            pltpu.VMEM(dims, jnp.int32),
            pltpu.VMEM((DOFS, DOFS), F32),
            pltpu.VMEM((DOFS, DOFS), BF16),
            pltpu.VMEM((4, face + META, LANES), F32),
            pltpu.SemaphoreType.DMA((12,)),
            pltpu.SemaphoreType.DMA((4,)),
        ],
        compiler_params=params,
        cost_estimate=cost,
        name="smooth",
    )(*far(flat, smoother, coef, element_cluster_index, restrict.T, coarse_block_matrix))
    def swaps(start):
        pairs = [(i, i + 1) for i in range(start, ngz - 1, 2)]
        return pairs + [(j, i) for i, j in pairs]

    z1 = lax.ppermute(z1, "gz", swaps(1))
    z2 = lax.ppermute(z2, "gz", swaps(0))
    xy = lax.all_to_all(xy, ("gx", "gy"), 0, 0, tiled=True)
    p, own, fh, fl, d = pl.pallas_call(
        functools.partial(prepare_kernel, dims),
        out_shape=(shape((8 * COARSE, DOFS), F32), few, wide, wide, shape((DOFS // LANES, LANES), F32)),
        in_specs=[hbm] * 2 + [vmem] * 7,
        scratch_shapes=[
            pltpu.VMEM((3 * LANES, DOFS), F32),
            pltpu.VMEM((DOFS // LANES, LANES, LANES), F32),
            pltpu.VMEM((DOFS, 3 * LANES), F32),
            pltpu.SemaphoreType.DMA((5,)),
        ],
        compiler_params=params,
        cost_estimate=cost,
        name="prepare",
    )(*far(lift, mass), uh, ul, th, nh, tr, rt, rn)
    slots = pl.pallas_call(
        functools.partial(relax_kernel, sizes, dims),
        out_shape=shape((count, COARSE // 2, LANES), F32),
        out_specs=hbm,
        scratch_shapes=[
            pltpu.VMEM((DOFS, LANES), F32),
            pltpu.VMEM((count + 1, COARSE // 2, LANES), F32),
            pltpu.SemaphoreType.DMA,
        ],
        compiler_params=params,
        cost_estimate=cost,
        name="relax",
    )(p, own, fh, fl, c, meta, xy, z1, z2)
    slots = lax.all_to_all(slots, ("gx", "gy", "gz"), 0, 0, tiled=True)
    second, rs, oh = pl.pallas_call(
        functools.partial(second_kernel, sizes, dims),
        out_shape=(
            full,
            shape((4 * COARSE, DOFS), BF16),
            shape((DOFS, LANES), BF16),
        ),
        in_specs=[hbm] * 3 + [vmem] * 9,
        scratch_shapes=[
            pltpu.VMEM((DOFS, DOFS), F32),
            pltpu.VMEM((DOFS, DOFS), F32),
            pltpu.VMEM((3 * LANES, DOFS), F32),
            pltpu.VMEM((DOFS, 3 * LANES), F32),
            pltpu.SemaphoreType.DMA((3,)),
        ],
        compiler_params=params,
        cost_estimate=cost,
        name="second",
    )(*far(flat, smoother, lift), uh, ul, tr, d, meta, rt, xy, z1, z2)
    out = pl.pallas_call(
        correct_kernel,
        out_shape=shape((DOFS, DOFS), F32),
        out_specs=hbm,
        scratch_shapes=[pltpu.VMEM((DOFS, DOFS), F32), pltpu.SemaphoreType.DMA((4,))],
        compiler_params=params,
        name="correct",
    )(second, slots, meta, oh, rs)
    return out.reshape(rhs.shape)


def solution(mesh):
    sizes = (mesh.shape["gx"], mesh.shape["gy"], mesh.shape["gz"])
    cells = P("gx", "gy", "gz")
    return jax.shard_map(
        functools.partial(shards, sizes),
        mesh=mesh,
        in_specs=(P("gx", "gy", "gz", None), cells, P(), P(), P(), P(), P(), cells),
        out_specs=P("gx", "gy", "gz", None),
        check_vma=False,
    )
```

```python
import functools

import jax
import jax.numpy as jnp
from jax import lax
from jax.experimental import pallas as pl
from jax.experimental.pallas import tpu as pltpu
from jax.sharding import PartitionSpec as P

EDGE = 8
DOFS = 512
FACE = 64
COARSE = 8
CLUSTERS = 64
LANES = 128
META = 8

F32 = jnp.float32
BF16 = jnp.bfloat16
NT = (((1,), (1,)), ((), ()))
TN = (((0,), (0,)), ((), ()))


def selection():
    column = lane((1, 4 * FACE))
    face, a, b = column // FACE, column % FACE // EDGE, column % EDGE
    node = jnp.where(face < 2, a * 64 + face * 56 + b, a * 64 + b * 8 + (face - 2) * 7)
    at = lax.broadcasted_iota(jnp.int32, (DOFS, 4 * FACE), 0)
    return jnp.where(at == node, 1.0, 0.0).astype(BF16)


def halves(x):
    high = x.astype(BF16)
    return high, (x - high.astype(F32)).astype(BF16)


def dot(a, b, dims=(((1,), (0,)), ((), ()))):
    return lax.dot_general(a, b, dims, preferred_element_type=F32)


def dot3(a, b, dims=(((1,), (0,)), ((), ()))):
    return dot(a[0], b[0], dims) + (dot(a[0], b[1], dims) + dot(a[1], b[0], dims))


def dot3_few(a, b):
    n = a[0].shape[0]
    both = dot(jnp.concatenate(a, 0), b[0], NT)
    return both[:n] + (both[n:] + dot(a[0], b[1], NT))


def lane(shape):
    return lax.broadcasted_iota(jnp.int32, shape, len(shape) - 1)


def swap(x):
    return pltpu.roll(x, FACE, 1)


def pack0(t):
    n = t.shape[0] // 2
    return jnp.where(lane((n, LANES)) < FACE, t[:n], swap(t[n:]))


def pack7(t):
    n = t.shape[0] // 2
    return jnp.where(lane((n, LANES)) < FACE, swap(t[:n]), t[n:])


def unpack0(p):
    return jnp.concatenate([p, swap(p)], 0)


def unpack7(p):
    return jnp.concatenate([swap(p), p], 0)


def cell_rows(ref):
    ex, ey, ez = ref.shape
    rows = []
    for x in range(ex):
        rows.append(jnp.concatenate([ref[x, y : y + 1, :] for y in range(ey)], 1))
    return jnp.concatenate(rows, 0).astype(F32)


def face_order(lift):
    return jnp.concatenate([lift[(f ^ 1) * FACE : ((f ^ 1) + 1) * FACE] for f in range(6)], 0)


def reciprocal(rows):
    n = rows.shape[0]
    columns = (1.0 / jnp.concatenate([rows, jnp.ones((LANES - n, LANES), F32)], 0)).T
    return jnp.concatenate([jnp.broadcast_to(columns[:, x : x + 1], (LANES, LANES)) for x in range(n)], 0)


def as_row(rows):
    return jnp.concatenate([rows[x : x + 1] for x in range(rows.shape[0])], 1)


def onehot_rows(row):
    n = row.shape[1]
    at = lax.broadcasted_iota(jnp.int32, (CLUSTERS, n), 0).astype(F32)
    return jnp.where(at == row, 1.0, 0.0).astype(BF16)


def position(sizes):
    return lax.axis_index("gx"), lax.axis_index("gy"), lax.axis_index("gz")


def near_identity(s_ref, part):
    diagonal = lax.broadcasted_iota(jnp.int32, (LANES, LANES), 0) == lane((LANES, LANES))
    identity = jnp.where(diagonal, 1.0, 0.0)
    rows = []
    for start in range(part.start, part.stop, LANES):
        s = s_ref[start : start + LANES]
        tile = identity - s[:, start : start + LANES]
        pieces = [-s[:, :start], tile, -s[:, start + LANES :]]
        rows.append(jnp.concatenate([piece for piece in pieces if piece.shape[1]], 1))
    return halves(jnp.concatenate(rows, 0))


def start_all(pairs, sems):
    copies = [pltpu.make_async_copy(src, dst, sems.at[i]) for i, (src, dst) in enumerate(pairs)]
    for copy in copies:
        copy.start()
    return copies


def fetch(names, sems, rhs=None, s=None, m=None, l=None):
    pairs = {"rhs": [rhs], "s": [s], "l": [l], "m": []}
    for i in range(DOFS // LANES if m else 0):
        block = slice(i * LANES, (i + 1) * LANES)
        pairs["m"].append((m[0].at[block, block], m[1].at[i]))
    counts = [len(pairs[name]) for name in names]
    first = [sum(counts[:i]) for i in range(len(names))]
    copies = start_all([pair for name in names for pair in pairs[name]], sems)

    def wait(name):
        i = names.index(name)
        for copy in copies[first[i] : first[i] + counts[i]]:
            copy.wait()

    return wait


def diagonal_rows(d_ref):
    here = lax.broadcasted_iota(jnp.int32, (LANES, LANES), 0) == lane((LANES, LANES))
    return jnp.concatenate(
        [jnp.sum(jnp.where(here, d_ref[i], 0.0), 0, keepdims=True) for i in range(d_ref.shape[0])], 0
    )


def traces(u, split, pick, scale):
    lower = lane((u.shape[0], LANES)) < FACE
    picked = dot(split[0], pick) + dot(split[1], pick)
    x_pair = jnp.where(lower, u[:, :LANES], u[:, DOFS - LANES :]) * scale
    return x_pair, picked[:, :LANES] * scale, picked[:, LANES:] * scale


def smooth_kernel(sizes, rhs_hbm, s_hbm, coef_hbm, lab_hbm, rt_hbm, c_hbm,
                  uh_ref, ul_ref, th_ref, nh_ref, tr_ref, meta_ref, xy_hbm, z1_ref, z2_ref, rt_ref, c_ref, rn_ref,
                  rhs_ref, s_ref, coef_ref, lab_ref, t_ref, nl_ref, out_ref, sems, out_sems):
    ngx, ngy, ngz = sizes
    gx, gy, gz = position(sizes)
    half = DOFS // 2
    blocks = [slice(0, half), slice(half, DOFS)]
    pairs = [(coef_hbm, coef_ref), (lab_hbm, lab_ref), (rt_hbm, rt_ref), (c_hbm, c_ref)]
    for part in blocks:
        quarters = [slice(part.start + i * half // 2, part.start + (i + 1) * half // 2) for i in range(2)]
        pairs += [(s_hbm.at[rows], s_ref.at[rows]) for rows in quarters]
        pairs += [(rhs_hbm.at[rows, part], rhs_ref.at[rows, part]) for rows in blocks]
    copies = start_all(pairs, sems)

    def wait(first, count):
        for copy in copies[first : first + count]:
            copy.wait()

    ex, ey, ez = lab_ref.shape
    plane = ey * ez
    pick = selection()
    wait(0, 4)
    lab = cell_rows(lab_ref)
    counts = dot(jnp.ones((8, DOFS), BF16), onehot_rows(as_row(lab)), NT)
    weights = 1.0 + jnp.concatenate([counts[0:1], counts[0:1]], 1)
    meta = jnp.concatenate([lab, weights, jnp.zeros((META - 5, LANES), F32)], 0)
    meta_ref[:META] = meta
    meta_ref[META : META + ex] = cell_rows(coef_ref)
    rc = reciprocal(meta_ref[META : META + ex])

    def near_part(part):
        near = near_identity(s_ref, part)
        nh_ref[part], nl_ref[part] = near
        return near

    here = gx * ngy + gy
    outs = []

    def send(i, there, slot, packed):
        n = packed.shape[0]
        out_ref[i, :n] = packed
        out_ref[i, n:] = meta
        out = pltpu.make_async_copy(out_ref.at[i], xy_hbm.at[jnp.where(there, slot, here)], out_sems.at[i])
        pl.when(there)(out.start)
        outs.append((there, out))

    wait(4, 2)
    near = near_part(blocks[0])
    for i, rows in enumerate(blocks):
        wait(6 + i, 1)
        t_ref[rows] = dot3(halves(rhs_ref[rows, blocks[0]]), near)
    wait(8, 2)
    near = near_part(blocks[1])
    pairs = []
    for i, rows in enumerate(blocks):
        wait(10 + i, 1)
        t = t_ref[rows] + dot3(halves(rhs_ref[rows, blocks[1]]), near)
        th_ref[rows] = t.astype(BF16)
        u = rhs_ref[rows] - t
        split = halves(u)
        uh_ref[rows], ul_ref[rows] = split
        pairs.append(traces(u, split, pick, rc[rows]))
        for j, pair in enumerate(pairs[-1]):
            tr_ref[rows, j * LANES : (j + 1) * LANES] = pair
        if rows is blocks[0]:
            send(0, gx > 0, here - ngy, pack0(pairs[0][0][:plane]))
    x_pair, y_pair, z_pair = [jnp.concatenate([block[i] for block in pairs], 0) for i in range(3)]

    def y_rows(y):
        return jnp.concatenate(
            [y_pair[x * plane + y * ez : x * plane + (y + 1) * ez] for x in range(ex)], 0
        )

    def z_rows(z):
        return jnp.concatenate([z_pair[i * ez + z : i * ez + z + 1] for i in range(ex * ey)], 0)

    send(1, gx < ngx - 1, here + ngy, pack7(x_pair[(ex - 1) * plane :]))
    send(2, gy < ngy - 1, here + 1, pack7(y_rows(ey - 1)))
    send(3, gy > 0, here - 1, pack0(y_rows(0)))
    rn_ref[...] = dot3_few(halves(rt_ref[...]), (nh_ref[...], nl_ref[...]))
    odd = lax.rem(gz, 2) == 1
    up, down = pack7(z_rows(ez - 1)), pack0(z_rows(0))
    z1_ref[...] = jnp.concatenate([jnp.where(odd, up, down), meta], 0)
    z2_ref[...] = jnp.concatenate([jnp.where(odd, down, up), meta], 0)
    for there, out in outs:
        pl.when(there)(out.wait)


def receive(sizes, dims, xy_ref, z1_ref, z2_ref):
    ngx, ngy, ngz = sizes
    gx, gy, gz = position(sizes)
    odd = lax.rem(gz, 2) == 1

    def one(got, there):
        n = got.shape[0] - META
        payload = jnp.where(there, got[:n], 0.0)
        labels = jnp.where(there, got[n : n + dims[0]], -1.0)
        weights = jnp.where(there, got[n + dims[0] : n + dims[0] + 1], 1.0)
        return payload, labels, weights

    return [
        one(xy_ref[jnp.minimum(gx + 1, ngx - 1) * ngy + gy], gx < ngx - 1),
        one(xy_ref[jnp.maximum(gx - 1, 0) * ngy + gy], gx > 0),
        one(xy_ref[gx * ngy + jnp.minimum(gy + 1, ngy - 1)], gy < ngy - 1),
        one(xy_ref[gx * ngy + jnp.maximum(gy - 1, 0)], gy > 0),
        one(jnp.where(odd, z1_ref[...], z2_ref[...]), gz < ngz - 1),
        one(jnp.where(odd, z2_ref[...], z1_ref[...]), gz > 0),
    ]


def faces(f_ref, dims, tr_ref, around):
    ex, ey, ez = dims
    lower = lane((ez, LANES)) < FACE
    inner = lax.broadcasted_iota(jnp.int32, (ez, LANES), 0)
    none = jnp.zeros((ez, LANES), F32)
    outer = None
    if around is not None:
        outer = [(unpack0 if i % 2 == 0 else unpack7)(a[0]) for i, a in enumerate(around)]

    def local(i, pair):
        if tr_ref is None:
            return none
        return tr_ref[i * ez : (i + 1) * ez, pair]

    def remote(side, strip):
        return none if outer is None else outer[side][strip]

    for x in range(ex):
        for y in range(ey):
            i = x * ey + y
            rows = slice(i * ez, (i + 1) * ez)
            pair = slice(0, LANES)
            strip = slice(y * ez, (y + 1) * ez)
            above = local(i + ey, pair) if x < ex - 1 else remote(0, strip)
            below = local(i - ey, pair) if x > 0 else remote(1, strip)
            f_ref[rows, pair] = jnp.where(lower, above, below)
            pair = slice(LANES, 2 * LANES)
            strip = slice(x * ez, (x + 1) * ez)
            above = local(i + 1, pair) if y < ey - 1 else remote(2, strip)
            below = local(i - 1, pair) if y > 0 else remote(3, strip)
            f_ref[rows, pair] = jnp.where(lower, above, below)
            pair = slice(2 * LANES, 3 * LANES)
            above = below = none
            if tr_ref is not None:
                column = tr_ref[rows, pair]
                above = jnp.where(inner == ez - 1, 0.0, pltpu.roll(column, ez - 1, 0))
                below = jnp.where(inner == 0, 0.0, pltpu.roll(column, 1, 0))
            if outer is not None:
                above = jnp.where(inner == ez - 1, outer[4][i : i + 1], above)
                below = jnp.where(inner == 0, outer[5][i : i + 1], below)
            f_ref[rows, pair] = jnp.where(lower, above, below)


def prepare_kernel(dims, l_hbm, m_hbm, uh_ref, ul_ref, th_ref, nh_ref, tr_ref, rt_ref, rn_ref,
                   p_ref, own_ref, qh_ref, ql_ref, d_out_ref, l_ref, d_ref, f_ref, sems):
    wait = fetch(("l", "m"), sems, l=(l_hbm, l_ref), m=(m_hbm, d_ref))
    faces(f_ref, dims, tr_ref, None)
    inside = halves(f_ref[...])
    near = nh_ref[...]
    pick = selection()
    wait("l")
    wait("m")
    diagonal = diagonal_rows(d_ref)
    d_out_ref[...] = diagonal
    d = as_row(diagonal)
    lift = halves(face_order(l_ref[...]))
    lrt = dot3_few(halves(rt_ref[...]), lift)
    zeros = jnp.zeros((COARSE, DOFS - FACE), F32)
    x0 = jnp.concatenate([lrt[:, :FACE], zeros], 1)
    x7 = jnp.concatenate([zeros, lrt[:, FACE:LANES]], 1)
    yz = lrt[:, LANES:]
    group = lane((COARSE, 4 * FACE)) // FACE
    spread = jnp.concatenate([jnp.where(group == f, yz, 0.0) for f in range(4)], 0)
    both = dot(jnp.concatenate(halves(spread), 0), pick, NT)
    yz = both[: 4 * COARSE] + both[4 * COARSE :]
    mrt = rt_ref[...] * d + rn_ref[...]
    q = jnp.concatenate([x0, x7, yz, mrt, jnp.zeros_like(mrt)], 0)
    rows = q.shape[0]
    both = dot(jnp.concatenate(halves(q), 0), near, NT)
    swept = q - (both[:rows] + both[rows:])
    split = halves(swept)
    of_t = dot(split[0], near, NT)
    of_f = halves(dot3_few(split, lift))
    qh_ref[...], ql_ref[...] = of_f
    of_u = halves(jnp.concatenate([q + swept * (1.0 - d), rt_ref[...] + rn_ref[...]], 0))
    by_t = dot(jnp.concatenate([of_t, rn_ref[...]], 0).astype(BF16), th_ref[...], NT)
    by_u = dot3_few(of_u, (uh_ref[...], ul_ref[...]))
    p_ref[...] = by_u[:rows] + by_t[:rows] + dot3_few(of_f, inside)
    own_ref[...] = by_u[rows:] + by_t[rows:]


def relax_kernel(sizes, dims, p_ref, own_ref, qh_ref, ql_ref, c_ref, meta_ref, xy_ref, z1_ref, z2_ref,
                 slots_hbm, f_ref, bins_ref, sem):
    ngx, ngy, ngz = sizes
    gx, gy, gz = position(sizes)
    ex, ey, ez = dims
    plane = ey * ez
    around = receive(sizes, dims, xy_ref, z1_ref, z2_ref)
    x_up, x_down, y_up, y_down, z_up, z_down = around
    q = qh_ref[...], ql_ref[...]
    rows = q[0].shape[0]
    keep = lane((rows, LANES)) < FACE

    def through(side, payload):
        pair = slice(side // 2 * LANES, (side // 2 + 1) * LANES)
        mine = keep if side % 2 == 0 else ~keep
        few = [jnp.where(mine, a[:, pair].astype(F32), 0.0).astype(BF16) for a in q]
        return dot3_few(few, halves(payload))

    added = []
    x_above, x_below = through(0, unpack0(x_up[0])), through(1, unpack7(x_down[0]))
    y_above, y_below = through(2, unpack0(y_up[0])), through(3, unpack7(y_down[0]))
    z_above, z_below = unpack0(z_up[0]), unpack7(z_down[0])
    inner = lax.broadcasted_iota(jnp.int32, (ez, LANES), 0)
    for i in range(ex * ey):
        f_ref[i * ez : (i + 1) * ez] = jnp.where(
            lane((ez, LANES)) < FACE,
            jnp.where(inner == ez - 1, z_above[i : i + 1], 0.0),
            jnp.where(inner == 0, z_below[i : i + 1], 0.0),
        )
    z_both = dot3_few([a[:, 2 * LANES :] for a in q], halves(f_ref[...]))
    at = lane((rows, LANES))
    for x in range(ex):
        tile = z_both[:, x * LANES : (x + 1) * LANES]
        up, down = (plane - ez - x * ez) % LANES, (LANES - x * ez) % LANES
        tile = tile + jnp.where(at >= plane - ez, pltpu.roll(y_above, up, 1) if up else y_above, 0.0)
        tile = tile + jnp.where(at < ez, pltpu.roll(y_below, down, 1) if down else y_below, 0.0)
        tile = tile + (x_above if x == ex - 1 else 0.0) + (x_below if x == 0 else 0.0)
        added.append(tile)
    p = p_ref[...] + jnp.concatenate(added, 1)
    own = own_ref[...]
    small = own - p[6 * COARSE : 7 * COARSE]
    p = p / as_row(meta_ref[META : META + ex])
    p_x0, p_x7, p_y0, p_y7, p_z0, p_z7 = [p[8 * f : 8 * f + 8] for f in range(6)]
    at = lane((COARSE, LANES))

    def tiles(a):
        return [a[:, x * LANES : (x + 1) * LANES] for x in range(ex)]

    none = jnp.zeros((COARSE, LANES), F32)
    total = []
    parts = [tiles(a) for a in (small, p_x0, p_x7, p_y0, p_y7, p_z0, p_z7)]
    for x in range(ex):
        s, _, _, y0, y7, z0, z7 = [a[x] for a in parts]
        s = s + (parts[1][x + 1] if x < ex - 1 else none)
        s = s + (parts[2][x - 1] if x > 0 else none)
        s = s + jnp.where(at < plane - ez, pltpu.roll(y0, LANES - ez, 1), 0.0)
        s = s + jnp.where(at >= ez, pltpu.roll(y7, ez, 1), 0.0)
        s = s + jnp.where(at % ez < ez - 1, pltpu.roll(z0, LANES - 1, 1), 0.0)
        s = s + jnp.where(at % ez > 0, pltpu.roll(z7, 1, 1), 0.0)
        total.append(s)
    total = jnp.concatenate(total, 1)

    def scatter(values, onehot):
        high, low = halves(values)
        out = dot(jnp.concatenate([high, low], 0), jnp.concatenate([onehot, onehot], 0), NT)
        return out[:COARSE] + out[COARSE:]

    def shifted(labels, shift, keep):
        return as_row(jnp.where(keep, pltpu.roll(labels, shift, 1), -1.0))

    rows = lane((ex, LANES))
    labels = meta_ref[0:ex]
    blocks = [
        (scatter(total, onehot_rows(as_row(labels))), meta_ref[ex : ex + 1]),
        (scatter(parts[2][ex - 1], onehot_rows(x_up[1][0:1])), x_up[2]),
        (scatter(parts[1][0], onehot_rows(x_down[1][ex - 1 : ex])), x_down[2]),
        (scatter(p_y7, onehot_rows(shifted(y_up[1], plane - ez, rows >= plane - ez))), y_up[2]),
        (scatter(p_y0, onehot_rows(shifted(y_down[1], ez, rows < ez))), y_down[2]),
        (scatter(p_z7, onehot_rows(shifted(z_up[1], ez - 1, rows % ez == ez - 1))), z_up[2]),
        (scatter(p_z0, onehot_rows(shifted(z_down[1], LANES - ez + 1, rows % ez == 0))), z_down[2]),
    ]
    columns = [jnp.broadcast_to(c_ref[:, k : k + 1], (COARSE, LANES)) for k in range(COARSE)]

    def mixed(block):
        out = block + block
        for k in range(COARSE):
            out = out - columns[k] * block[k : k + 1]
        return out

    def packed(block):
        half = COARSE // 2
        return jnp.where(lane((half, LANES)) < FACE, block[:half], block[half:])

    b0, xu, xd, yu, yd, zu, zd = [packed(z / w) for z, w in blocks]
    a0, axu, axd, ayu, ayd, azu, azd = [packed(mixed(z)) for z, _ in blocks]

    count = slots_hbm.shape[0]
    bins_ref[...] = jnp.zeros_like(bins_ref)

    def put(dx, dy, dz, share):
        there = (dy >= 0) & (dy < ngy) & (dz >= 0) & (dz < ngz)
        bins_ref[jnp.where(there, (dx * ngy + dy) * ngz + dz, count)] = share

    line = b0 + xu + xd
    sides = yu + yd + zu + zd
    for dx in range(ngx):
        same = (gx == dx).astype(F32)
        up = (gx + 1 == dx).astype(F32)
        down = (gx - 1 == dx).astype(F32)
        column = same * b0 + up * xu + down * xd
        put(dx, gy, gz, line + same * (sides + a0) + up * axu + down * axd)
        put(dx, gy + 1, gz, yu + column + same * ayu)
        put(dx, gy - 1, gz, yd + column + same * ayd)
        put(dx, gy, gz + 1, zu + column + same * azu)
        put(dx, gy, gz - 1, zd + column + same * azd)
    put(gx, gy + 2, gz, yu)
    put(gx, gy - 2, gz, yd)
    put(gx, gy, gz + 2, zu)
    put(gx, gy, gz - 2, zd)
    put(gx, gy + 1, gz + 1, yu + zu)
    put(gx, gy + 1, gz - 1, yu + zd)
    put(gx, gy - 1, gz + 1, yd + zu)
    put(gx, gy - 1, gz - 1, yd + zd)
    copy = pltpu.make_async_copy(bins_ref.at[pl.ds(0, count)], slots_hbm, sem)
    copy.start()
    copy.wait()


def second_kernel(sizes, dims, rhs_hbm, s_hbm, l_hbm, uh_ref, ul_ref, tr_ref, d_ref, meta_ref, rt_ref, xy_ref, z1_ref, z2_ref,
                  second_ref, rs_ref, oh_ref, rhs_ref, s_ref, l_ref, f_ref, sems):
    wait = fetch(("l", "s", "rhs"), sems, rhs=(rhs_hbm, rhs_ref), s=(s_hbm, s_ref), l=(l_hbm, l_ref))
    ex = dims[0]
    faces(f_ref, dims, tr_ref, receive(sizes, dims, xy_ref, z1_ref, z2_ref))
    onehot = onehot_rows(as_row(meta_ref[:ex]))
    oh_ref[...] = jnp.concatenate([onehot, onehot], 0).astype(F32).T.astype(BF16)
    rt = halves(rt_ref[...])
    rs_ref[...] = jnp.concatenate([rt[0], rt[0], rt[1], jnp.zeros_like(rt[0])], 0)
    wait("l")
    r1 = dot3(halves(f_ref[...]), halves(face_order(l_ref[...])))
    wait("s")
    near = near_identity(s_ref, slice(0, DOFS))
    wait("rhs")
    u = uh_ref[...].astype(F32) + ul_ref[...].astype(F32)
    d = as_row(d_ref[...])
    r1 = r1 + dot3(halves(rhs_ref[...] - u), near) + u * (1.0 - d)
    v = u + (r1 - dot3(halves(r1), near))
    rc = reciprocal(meta_ref[META : META + ex])
    second_ref[...] = v * jnp.concatenate([rc] * (DOFS // LANES), 1)


def correct_kernel(second_ref, slots_ref, meta_ref, oh_ref, rs_ref, out_hbm, out_ref, sems):
    total = jnp.sum(slots_ref[...], 0)
    ztwo = jnp.concatenate([total[:, :FACE], total[:, FACE:]], 0) / meta_ref[4:5, :FACE]
    high, low = halves(ztwo)
    stacked = jnp.concatenate([high, low, high, jnp.zeros_like(high)], 0)
    prolonged = dot(stacked, rs_ref[...], TN)
    prolonged = jnp.concatenate(halves(prolonged), 0)
    chunk = DOFS // sems.shape[0]
    copies = []
    for i in range(sems.shape[0]):
        rows = slice(i * chunk, (i + 1) * chunk)
        out_ref[rows] = second_ref[rows] + dot(oh_ref[rows], prolonged)
        copy = pltpu.make_async_copy(out_ref.at[rows], out_hbm.at[rows], sems.at[i])
        copy.start()
        copies.append(copy)
    for copy in copies:
        copy.wait()


def shards(sizes, rhs, coef, mass, smoother, lift, restrict, coarse_block_matrix, element_cluster_index):
    ngx, ngy, ngz = sizes
    dims = coef.shape
    ex, ey, ez = dims
    flat = rhs.reshape(ex * ey * ez, DOFS)
    face = ey * ez * FACE // LANES
    tip = ex * ey * FACE // LANES
    params = pltpu.CompilerParams(vmem_limit_bytes=40 * 1024 * 1024)
    shape = jax.ShapeDtypeStruct
    hbm = pl.BlockSpec(memory_space=pltpu.HBM)
    vmem = pl.BlockSpec(memory_space=pltpu.VMEM)
    cost = pl.CostEstimate(flops=2 * 10**9, bytes_accessed=4 * 2**20, transcendentals=0)
    def far(*arrays):
        return [pltpu.with_memory_space_constraint(a, pltpu.HBM) for a in arrays]

    full = shape((DOFS, DOFS), F32)
    split = shape((DOFS, DOFS), BF16)
    count = ngx * ngy * ngz
    wide = shape((8 * COARSE, 3 * LANES), BF16)
    few = shape((COARSE, DOFS), F32)
    uh, ul, th, nh, tr, meta, xy, z1, z2, rt, c, rn = pl.pallas_call(
        functools.partial(smooth_kernel, sizes),
        out_shape=(
            split,
            split,
            split,
            split,
            shape((DOFS, 3 * LANES), F32),
            shape((2 * META, LANES), F32),
            shape((ngx * ngy, face + META, LANES), F32),
            shape((tip + META, LANES), F32),
            shape((tip + META, LANES), F32),
            few,
            shape((COARSE, COARSE), F32),
            few,
        ),
        in_specs=[hbm] * 6,
        out_specs=[vmem] * 6 + [hbm] + [vmem] * 5,
        scratch_shapes=[
            pltpu.VMEM((DOFS, DOFS), F32),
            pltpu.VMEM((DOFS, DOFS), F32),
            pltpu.VMEM(dims, F32),
            pltpu.VMEM(dims, jnp.int32),
            pltpu.VMEM((DOFS, DOFS), F32),
            pltpu.VMEM((DOFS, DOFS), BF16),
            pltpu.VMEM((4, face + META, LANES), F32),
            pltpu.SemaphoreType.DMA((12,)),
            pltpu.SemaphoreType.DMA((4,)),
        ],
        compiler_params=params,
        cost_estimate=cost,
        name="smooth",
    )(*far(flat, smoother, coef, element_cluster_index, restrict.T, coarse_block_matrix))
    def swaps(start):
        pairs = [(i, i + 1) for i in range(start, ngz - 1, 2)]
        return pairs + [(j, i) for i, j in pairs]

    z1 = lax.ppermute(z1, "gz", swaps(1))
    z2 = lax.ppermute(z2, "gz", swaps(0))
    xy = lax.all_to_all(xy, ("gx", "gy"), 0, 0, tiled=True)
    p, own, fh, fl, d = pl.pallas_call(
        functools.partial(prepare_kernel, dims),
        out_shape=(shape((8 * COARSE, DOFS), F32), few, wide, wide, shape((DOFS // LANES, LANES), F32)),
        in_specs=[hbm] * 2 + [vmem] * 7,
        scratch_shapes=[
            pltpu.VMEM((3 * LANES, DOFS), F32),
            pltpu.VMEM((DOFS // LANES, LANES, LANES), F32),
            pltpu.VMEM((DOFS, 3 * LANES), F32),
            pltpu.SemaphoreType.DMA((5,)),
        ],
        compiler_params=params,
        cost_estimate=cost,
        name="prepare",
    )(*far(lift, mass), uh, ul, th, nh, tr, rt, rn)
    slots = pl.pallas_call(
        functools.partial(relax_kernel, sizes, dims),
        out_shape=shape((count, COARSE // 2, LANES), F32),
        out_specs=hbm,
        scratch_shapes=[
            pltpu.VMEM((DOFS, LANES), F32),
            pltpu.VMEM((count + 1, COARSE // 2, LANES), F32),
            pltpu.SemaphoreType.DMA,
        ],
        compiler_params=params,
        cost_estimate=cost,
        name="relax",
    )(p, own, fh, fl, c, meta, xy, z1, z2)
    slots = lax.all_to_all(slots, ("gx", "gy", "gz"), 0, 0, tiled=True)
    second, rs, oh = pl.pallas_call(
        functools.partial(second_kernel, sizes, dims),
        out_shape=(
            full,
            shape((4 * COARSE, DOFS), BF16),
            shape((DOFS, LANES), BF16),
        ),
        in_specs=[hbm] * 3 + [vmem] * 9,
        scratch_shapes=[
            pltpu.VMEM((DOFS, DOFS), F32),
            pltpu.VMEM((DOFS, DOFS), F32),
            pltpu.VMEM((3 * LANES, DOFS), F32),
            pltpu.VMEM((DOFS, 3 * LANES), F32),
            pltpu.SemaphoreType.DMA((3,)),
        ],
        compiler_params=params,
        cost_estimate=cost,
        name="second",
    )(*far(flat, smoother, lift), uh, ul, tr, d, meta, rt, xy, z1, z2)
    out = pl.pallas_call(
        correct_kernel,
        out_shape=shape((DOFS, DOFS), F32),
        out_specs=hbm,
        scratch_shapes=[pltpu.VMEM((DOFS, DOFS), F32), pltpu.SemaphoreType.DMA((4,))],
        compiler_params=params,
        name="correct",
    )(second, slots, meta, oh, rs)
    return out.reshape(rhs.shape)


def solution(mesh):
    sizes = (mesh.shape["gx"], mesh.shape["gy"], mesh.shape["gz"])
    cells = P("gx", "gy", "gz")
    return jax.shard_map(
        functools.partial(shards, sizes),
        mesh=mesh,
        in_specs=(P("gx", "gy", "gz", None), cells, P(), P(), P(), P(), P(), cells),
        out_specs=P("gx", "gy", "gz", None),
        check_vma=False,
    )
```

```python
import functools

import jax
import jax.numpy as jnp
from jax import lax
from jax.experimental import pallas as pl
from jax.experimental.pallas import tpu as pltpu
from jax.sharding import PartitionSpec as P

EDGE = 8
DOFS = 512
FACE = 64
COARSE = 8
CLUSTERS = 64
LANES = 128
META = 8

F32 = jnp.float32
BF16 = jnp.bfloat16
NT = (((1,), (1,)), ((), ()))
TN = (((0,), (0,)), ((), ()))


def selection():
    column = lane((1, 4 * FACE))
    face, a, b = column // FACE, column % FACE // EDGE, column % EDGE
    node = jnp.where(face < 2, a * 64 + face * 56 + b, a * 64 + b * 8 + (face - 2) * 7)
    at = lax.broadcasted_iota(jnp.int32, (DOFS, 4 * FACE), 0)
    return jnp.where(at == node, 1.0, 0.0).astype(BF16)


def halves(x):
    high = x.astype(BF16)
    return high, (x - high.astype(F32)).astype(BF16)


def dot(a, b, dims=(((1,), (0,)), ((), ()))):
    return lax.dot_general(a, b, dims, preferred_element_type=F32)


def dot3(a, b, dims=(((1,), (0,)), ((), ()))):
    return dot(a[0], b[0], dims) + (dot(a[0], b[1], dims) + dot(a[1], b[0], dims))


def dot3_few(a, b):
    n = a[0].shape[0]
    both = dot(jnp.concatenate(a, 0), b[0], NT)
    return both[:n] + (both[n:] + dot(a[0], b[1], NT))


def lane(shape):
    return lax.broadcasted_iota(jnp.int32, shape, len(shape) - 1)


def swap(x):
    return pltpu.roll(x, FACE, 1)


def pack0(t):
    n = t.shape[0] // 2
    return jnp.where(lane((n, LANES)) < FACE, t[:n], swap(t[n:]))


def pack7(t):
    n = t.shape[0] // 2
    return jnp.where(lane((n, LANES)) < FACE, swap(t[:n]), t[n:])


def unpack0(p):
    return jnp.concatenate([p, swap(p)], 0)


def unpack7(p):
    return jnp.concatenate([swap(p), p], 0)


def cell_rows(ref):
    ex, ey, ez = ref.shape
    rows = []
    for x in range(ex):
        rows.append(jnp.concatenate([ref[x, y : y + 1, :] for y in range(ey)], 1))
    return jnp.concatenate(rows, 0).astype(F32)


def face_order(lift):
    return jnp.concatenate([lift[(f ^ 1) * FACE : ((f ^ 1) + 1) * FACE] for f in range(6)], 0)


def reciprocal(rows):
    n = rows.shape[0]
    columns = (1.0 / jnp.concatenate([rows, jnp.ones((LANES - n, LANES), F32)], 0)).T
    return jnp.concatenate([jnp.broadcast_to(columns[:, x : x + 1], (LANES, LANES)) for x in range(n)], 0)


def as_row(rows):
    return jnp.concatenate([rows[x : x + 1] for x in range(rows.shape[0])], 1)


def onehot_rows(row):
    n = row.shape[1]
    at = lax.broadcasted_iota(jnp.int32, (CLUSTERS, n), 0).astype(F32)
    return jnp.where(at == row, 1.0, 0.0).astype(BF16)


def position(sizes):
    return lax.axis_index("gx"), lax.axis_index("gy"), lax.axis_index("gz")


def near_identity(s_ref, part):
    diagonal = lax.broadcasted_iota(jnp.int32, (LANES, LANES), 0) == lane((LANES, LANES))
    identity = jnp.where(diagonal, 1.0, 0.0)
    rows = []
    for start in range(part.start, part.stop, LANES):
        s = s_ref[start : start + LANES]
        tile = identity - s[:, start : start + LANES]
        pieces = [-s[:, :start], tile, -s[:, start + LANES :]]
        rows.append(jnp.concatenate([piece for piece in pieces if piece.shape[1]], 1))
    return halves(jnp.concatenate(rows, 0))


def start_all(pairs, sems):
    copies = [pltpu.make_async_copy(src, dst, sems.at[i]) for i, (src, dst) in enumerate(pairs)]
    for copy in copies:
        copy.start()
    return copies


def fetch(names, sems, rhs=None, s=None, m=None, l=None):
    pairs = {"rhs": [rhs], "s": [s], "l": [l], "m": []}
    for i in range(DOFS // LANES if m else 0):
        block = slice(i * LANES, (i + 1) * LANES)
        pairs["m"].append((m[0].at[block, block], m[1].at[i]))
    counts = [len(pairs[name]) for name in names]
    first = [sum(counts[:i]) for i in range(len(names))]
    copies = start_all([pair for name in names for pair in pairs[name]], sems)

    def wait(name):
        i = names.index(name)
        for copy in copies[first[i] : first[i] + counts[i]]:
            copy.wait()

    return wait


def diagonal_rows(d_ref):
    here = lax.broadcasted_iota(jnp.int32, (LANES, LANES), 0) == lane((LANES, LANES))
    return jnp.concatenate(
        [jnp.sum(jnp.where(here, d_ref[i], 0.0), 0, keepdims=True) for i in range(d_ref.shape[0])], 0
    )


def traces(u, split, pick, scale):
    lower = lane((u.shape[0], LANES)) < FACE
    picked = dot(split[0], pick) + dot(split[1], pick)
    x_pair = jnp.where(lower, u[:, :LANES], u[:, DOFS - LANES :]) * scale
    return x_pair, picked[:, :LANES] * scale, picked[:, LANES:] * scale


def smooth_kernel(sizes, rhs_hbm, s_hbm, coef_hbm, lab_hbm, rt_hbm, c_hbm,
                  uh_ref, ul_ref, th_ref, nh_ref, tr_ref, meta_ref, xy_hbm, z1_ref, z2_ref, rt_ref, c_ref, rn_ref,
                  rhs_ref, s_ref, coef_ref, lab_ref, t_ref, nl_ref, out_ref, sems, out_sems):
    ngx, ngy, ngz = sizes
    gx, gy, gz = position(sizes)
    half = DOFS // 2
    blocks = [slice(0, half), slice(half, DOFS)]
    pairs = [(coef_hbm, coef_ref), (lab_hbm, lab_ref), (rt_hbm, rt_ref), (c_hbm, c_ref)]
    for part in blocks:
        quarters = [slice(part.start + i * half // 2, part.start + (i + 1) * half // 2) for i in range(2)]
        pairs += [(s_hbm.at[rows], s_ref.at[rows]) for rows in quarters]
        pairs += [(rhs_hbm.at[rows, part], rhs_ref.at[rows, part]) for rows in blocks]
    copies = start_all(pairs, sems)

    def wait(first, count):
        for copy in copies[first : first + count]:
            copy.wait()

    ex, ey, ez = lab_ref.shape
    plane = ey * ez
    pick = selection()
    wait(0, 4)
    lab = cell_rows(lab_ref)
    counts = dot(jnp.ones((8, DOFS), BF16), onehot_rows(as_row(lab)), NT)
    weights = 1.0 + jnp.concatenate([counts[0:1], counts[0:1]], 1)
    meta = jnp.concatenate([lab, weights, jnp.zeros((META - 5, LANES), F32)], 0)
    meta_ref[:META] = meta
    meta_ref[META : META + ex] = cell_rows(coef_ref)
    rc = reciprocal(meta_ref[META : META + ex])

    def near_part(part):
        near = near_identity(s_ref, part)
        nh_ref[part], nl_ref[part] = near
        return near

    here = gx * ngy + gy
    outs = []

    def send(i, there, slot, packed):
        n = packed.shape[0]
        out_ref[i, :n] = packed
        out_ref[i, n:] = meta
        out = pltpu.make_async_copy(out_ref.at[i], xy_hbm.at[jnp.where(there, slot, here)], out_sems.at[i])
        pl.when(there)(out.start)
        outs.append((there, out))

    wait(4, 2)
    near = near_part(blocks[0])
    wait(6, 2)
    t_ref[...] = dot3(halves(rhs_ref[:, blocks[0]]), near)
    wait(8, 4)
    near = near_part(blocks[1])
    pairs = []
    for rows in blocks:
        t = t_ref[rows] + dot3(halves(rhs_ref[rows, blocks[1]]), near)
        th_ref[rows] = t.astype(BF16)
        u = rhs_ref[rows] - t
        split = halves(u)
        uh_ref[rows], ul_ref[rows] = split
        pairs.append(traces(u, split, pick, rc[rows]))
        for i, pair in enumerate(pairs[-1]):
            tr_ref[rows, i * LANES : (i + 1) * LANES] = pair
        if rows is blocks[0]:
            send(0, gx > 0, here - ngy, pack0(pairs[0][0][:plane]))
    x_pair, y_pair, z_pair = [jnp.concatenate([block[i] for block in pairs], 0) for i in range(3)]

    def y_rows(y):
        return jnp.concatenate(
            [y_pair[x * plane + y * ez : x * plane + (y + 1) * ez] for x in range(ex)], 0
        )

    def z_rows(z):
        return jnp.concatenate([z_pair[i * ez + z : i * ez + z + 1] for i in range(ex * ey)], 0)

    send(1, gx < ngx - 1, here + ngy, pack7(x_pair[(ex - 1) * plane :]))
    send(2, gy < ngy - 1, here + 1, pack7(y_rows(ey - 1)))
    send(3, gy > 0, here - 1, pack0(y_rows(0)))
    rn_ref[...] = dot3_few(halves(rt_ref[...]), (nh_ref[...], nl_ref[...]))
    odd = lax.rem(gz, 2) == 1
    up, down = pack7(z_rows(ez - 1)), pack0(z_rows(0))
    z1_ref[...] = jnp.concatenate([jnp.where(odd, up, down), meta], 0)
    z2_ref[...] = jnp.concatenate([jnp.where(odd, down, up), meta], 0)
    for there, out in outs:
        pl.when(there)(out.wait)


def receive(sizes, dims, xy_ref, z1_ref, z2_ref):
    ngx, ngy, ngz = sizes
    gx, gy, gz = position(sizes)
    odd = lax.rem(gz, 2) == 1

    def one(got, there):
        n = got.shape[0] - META
        payload = jnp.where(there, got[:n], 0.0)
        labels = jnp.where(there, got[n : n + dims[0]], -1.0)
        weights = jnp.where(there, got[n + dims[0] : n + dims[0] + 1], 1.0)
        return payload, labels, weights

    return [
        one(xy_ref[jnp.minimum(gx + 1, ngx - 1) * ngy + gy], gx < ngx - 1),
        one(xy_ref[jnp.maximum(gx - 1, 0) * ngy + gy], gx > 0),
        one(xy_ref[gx * ngy + jnp.minimum(gy + 1, ngy - 1)], gy < ngy - 1),
        one(xy_ref[gx * ngy + jnp.maximum(gy - 1, 0)], gy > 0),
        one(jnp.where(odd, z1_ref[...], z2_ref[...]), gz < ngz - 1),
        one(jnp.where(odd, z2_ref[...], z1_ref[...]), gz > 0),
    ]


def faces(f_ref, dims, tr_ref, around):
    ex, ey, ez = dims
    lower = lane((ez, LANES)) < FACE
    inner = lax.broadcasted_iota(jnp.int32, (ez, LANES), 0)
    none = jnp.zeros((ez, LANES), F32)
    outer = None
    if around is not None:
        outer = [(unpack0 if i % 2 == 0 else unpack7)(a[0]) for i, a in enumerate(around)]

    def local(i, pair):
        if tr_ref is None:
            return none
        return tr_ref[i * ez : (i + 1) * ez, pair]

    def remote(side, strip):
        return none if outer is None else outer[side][strip]

    for x in range(ex):
        for y in range(ey):
            i = x * ey + y
            rows = slice(i * ez, (i + 1) * ez)
            pair = slice(0, LANES)
            strip = slice(y * ez, (y + 1) * ez)
            above = local(i + ey, pair) if x < ex - 1 else remote(0, strip)
            below = local(i - ey, pair) if x > 0 else remote(1, strip)
            f_ref[rows, pair] = jnp.where(lower, above, below)
            pair = slice(LANES, 2 * LANES)
            strip = slice(x * ez, (x + 1) * ez)
            above = local(i + 1, pair) if y < ey - 1 else remote(2, strip)
            below = local(i - 1, pair) if y > 0 else remote(3, strip)
            f_ref[rows, pair] = jnp.where(lower, above, below)
            pair = slice(2 * LANES, 3 * LANES)
            above = below = none
            if tr_ref is not None:
                column = tr_ref[rows, pair]
                above = jnp.where(inner == ez - 1, 0.0, pltpu.roll(column, ez - 1, 0))
                below = jnp.where(inner == 0, 0.0, pltpu.roll(column, 1, 0))
            if outer is not None:
                above = jnp.where(inner == ez - 1, outer[4][i : i + 1], above)
                below = jnp.where(inner == 0, outer[5][i : i + 1], below)
            f_ref[rows, pair] = jnp.where(lower, above, below)


def prepare_kernel(dims, l_hbm, m_hbm, uh_ref, ul_ref, th_ref, nh_ref, tr_ref, rt_ref, rn_ref,
                   p_ref, own_ref, qh_ref, ql_ref, d_out_ref, l_ref, d_ref, f_ref, sems):
    wait = fetch(("l", "m"), sems, l=(l_hbm, l_ref), m=(m_hbm, d_ref))
    faces(f_ref, dims, tr_ref, None)
    inside = halves(f_ref[...])
    near = nh_ref[...]
    pick = selection()
    wait("l")
    wait("m")
    diagonal = diagonal_rows(d_ref)
    d_out_ref[...] = diagonal
    d = as_row(diagonal)
    lift = halves(face_order(l_ref[...]))
    lrt = dot3_few(halves(rt_ref[...]), lift)
    zeros = jnp.zeros((COARSE, DOFS - FACE), F32)
    x0 = jnp.concatenate([lrt[:, :FACE], zeros], 1)
    x7 = jnp.concatenate([zeros, lrt[:, FACE:LANES]], 1)
    yz = lrt[:, LANES:]
    group = lane((COARSE, 4 * FACE)) // FACE
    spread = jnp.concatenate([jnp.where(group == f, yz, 0.0) for f in range(4)], 0)
    both = dot(jnp.concatenate(halves(spread), 0), pick, NT)
    yz = both[: 4 * COARSE] + both[4 * COARSE :]
    mrt = rt_ref[...] * d + rn_ref[...]
    q = jnp.concatenate([x0, x7, yz, mrt, jnp.zeros_like(mrt)], 0)
    rows = q.shape[0]
    both = dot(jnp.concatenate(halves(q), 0), near, NT)
    swept = q - (both[:rows] + both[rows:])
    split = halves(swept)
    of_t = dot(split[0], near, NT)
    of_f = halves(dot3_few(split, lift))
    qh_ref[...], ql_ref[...] = of_f
    of_u = halves(jnp.concatenate([q + swept * (1.0 - d), rt_ref[...] + rn_ref[...]], 0))
    by_t = dot(jnp.concatenate([of_t, rn_ref[...]], 0).astype(BF16), th_ref[...], NT)
    by_u = dot3_few(of_u, (uh_ref[...], ul_ref[...]))
    p_ref[...] = by_u[:rows] + by_t[:rows] + dot3_few(of_f, inside)
    own_ref[...] = by_u[rows:] + by_t[rows:]


def relax_kernel(sizes, dims, p_ref, own_ref, qh_ref, ql_ref, c_ref, meta_ref, xy_ref, z1_ref, z2_ref,
                 slots_hbm, f_ref, bins_ref, sem):
    ngx, ngy, ngz = sizes
    gx, gy, gz = position(sizes)
    ex, ey, ez = dims
    plane = ey * ez
    around = receive(sizes, dims, xy_ref, z1_ref, z2_ref)
    x_up, x_down, y_up, y_down, z_up, z_down = around
    q = qh_ref[...], ql_ref[...]
    rows = q[0].shape[0]
    keep = lane((rows, LANES)) < FACE

    def through(side, payload):
        pair = slice(side // 2 * LANES, (side // 2 + 1) * LANES)
        mine = keep if side % 2 == 0 else ~keep
        few = [jnp.where(mine, a[:, pair].astype(F32), 0.0).astype(BF16) for a in q]
        return dot3_few(few, halves(payload))

    added = []
    x_above, x_below = through(0, unpack0(x_up[0])), through(1, unpack7(x_down[0]))
    y_above, y_below = through(2, unpack0(y_up[0])), through(3, unpack7(y_down[0]))
    z_above, z_below = unpack0(z_up[0]), unpack7(z_down[0])
    inner = lax.broadcasted_iota(jnp.int32, (ez, LANES), 0)
    for i in range(ex * ey):
        f_ref[i * ez : (i + 1) * ez] = jnp.where(
            lane((ez, LANES)) < FACE,
            jnp.where(inner == ez - 1, z_above[i : i + 1], 0.0),
            jnp.where(inner == 0, z_below[i : i + 1], 0.0),
        )
    z_both = dot3_few([a[:, 2 * LANES :] for a in q], halves(f_ref[...]))
    at = lane((rows, LANES))
    for x in range(ex):
        tile = z_both[:, x * LANES : (x + 1) * LANES]
        up, down = (plane - ez - x * ez) % LANES, (LANES - x * ez) % LANES
        tile = tile + jnp.where(at >= plane - ez, pltpu.roll(y_above, up, 1) if up else y_above, 0.0)
        tile = tile + jnp.where(at < ez, pltpu.roll(y_below, down, 1) if down else y_below, 0.0)
        tile = tile + (x_above if x == ex - 1 else 0.0) + (x_below if x == 0 else 0.0)
        added.append(tile)
    p = p_ref[...] + jnp.concatenate(added, 1)
    own = own_ref[...]
    small = own - p[6 * COARSE : 7 * COARSE]
    p = p / as_row(meta_ref[META : META + ex])
    p_x0, p_x7, p_y0, p_y7, p_z0, p_z7 = [p[8 * f : 8 * f + 8] for f in range(6)]
    at = lane((COARSE, LANES))

    def tiles(a):
        return [a[:, x * LANES : (x + 1) * LANES] for x in range(ex)]

    none = jnp.zeros((COARSE, LANES), F32)
    total = []
    parts = [tiles(a) for a in (small, p_x0, p_x7, p_y0, p_y7, p_z0, p_z7)]
    for x in range(ex):
        s, _, _, y0, y7, z0, z7 = [a[x] for a in parts]
        s = s + (parts[1][x + 1] if x < ex - 1 else none)
        s = s + (parts[2][x - 1] if x > 0 else none)
        s = s + jnp.where(at < plane - ez, pltpu.roll(y0, LANES - ez, 1), 0.0)
        s = s + jnp.where(at >= ez, pltpu.roll(y7, ez, 1), 0.0)
        s = s + jnp.where(at % ez < ez - 1, pltpu.roll(z0, LANES - 1, 1), 0.0)
        s = s + jnp.where(at % ez > 0, pltpu.roll(z7, 1, 1), 0.0)
        total.append(s)
    total = jnp.concatenate(total, 1)

    def scatter(values, onehot):
        high, low = halves(values)
        out = dot(jnp.concatenate([high, low], 0), jnp.concatenate([onehot, onehot], 0), NT)
        return out[:COARSE] + out[COARSE:]

    def shifted(labels, shift, keep):
        return as_row(jnp.where(keep, pltpu.roll(labels, shift, 1), -1.0))

    rows = lane((ex, LANES))
    labels = meta_ref[0:ex]
    blocks = [
        (scatter(total, onehot_rows(as_row(labels))), meta_ref[ex : ex + 1]),
        (scatter(parts[2][ex - 1], onehot_rows(x_up[1][0:1])), x_up[2]),
        (scatter(parts[1][0], onehot_rows(x_down[1][ex - 1 : ex])), x_down[2]),
        (scatter(p_y7, onehot_rows(shifted(y_up[1], plane - ez, rows >= plane - ez))), y_up[2]),
        (scatter(p_y0, onehot_rows(shifted(y_down[1], ez, rows < ez))), y_down[2]),
        (scatter(p_z7, onehot_rows(shifted(z_up[1], ez - 1, rows % ez == ez - 1))), z_up[2]),
        (scatter(p_z0, onehot_rows(shifted(z_down[1], LANES - ez + 1, rows % ez == 0))), z_down[2]),
    ]
    columns = [jnp.broadcast_to(c_ref[:, k : k + 1], (COARSE, LANES)) for k in range(COARSE)]

    def mixed(block):
        out = block + block
        for k in range(COARSE):
            out = out - columns[k] * block[k : k + 1]
        return out

    def packed(block):
        half = COARSE // 2
        return jnp.where(lane((half, LANES)) < FACE, block[:half], block[half:])

    b0, xu, xd, yu, yd, zu, zd = [packed(z / w) for z, w in blocks]
    a0, axu, axd, ayu, ayd, azu, azd = [packed(mixed(z)) for z, _ in blocks]

    count = slots_hbm.shape[0]
    bins_ref[...] = jnp.zeros_like(bins_ref)

    def put(dx, dy, dz, share):
        there = (dy >= 0) & (dy < ngy) & (dz >= 0) & (dz < ngz)
        bins_ref[jnp.where(there, (dx * ngy + dy) * ngz + dz, count)] = share

    line = b0 + xu + xd
    sides = yu + yd + zu + zd
    for dx in range(ngx):
        same = (gx == dx).astype(F32)
        up = (gx + 1 == dx).astype(F32)
        down = (gx - 1 == dx).astype(F32)
        column = same * b0 + up * xu + down * xd
        put(dx, gy, gz, line + same * (sides + a0) + up * axu + down * axd)
        put(dx, gy + 1, gz, yu + column + same * ayu)
        put(dx, gy - 1, gz, yd + column + same * ayd)
        put(dx, gy, gz + 1, zu + column + same * azu)
        put(dx, gy, gz - 1, zd + column + same * azd)
    put(gx, gy + 2, gz, yu)
    put(gx, gy - 2, gz, yd)
    put(gx, gy, gz + 2, zu)
    put(gx, gy, gz - 2, zd)
    put(gx, gy + 1, gz + 1, yu + zu)
    put(gx, gy + 1, gz - 1, yu + zd)
    put(gx, gy - 1, gz + 1, yd + zu)
    put(gx, gy - 1, gz - 1, yd + zd)
    copy = pltpu.make_async_copy(bins_ref.at[pl.ds(0, count)], slots_hbm, sem)
    copy.start()
    copy.wait()


def second_kernel(sizes, dims, rhs_hbm, s_hbm, l_hbm, uh_ref, ul_ref, tr_ref, d_ref, meta_ref, rt_ref, xy_ref, z1_ref, z2_ref,
                  second_ref, rs_ref, oh_ref, rhs_ref, s_ref, l_ref, f_ref, sems):
    wait = fetch(("l", "s", "rhs"), sems, rhs=(rhs_hbm, rhs_ref), s=(s_hbm, s_ref), l=(l_hbm, l_ref))
    ex = dims[0]
    faces(f_ref, dims, tr_ref, receive(sizes, dims, xy_ref, z1_ref, z2_ref))
    onehot = onehot_rows(as_row(meta_ref[:ex]))
    oh_ref[...] = jnp.concatenate([onehot, onehot], 0).astype(F32).T.astype(BF16)
    rt = halves(rt_ref[...])
    rs_ref[...] = jnp.concatenate([rt[0], rt[0], rt[1], jnp.zeros_like(rt[0])], 0)
    wait("l")
    r1 = dot3(halves(f_ref[...]), halves(face_order(l_ref[...])))
    wait("s")
    near = near_identity(s_ref, slice(0, DOFS))
    wait("rhs")
    u = uh_ref[...].astype(F32) + ul_ref[...].astype(F32)
    d = as_row(d_ref[...])
    r1 = r1 + dot3(halves(rhs_ref[...] - u), near) + u * (1.0 - d)
    v = u + (r1 - dot3(halves(r1), near))
    rc = reciprocal(meta_ref[META : META + ex])
    second_ref[...] = v * jnp.concatenate([rc] * (DOFS // LANES), 1)


def correct_kernel(second_ref, slots_ref, meta_ref, oh_ref, rs_ref, out_hbm, out_ref, sems):
    total = jnp.sum(slots_ref[...], 0)
    ztwo = jnp.concatenate([total[:, :FACE], total[:, FACE:]], 0) / meta_ref[4:5, :FACE]
    high, low = halves(ztwo)
    stacked = jnp.concatenate([high, low, high, jnp.zeros_like(high)], 0)
    prolonged = dot(stacked, rs_ref[...], TN)
    prolonged = jnp.concatenate(halves(prolonged), 0)
    chunk = DOFS // sems.shape[0]
    copies = []
    for i in range(sems.shape[0]):
        rows = slice(i * chunk, (i + 1) * chunk)
        out_ref[rows] = second_ref[rows] + dot(oh_ref[rows], prolonged)
        copy = pltpu.make_async_copy(out_ref.at[rows], out_hbm.at[rows], sems.at[i])
        copy.start()
        copies.append(copy)
    for copy in copies:
        copy.wait()


def shards(sizes, rhs, coef, mass, smoother, lift, restrict, coarse_block_matrix, element_cluster_index):
    ngx, ngy, ngz = sizes
    dims = coef.shape
    ex, ey, ez = dims
    flat = rhs.reshape(ex * ey * ez, DOFS)
    face = ey * ez * FACE // LANES
    tip = ex * ey * FACE // LANES
    params = pltpu.CompilerParams(vmem_limit_bytes=40 * 1024 * 1024)
    shape = jax.ShapeDtypeStruct
    hbm = pl.BlockSpec(memory_space=pltpu.HBM)
    vmem = pl.BlockSpec(memory_space=pltpu.VMEM)
    cost = pl.CostEstimate(flops=2 * 10**9, bytes_accessed=4 * 2**20, transcendentals=0)
    def far(*arrays):
        return [pltpu.with_memory_space_constraint(a, pltpu.HBM) for a in arrays]

    full = shape((DOFS, DOFS), F32)
    split = shape((DOFS, DOFS), BF16)
    count = ngx * ngy * ngz
    wide = shape((8 * COARSE, 3 * LANES), BF16)
    few = shape((COARSE, DOFS), F32)
    uh, ul, th, nh, tr, meta, xy, z1, z2, rt, c, rn = pl.pallas_call(
        functools.partial(smooth_kernel, sizes),
        out_shape=(
            split,
            split,
            split,
            split,
            shape((DOFS, 3 * LANES), F32),
            shape((2 * META, LANES), F32),
            shape((ngx * ngy, face + META, LANES), F32),
            shape((tip + META, LANES), F32),
            shape((tip + META, LANES), F32),
            few,
            shape((COARSE, COARSE), F32),
            few,
        ),
        in_specs=[hbm] * 6,
        out_specs=[vmem] * 6 + [hbm] + [vmem] * 5,
        scratch_shapes=[
            pltpu.VMEM((DOFS, DOFS), F32),
            pltpu.VMEM((DOFS, DOFS), F32),
            pltpu.VMEM(dims, F32),
            pltpu.VMEM(dims, jnp.int32),
            pltpu.VMEM((DOFS, DOFS), F32),
            pltpu.VMEM((DOFS, DOFS), BF16),
            pltpu.VMEM((4, face + META, LANES), F32),
            pltpu.SemaphoreType.DMA((12,)),
            pltpu.SemaphoreType.DMA((4,)),
        ],
        compiler_params=params,
        cost_estimate=cost,
        name="smooth",
    )(*far(flat, smoother, coef, element_cluster_index, restrict.T, coarse_block_matrix))
    def swaps(start):
        pairs = [(i, i + 1) for i in range(start, ngz - 1, 2)]
        return pairs + [(j, i) for i, j in pairs]

    z1 = lax.ppermute(z1, "gz", swaps(1))
    z2 = lax.ppermute(z2, "gz", swaps(0))
    xy = lax.all_to_all(xy, ("gx", "gy"), 0, 0, tiled=True)
    p, own, fh, fl, d = pl.pallas_call(
        functools.partial(prepare_kernel, dims),
        out_shape=(shape((8 * COARSE, DOFS), F32), few, wide, wide, shape((DOFS // LANES, LANES), F32)),
        in_specs=[hbm] * 2 + [vmem] * 7,
        scratch_shapes=[
            pltpu.VMEM((3 * LANES, DOFS), F32),
            pltpu.VMEM((DOFS // LANES, LANES, LANES), F32),
            pltpu.VMEM((DOFS, 3 * LANES), F32),
            pltpu.SemaphoreType.DMA((5,)),
        ],
        compiler_params=params,
        cost_estimate=cost,
        name="prepare",
    )(*far(lift, mass), uh, ul, th, nh, tr, rt, rn)
    slots = pl.pallas_call(
        functools.partial(relax_kernel, sizes, dims),
        out_shape=shape((count, COARSE // 2, LANES), F32),
        out_specs=hbm,
        scratch_shapes=[
            pltpu.VMEM((DOFS, LANES), F32),
            pltpu.VMEM((count + 1, COARSE // 2, LANES), F32),
            pltpu.SemaphoreType.DMA,
        ],
        compiler_params=params,
        cost_estimate=cost,
        name="relax",
    )(p, own, fh, fl, c, meta, xy, z1, z2)
    slots = lax.all_to_all(slots, ("gx", "gy", "gz"), 0, 0, tiled=True)
    second, rs, oh = pl.pallas_call(
        functools.partial(second_kernel, sizes, dims),
        out_shape=(
            full,
            shape((4 * COARSE, DOFS), BF16),
            shape((DOFS, LANES), BF16),
        ),
        in_specs=[hbm] * 3 + [vmem] * 9,
        scratch_shapes=[
            pltpu.VMEM((DOFS, DOFS), F32),
            pltpu.VMEM((DOFS, DOFS), F32),
            pltpu.VMEM((3 * LANES, DOFS), F32),
            pltpu.VMEM((DOFS, 3 * LANES), F32),
            pltpu.SemaphoreType.DMA((3,)),
        ],
        compiler_params=params,
        cost_estimate=cost,
        name="second",
    )(*far(flat, smoother, lift), uh, ul, tr, d, meta, rt, xy, z1, z2)
    out = pl.pallas_call(
        correct_kernel,
        out_shape=shape((DOFS, DOFS), F32),
        out_specs=hbm,
        scratch_shapes=[pltpu.VMEM((DOFS, DOFS), F32), pltpu.SemaphoreType.DMA((4,))],
        compiler_params=params,
        name="correct",
    )(second, slots, meta, oh, rs)
    return out.reshape(rhs.shape)


def solution(mesh):
    sizes = (mesh.shape["gx"], mesh.shape["gy"], mesh.shape["gz"])
    cells = P("gx", "gy", "gz")
    return jax.shard_map(
        functools.partial(shards, sizes),
        mesh=mesh,
        in_specs=(P("gx", "gy", "gz", None), cells, P(), P(), P(), P(), P(), cells),
        out_specs=P("gx", "gy", "gz", None),
        check_vma=False,
    )
```

```python
import functools

import jax
import jax.numpy as jnp
from jax import lax
from jax.experimental import pallas as pl
from jax.experimental.pallas import tpu as pltpu
from jax.sharding import PartitionSpec as P

EDGE = 8
DOFS = 512
FACE = 64
COARSE = 8
CLUSTERS = 64
LANES = 128
META = 8

F32 = jnp.float32
BF16 = jnp.bfloat16
NT = (((1,), (1,)), ((), ()))
TN = (((0,), (0,)), ((), ()))


def selection():
    column = lane((1, 4 * FACE))
    face, a, b = column // FACE, column % FACE // EDGE, column % EDGE
    node = jnp.where(face < 2, a * 64 + face * 56 + b, a * 64 + b * 8 + (face - 2) * 7)
    at = lax.broadcasted_iota(jnp.int32, (DOFS, 4 * FACE), 0)
    return jnp.where(at == node, 1.0, 0.0).astype(BF16)


def halves(x):
    high = x.astype(BF16)
    return high, (x - high.astype(F32)).astype(BF16)


def dot(a, b, dims=(((1,), (0,)), ((), ()))):
    return lax.dot_general(a, b, dims, preferred_element_type=F32)


def dot3(a, b, dims=(((1,), (0,)), ((), ()))):
    return dot(a[0], b[0], dims) + (dot(a[0], b[1], dims) + dot(a[1], b[0], dims))


def dot3_few(a, b):
    n = a[0].shape[0]
    both = dot(jnp.concatenate(a, 0), b[0], NT)
    return both[:n] + (both[n:] + dot(a[0], b[1], NT))


def lane(shape):
    return lax.broadcasted_iota(jnp.int32, shape, len(shape) - 1)


def swap(x):
    return pltpu.roll(x, FACE, 1)


def pack0(t):
    n = t.shape[0] // 2
    return jnp.where(lane((n, LANES)) < FACE, t[:n], swap(t[n:]))


def pack7(t):
    n = t.shape[0] // 2
    return jnp.where(lane((n, LANES)) < FACE, swap(t[:n]), t[n:])


def unpack0(p):
    return jnp.concatenate([p, swap(p)], 0)


def unpack7(p):
    return jnp.concatenate([swap(p), p], 0)


def cell_rows(ref):
    ex, ey, ez = ref.shape
    rows = []
    for x in range(ex):
        rows.append(jnp.concatenate([ref[x, y : y + 1, :] for y in range(ey)], 1))
    return jnp.concatenate(rows, 0).astype(F32)


def face_order(lift):
    return jnp.concatenate([lift[(f ^ 1) * FACE : ((f ^ 1) + 1) * FACE] for f in range(6)], 0)


def reciprocal(rows):
    n = rows.shape[0]
    columns = (1.0 / jnp.concatenate([rows, jnp.ones((LANES - n, LANES), F32)], 0)).T
    return jnp.concatenate([jnp.broadcast_to(columns[:, x : x + 1], (LANES, LANES)) for x in range(n)], 0)


def as_row(rows):
    return jnp.concatenate([rows[x : x + 1] for x in range(rows.shape[0])], 1)


def onehot_rows(row):
    n = row.shape[1]
    at = lax.broadcasted_iota(jnp.int32, (CLUSTERS, n), 0).astype(F32)
    return jnp.where(at == row, 1.0, 0.0).astype(BF16)


def position(sizes):
    return lax.axis_index("gx"), lax.axis_index("gy"), lax.axis_index("gz")


def near_identity(s_ref, part):
    diagonal = lax.broadcasted_iota(jnp.int32, (LANES, LANES), 0) == lane((LANES, LANES))
    identity = jnp.where(diagonal, 1.0, 0.0)
    rows = []
    for start in range(part.start, part.stop, LANES):
        s = s_ref[start : start + LANES]
        tile = identity - s[:, start : start + LANES]
        pieces = [-s[:, :start], tile, -s[:, start + LANES :]]
        rows.append(jnp.concatenate([piece for piece in pieces if piece.shape[1]], 1))
    return halves(jnp.concatenate(rows, 0))


def start_all(pairs, sems):
    copies = [pltpu.make_async_copy(src, dst, sems.at[i]) for i, (src, dst) in enumerate(pairs)]
    for copy in copies:
        copy.start()
    return copies


def fetch(names, sems, rhs=None, s=None, m=None, l=None):
    pairs = {"rhs": [rhs], "s": [s], "l": [l], "m": []}
    for i in range(DOFS // LANES if m else 0):
        block = slice(i * LANES, (i + 1) * LANES)
        pairs["m"].append((m[0].at[block, block], m[1].at[i]))
    counts = [len(pairs[name]) for name in names]
    first = [sum(counts[:i]) for i in range(len(names))]
    copies = start_all([pair for name in names for pair in pairs[name]], sems)

    def wait(name):
        i = names.index(name)
        for copy in copies[first[i] : first[i] + counts[i]]:
            copy.wait()

    return wait


def diagonal_rows(d_ref):
    here = lax.broadcasted_iota(jnp.int32, (LANES, LANES), 0) == lane((LANES, LANES))
    return jnp.concatenate(
        [jnp.sum(jnp.where(here, d_ref[i], 0.0), 0, keepdims=True) for i in range(d_ref.shape[0])], 0
    )


def traces(u, split, pick, scale):
    lower = lane((u.shape[0], LANES)) < FACE
    picked = dot(split[0], pick) + dot(split[1], pick)
    x_pair = jnp.where(lower, u[:, :LANES], u[:, DOFS - LANES :]) * scale
    return x_pair, picked[:, :LANES] * scale, picked[:, LANES:] * scale


def smooth_kernel(sizes, rhs_hbm, s_hbm, coef_hbm, lab_hbm, rt_hbm, c_hbm,
                  uh_ref, ul_ref, th_ref, nh_ref, tr_ref, meta_ref, xy_hbm, z1_ref, z2_ref, rt_ref, c_ref, rn_ref,
                  rhs_ref, s_ref, coef_ref, lab_ref, t_ref, nl_ref, out_ref, sems, out_sems):
    ngx, ngy, ngz = sizes
    gx, gy, gz = position(sizes)
    half = DOFS // 2
    blocks = [slice(0, half), slice(half, DOFS)]
    pairs = [(coef_hbm, coef_ref), (lab_hbm, lab_ref), (rt_hbm, rt_ref), (c_hbm, c_ref)]
    for part in blocks:
        quarters = [slice(part.start + i * half // 2, part.start + (i + 1) * half // 2) for i in range(2)]
        pairs += [(s_hbm.at[rows], s_ref.at[rows]) for rows in quarters]
        pairs += [(rhs_hbm.at[rows, part], rhs_ref.at[rows, part]) for rows in blocks]
    copies = start_all(pairs, sems)

    def wait(first, count):
        for copy in copies[first : first + count]:
            copy.wait()

    ex, ey, ez = lab_ref.shape
    plane = ey * ez
    pick = selection()
    wait(0, 4)
    lab = cell_rows(lab_ref)
    counts = dot(jnp.ones((8, DOFS), BF16), onehot_rows(as_row(lab)), NT)
    weights = 1.0 + jnp.concatenate([counts[0:1], counts[0:1]], 1)
    meta = jnp.concatenate([lab, weights, jnp.zeros((META - 5, LANES), F32)], 0)
    meta_ref[:META] = meta
    meta_ref[META : META + ex] = cell_rows(coef_ref)
    rc = reciprocal(meta_ref[META : META + ex])

    def near_part(part):
        near = near_identity(s_ref, part)
        nh_ref[part], nl_ref[part] = near
        return near

    here = gx * ngy + gy
    outs = []

    def send(i, there, slot, packed):
        n = packed.shape[0]
        out_ref[i, :n] = packed
        out_ref[i, n:] = meta
        out = pltpu.make_async_copy(out_ref.at[i], xy_hbm.at[jnp.where(there, slot, here)], out_sems.at[i])
        pl.when(there)(out.start)
        outs.append((there, out))

    wait(4, 4)
    near = near_part(blocks[0])
    t_ref[...] = dot3(halves(rhs_ref[:, blocks[0]]), near)
    wait(8, 4)
    near = near_part(blocks[1])
    pairs = []
    for rows in blocks:
        t = t_ref[rows] + dot3(halves(rhs_ref[rows, blocks[1]]), near)
        th_ref[rows] = t.astype(BF16)
        u = rhs_ref[rows] - t
        split = halves(u)
        uh_ref[rows], ul_ref[rows] = split
        pairs.append(traces(u, split, pick, rc[rows]))
        for i, pair in enumerate(pairs[-1]):
            tr_ref[rows, i * LANES : (i + 1) * LANES] = pair
        if rows is blocks[0]:
            send(0, gx > 0, here - ngy, pack0(pairs[0][0][:plane]))
    x_pair, y_pair, z_pair = [jnp.concatenate([block[i] for block in pairs], 0) for i in range(3)]

    def y_rows(y):
        return jnp.concatenate(
            [y_pair[x * plane + y * ez : x * plane + (y + 1) * ez] for x in range(ex)], 0
        )

    def z_rows(z):
        return jnp.concatenate([z_pair[i * ez + z : i * ez + z + 1] for i in range(ex * ey)], 0)

    send(1, gx < ngx - 1, here + ngy, pack7(x_pair[(ex - 1) * plane :]))
    send(2, gy < ngy - 1, here + 1, pack7(y_rows(ey - 1)))
    send(3, gy > 0, here - 1, pack0(y_rows(0)))
    rn_ref[...] = dot3_few(halves(rt_ref[...]), (nh_ref[...], nl_ref[...]))
    odd = lax.rem(gz, 2) == 1
    up, down = pack7(z_rows(ez - 1)), pack0(z_rows(0))
    z1_ref[...] = jnp.concatenate([jnp.where(odd, up, down), meta], 0)
    z2_ref[...] = jnp.concatenate([jnp.where(odd, down, up), meta], 0)
    for there, out in outs:
        pl.when(there)(out.wait)


def receive(sizes, dims, xy_ref, z1_ref, z2_ref):
    ngx, ngy, ngz = sizes
    gx, gy, gz = position(sizes)
    odd = lax.rem(gz, 2) == 1

    def one(got, there):
        n = got.shape[0] - META
        payload = jnp.where(there, got[:n], 0.0)
        labels = jnp.where(there, got[n : n + dims[0]], -1.0)
        weights = jnp.where(there, got[n + dims[0] : n + dims[0] + 1], 1.0)
        return payload, labels, weights

    return [
        one(xy_ref[jnp.minimum(gx + 1, ngx - 1) * ngy + gy], gx < ngx - 1),
        one(xy_ref[jnp.maximum(gx - 1, 0) * ngy + gy], gx > 0),
        one(xy_ref[gx * ngy + jnp.minimum(gy + 1, ngy - 1)], gy < ngy - 1),
        one(xy_ref[gx * ngy + jnp.maximum(gy - 1, 0)], gy > 0),
        one(jnp.where(odd, z1_ref[...], z2_ref[...]), gz < ngz - 1),
        one(jnp.where(odd, z2_ref[...], z1_ref[...]), gz > 0),
    ]


def faces(f_ref, dims, tr_ref, around):
    ex, ey, ez = dims
    lower = lane((ez, LANES)) < FACE
    inner = lax.broadcasted_iota(jnp.int32, (ez, LANES), 0)
    none = jnp.zeros((ez, LANES), F32)
    outer = None
    if around is not None:
        outer = [(unpack0 if i % 2 == 0 else unpack7)(a[0]) for i, a in enumerate(around)]

    def local(i, pair):
        if tr_ref is None:
            return none
        return tr_ref[i * ez : (i + 1) * ez, pair]

    def remote(side, strip):
        return none if outer is None else outer[side][strip]

    for x in range(ex):
        for y in range(ey):
            i = x * ey + y
            rows = slice(i * ez, (i + 1) * ez)
            pair = slice(0, LANES)
            strip = slice(y * ez, (y + 1) * ez)
            above = local(i + ey, pair) if x < ex - 1 else remote(0, strip)
            below = local(i - ey, pair) if x > 0 else remote(1, strip)
            f_ref[rows, pair] = jnp.where(lower, above, below)
            pair = slice(LANES, 2 * LANES)
            strip = slice(x * ez, (x + 1) * ez)
            above = local(i + 1, pair) if y < ey - 1 else remote(2, strip)
            below = local(i - 1, pair) if y > 0 else remote(3, strip)
            f_ref[rows, pair] = jnp.where(lower, above, below)
            pair = slice(2 * LANES, 3 * LANES)
            above = below = none
            if tr_ref is not None:
                column = tr_ref[rows, pair]
                above = jnp.where(inner == ez - 1, 0.0, pltpu.roll(column, ez - 1, 0))
                below = jnp.where(inner == 0, 0.0, pltpu.roll(column, 1, 0))
            if outer is not None:
                above = jnp.where(inner == ez - 1, outer[4][i : i + 1], above)
                below = jnp.where(inner == 0, outer[5][i : i + 1], below)
            f_ref[rows, pair] = jnp.where(lower, above, below)


def prepare_kernel(dims, l_hbm, m_hbm, uh_ref, ul_ref, th_ref, nh_ref, tr_ref, rt_ref, rn_ref,
                   p_ref, own_ref, qh_ref, ql_ref, d_out_ref, l_ref, d_ref, f_ref, sems):
    wait = fetch(("l", "m"), sems, l=(l_hbm, l_ref), m=(m_hbm, d_ref))
    faces(f_ref, dims, tr_ref, None)
    inside = halves(f_ref[...])
    near = nh_ref[...]
    pick = selection()
    wait("l")
    wait("m")
    diagonal = diagonal_rows(d_ref)
    d_out_ref[...] = diagonal
    d = as_row(diagonal)
    lift = halves(face_order(l_ref[...]))
    lrt = dot3_few(halves(rt_ref[...]), lift)
    zeros = jnp.zeros((COARSE, DOFS - FACE), F32)
    x0 = jnp.concatenate([lrt[:, :FACE], zeros], 1)
    x7 = jnp.concatenate([zeros, lrt[:, FACE:LANES]], 1)
    yz = lrt[:, LANES:]
    group = lane((COARSE, 4 * FACE)) // FACE
    spread = jnp.concatenate([jnp.where(group == f, yz, 0.0) for f in range(4)], 0)
    both = dot(jnp.concatenate(halves(spread), 0), pick, NT)
    yz = both[: 4 * COARSE] + both[4 * COARSE :]
    mrt = rt_ref[...] * d + rn_ref[...]
    q = jnp.concatenate([x0, x7, yz, mrt, jnp.zeros_like(mrt)], 0)
    rows = q.shape[0]
    both = dot(jnp.concatenate(halves(q), 0), near, NT)
    swept = q - (both[:rows] + both[rows:])
    split = halves(swept)
    of_t = dot(split[0], near, NT)
    of_f = halves(dot3_few(split, lift))
    qh_ref[...], ql_ref[...] = of_f
    of_u = halves(jnp.concatenate([q + swept * (1.0 - d), rt_ref[...] + rn_ref[...]], 0))
    by_t = dot(jnp.concatenate([of_t, rn_ref[...]], 0).astype(BF16), th_ref[...], NT)
    by_u = dot3_few(of_u, (uh_ref[...], ul_ref[...]))
    p_ref[...] = by_u[:rows] + by_t[:rows] + dot3_few(of_f, inside)
    own_ref[...] = by_u[rows:] + by_t[rows:]


def relax_kernel(sizes, dims, p_ref, own_ref, qh_ref, ql_ref, c_ref, meta_ref, xy_ref, z1_ref, z2_ref,
                 slots_hbm, f_ref, bins_ref, sem):
    ngx, ngy, ngz = sizes
    gx, gy, gz = position(sizes)
    ex, ey, ez = dims
    plane = ey * ez
    around = receive(sizes, dims, xy_ref, z1_ref, z2_ref)
    x_up, x_down, y_up, y_down, z_up, z_down = around
    q = qh_ref[...], ql_ref[...]
    rows = q[0].shape[0]
    keep = lane((rows, LANES)) < FACE

    def through(side, payload):
        pair = slice(side // 2 * LANES, (side // 2 + 1) * LANES)
        mine = keep if side % 2 == 0 else ~keep
        few = [jnp.where(mine, a[:, pair].astype(F32), 0.0).astype(BF16) for a in q]
        return dot3_few(few, halves(payload))

    added = []
    x_above, x_below = through(0, unpack0(x_up[0])), through(1, unpack7(x_down[0]))
    y_above, y_below = through(2, unpack0(y_up[0])), through(3, unpack7(y_down[0]))
    z_above, z_below = unpack0(z_up[0]), unpack7(z_down[0])
    inner = lax.broadcasted_iota(jnp.int32, (ez, LANES), 0)
    for i in range(ex * ey):
        f_ref[i * ez : (i + 1) * ez] = jnp.where(
            lane((ez, LANES)) < FACE,
            jnp.where(inner == ez - 1, z_above[i : i + 1], 0.0),
            jnp.where(inner == 0, z_below[i : i + 1], 0.0),
        )
    z_both = dot3_few([a[:, 2 * LANES :] for a in q], halves(f_ref[...]))
    at = lane((rows, LANES))
    for x in range(ex):
        tile = z_both[:, x * LANES : (x + 1) * LANES]
        up, down = (plane - ez - x * ez) % LANES, (LANES - x * ez) % LANES
        tile = tile + jnp.where(at >= plane - ez, pltpu.roll(y_above, up, 1) if up else y_above, 0.0)
        tile = tile + jnp.where(at < ez, pltpu.roll(y_below, down, 1) if down else y_below, 0.0)
        tile = tile + (x_above if x == ex - 1 else 0.0) + (x_below if x == 0 else 0.0)
        added.append(tile)
    p = p_ref[...] + jnp.concatenate(added, 1)
    own = own_ref[...]
    small = own - p[6 * COARSE : 7 * COARSE]
    p = p / as_row(meta_ref[META : META + ex])
    p_x0, p_x7, p_y0, p_y7, p_z0, p_z7 = [p[8 * f : 8 * f + 8] for f in range(6)]
    at = lane((COARSE, LANES))

    def tiles(a):
        return [a[:, x * LANES : (x + 1) * LANES] for x in range(ex)]

    none = jnp.zeros((COARSE, LANES), F32)
    total = []
    parts = [tiles(a) for a in (small, p_x0, p_x7, p_y0, p_y7, p_z0, p_z7)]
    for x in range(ex):
        s, _, _, y0, y7, z0, z7 = [a[x] for a in parts]
        s = s + (parts[1][x + 1] if x < ex - 1 else none)
        s = s + (parts[2][x - 1] if x > 0 else none)
        s = s + jnp.where(at < plane - ez, pltpu.roll(y0, LANES - ez, 1), 0.0)
        s = s + jnp.where(at >= ez, pltpu.roll(y7, ez, 1), 0.0)
        s = s + jnp.where(at % ez < ez - 1, pltpu.roll(z0, LANES - 1, 1), 0.0)
        s = s + jnp.where(at % ez > 0, pltpu.roll(z7, 1, 1), 0.0)
        total.append(s)
    total = jnp.concatenate(total, 1)

    def scatter(values, onehot):
        high, low = halves(values)
        out = dot(jnp.concatenate([high, low], 0), jnp.concatenate([onehot, onehot], 0), NT)
        return out[:COARSE] + out[COARSE:]

    def shifted(labels, shift, keep):
        return as_row(jnp.where(keep, pltpu.roll(labels, shift, 1), -1.0))

    rows = lane((ex, LANES))
    labels = meta_ref[0:ex]
    blocks = [
        (scatter(total, onehot_rows(as_row(labels))), meta_ref[ex : ex + 1]),
        (scatter(parts[2][ex - 1], onehot_rows(x_up[1][0:1])), x_up[2]),
        (scatter(parts[1][0], onehot_rows(x_down[1][ex - 1 : ex])), x_down[2]),
        (scatter(p_y7, onehot_rows(shifted(y_up[1], plane - ez, rows >= plane - ez))), y_up[2]),
        (scatter(p_y0, onehot_rows(shifted(y_down[1], ez, rows < ez))), y_down[2]),
        (scatter(p_z7, onehot_rows(shifted(z_up[1], ez - 1, rows % ez == ez - 1))), z_up[2]),
        (scatter(p_z0, onehot_rows(shifted(z_down[1], LANES - ez + 1, rows % ez == 0))), z_down[2]),
    ]
    columns = [jnp.broadcast_to(c_ref[:, k : k + 1], (COARSE, LANES)) for k in range(COARSE)]

    def mixed(block):
        out = block + block
        for k in range(COARSE):
            out = out - columns[k] * block[k : k + 1]
        return out

    def packed(block):
        half = COARSE // 2
        return jnp.where(lane((half, LANES)) < FACE, block[:half], block[half:])

    b0, xu, xd, yu, yd, zu, zd = [packed(z / w) for z, w in blocks]
    a0, axu, axd, ayu, ayd, azu, azd = [packed(mixed(z)) for z, _ in blocks]

    count = slots_hbm.shape[0]
    bins_ref[...] = jnp.zeros_like(bins_ref)

    def put(dx, dy, dz, share):
        there = (dy >= 0) & (dy < ngy) & (dz >= 0) & (dz < ngz)
        bins_ref[jnp.where(there, (dx * ngy + dy) * ngz + dz, count)] = share

    line = b0 + xu + xd
    sides = yu + yd + zu + zd
    for dx in range(ngx):
        same = (gx == dx).astype(F32)
        up = (gx + 1 == dx).astype(F32)
        down = (gx - 1 == dx).astype(F32)
        column = same * b0 + up * xu + down * xd
        put(dx, gy, gz, line + same * (sides + a0) + up * axu + down * axd)
        put(dx, gy + 1, gz, yu + column + same * ayu)
        put(dx, gy - 1, gz, yd + column + same * ayd)
        put(dx, gy, gz + 1, zu + column + same * azu)
        put(dx, gy, gz - 1, zd + column + same * azd)
    put(gx, gy + 2, gz, yu)
    put(gx, gy - 2, gz, yd)
    put(gx, gy, gz + 2, zu)
    put(gx, gy, gz - 2, zd)
    put(gx, gy + 1, gz + 1, yu + zu)
    put(gx, gy + 1, gz - 1, yu + zd)
    put(gx, gy - 1, gz + 1, yd + zu)
    put(gx, gy - 1, gz - 1, yd + zd)
    copy = pltpu.make_async_copy(bins_ref.at[pl.ds(0, count)], slots_hbm, sem)
    copy.start()
    copy.wait()


def second_kernel(sizes, dims, rhs_hbm, s_hbm, l_hbm, uh_ref, ul_ref, tr_ref, d_ref, meta_ref, rt_ref, xy_ref, z1_ref, z2_ref,
                  second_ref, rs_ref, oh_ref, rhs_ref, s_ref, l_ref, f_ref, sems):
    wait = fetch(("l", "s", "rhs"), sems, rhs=(rhs_hbm, rhs_ref), s=(s_hbm, s_ref), l=(l_hbm, l_ref))
    ex = dims[0]
    faces(f_ref, dims, tr_ref, receive(sizes, dims, xy_ref, z1_ref, z2_ref))
    onehot = onehot_rows(as_row(meta_ref[:ex]))
    oh_ref[...] = jnp.concatenate([onehot, onehot], 0).astype(F32).T.astype(BF16)
    rt = halves(rt_ref[...])
    rs_ref[...] = jnp.concatenate([rt[0], rt[0], rt[1], jnp.zeros_like(rt[0])], 0)
    wait("l")
    r1 = dot3(halves(f_ref[...]), halves(face_order(l_ref[...])))
    wait("s")
    near = near_identity(s_ref, slice(0, DOFS))
    wait("rhs")
    u = uh_ref[...].astype(F32) + ul_ref[...].astype(F32)
    d = as_row(d_ref[...])
    r1 = r1 + dot3(halves(rhs_ref[...] - u), near) + u * (1.0 - d)
    v = u + (r1 - dot3(halves(r1), near))
    rc = reciprocal(meta_ref[META : META + ex])
    second_ref[...] = v * jnp.concatenate([rc] * (DOFS // LANES), 1)


def correct_kernel(second_ref, slots_ref, meta_ref, oh_ref, rs_ref, out_hbm, out_ref, sems):
    total = jnp.sum(slots_ref[...], 0)
    ztwo = jnp.concatenate([total[:, :FACE], total[:, FACE:]], 0) / meta_ref[4:5, :FACE]
    high, low = halves(ztwo)
    stacked = jnp.concatenate([high, low, high, jnp.zeros_like(high)], 0)
    prolonged = dot(stacked, rs_ref[...], TN)
    prolonged = jnp.concatenate(halves(prolonged), 0)
    chunk = DOFS // sems.shape[0]
    copies = []
    for i in range(sems.shape[0]):
        rows = slice(i * chunk, (i + 1) * chunk)
        out_ref[rows] = second_ref[rows] + dot(oh_ref[rows], prolonged)
        copy = pltpu.make_async_copy(out_ref.at[rows], out_hbm.at[rows], sems.at[i])
        copy.start()
        copies.append(copy)
    for copy in copies:
        copy.wait()


def shards(sizes, rhs, coef, mass, smoother, lift, restrict, coarse_block_matrix, element_cluster_index):
    ngx, ngy, ngz = sizes
    dims = coef.shape
    ex, ey, ez = dims
    flat = rhs.reshape(ex * ey * ez, DOFS)
    face = ey * ez * FACE // LANES
    tip = ex * ey * FACE // LANES
    params = pltpu.CompilerParams(vmem_limit_bytes=40 * 1024 * 1024)
    shape = jax.ShapeDtypeStruct
    hbm = pl.BlockSpec(memory_space=pltpu.HBM)
    vmem = pl.BlockSpec(memory_space=pltpu.VMEM)
    cost = pl.CostEstimate(flops=2 * 10**9, bytes_accessed=4 * 2**20, transcendentals=0)
    def far(*arrays):
        return [pltpu.with_memory_space_constraint(a, pltpu.HBM) for a in arrays]

    full = shape((DOFS, DOFS), F32)
    split = shape((DOFS, DOFS), BF16)
    count = ngx * ngy * ngz
    wide = shape((8 * COARSE, 3 * LANES), BF16)
    few = shape((COARSE, DOFS), F32)
    uh, ul, th, nh, tr, meta, xy, z1, z2, rt, c, rn = pl.pallas_call(
        functools.partial(smooth_kernel, sizes),
        out_shape=(
            split,
            split,
            split,
            split,
            shape((DOFS, 3 * LANES), F32),
            shape((2 * META, LANES), F32),
            shape((ngx * ngy, face + META, LANES), F32),
            shape((tip + META, LANES), F32),
            shape((tip + META, LANES), F32),
            few,
            shape((COARSE, COARSE), F32),
            few,
        ),
        in_specs=[hbm] * 6,
        out_specs=[vmem] * 6 + [hbm] + [vmem] * 5,
        scratch_shapes=[
            pltpu.VMEM((DOFS, DOFS), F32),
            pltpu.VMEM((DOFS, DOFS), F32),
            pltpu.VMEM(dims, F32),
            pltpu.VMEM(dims, jnp.int32),
            pltpu.VMEM((DOFS, DOFS), F32),
            pltpu.VMEM((DOFS, DOFS), BF16),
            pltpu.VMEM((4, face + META, LANES), F32),
            pltpu.SemaphoreType.DMA((12,)),
            pltpu.SemaphoreType.DMA((4,)),
        ],
        compiler_params=params,
        cost_estimate=cost,
        name="smooth",
    )(*far(flat, smoother, coef, element_cluster_index, restrict.T, coarse_block_matrix))
    def swaps(start):
        pairs = [(i, i + 1) for i in range(start, ngz - 1, 2)]
        return pairs + [(j, i) for i, j in pairs]

    z1 = lax.ppermute(z1, "gz", swaps(1))
    z2 = lax.ppermute(z2, "gz", swaps(0))
    xy = lax.all_to_all(xy, ("gx", "gy"), 0, 0, tiled=True)
    p, own, fh, fl, d = pl.pallas_call(
        functools.partial(prepare_kernel, dims),
        out_shape=(shape((8 * COARSE, DOFS), F32), few, wide, wide, shape((DOFS // LANES, LANES), F32)),
        in_specs=[hbm] * 2 + [vmem] * 7,
        scratch_shapes=[
            pltpu.VMEM((3 * LANES, DOFS), F32),
            pltpu.VMEM((DOFS // LANES, LANES, LANES), F32),
            pltpu.VMEM((DOFS, 3 * LANES), F32),
            pltpu.SemaphoreType.DMA((5,)),
        ],
        compiler_params=params,
        cost_estimate=cost,
        name="prepare",
    )(*far(lift, mass), uh, ul, th, nh, tr, rt, rn)
    slots = pl.pallas_call(
        functools.partial(relax_kernel, sizes, dims),
        out_shape=shape((count, COARSE // 2, LANES), F32),
        out_specs=hbm,
        scratch_shapes=[
            pltpu.VMEM((DOFS, LANES), F32),
            pltpu.VMEM((count + 1, COARSE // 2, LANES), F32),
            pltpu.SemaphoreType.DMA,
        ],
        compiler_params=params,
        cost_estimate=cost,
        name="relax",
    )(p, own, fh, fl, c, meta, xy, z1, z2)
    slots = lax.all_to_all(slots, ("gx", "gy", "gz"), 0, 0, tiled=True)
    second, rs, oh = pl.pallas_call(
        functools.partial(second_kernel, sizes, dims),
        out_shape=(
            full,
            shape((4 * COARSE, DOFS), BF16),
            shape((DOFS, LANES), BF16),
        ),
        in_specs=[hbm] * 3 + [vmem] * 9,
        scratch_shapes=[
            pltpu.VMEM((DOFS, DOFS), F32),
            pltpu.VMEM((DOFS, DOFS), F32),
            pltpu.VMEM((3 * LANES, DOFS), F32),
            pltpu.VMEM((DOFS, 3 * LANES), F32),
            pltpu.SemaphoreType.DMA((3,)),
        ],
        compiler_params=params,
        cost_estimate=cost,
        name="second",
    )(*far(flat, smoother, lift), uh, ul, tr, d, meta, rt, xy, z1, z2)
    out = pl.pallas_call(
        correct_kernel,
        out_shape=shape((DOFS, DOFS), F32),
        out_specs=hbm,
        scratch_shapes=[pltpu.VMEM((DOFS, DOFS), F32), pltpu.SemaphoreType.DMA((4,))],
        compiler_params=params,
        name="correct",
    )(second, slots, meta, oh, rs)
    return out.reshape(rhs.shape)


def solution(mesh):
    sizes = (mesh.shape["gx"], mesh.shape["gy"], mesh.shape["gz"])
    cells = P("gx", "gy", "gz")
    return jax.shard_map(
        functools.partial(shards, sizes),
        mesh=mesh,
        in_specs=(P("gx", "gy", "gz", None), cells, P(), P(), P(), P(), P(), cells),
        out_specs=P("gx", "gy", "gz", None),
        check_vma=False,
    )
```
